32 devices in a mesh: expert: 16 (over z, y, x), tensor: 2 (over core).
Axes of the slice: x: 2, y: 2, z: 4, core: 2. Of those that a mesh axis runs over, the one named last changes fastest.
Arguments:
- hidden_in: bfloat16 [8192, 1536], P('expert'), may hold values from -6 to 6
- attn_gain: float32 [1536], replicated, may hold values from 0.5 to 1.5
- w_query: bfloat16 [1536, 1536], P(None, 'tensor'), may hold values from -0.15625 to 0.15625
- w_key: bfloat16 [1536, 256], P(None, 'tensor'), may hold values from -0.15625 to 0.15625
- w_value: bfloat16 [1536, 256], P(None, 'tensor'), may hold values from -0.15625 to 0.15625
- w_output: bfloat16 [1536, 1536], P('tensor'), may hold values from -0.625 to 0.625
- moe_gain: float32 [1536], replicated, may hold values from 0.5 to 1.5
- w_gate: bfloat16 [16, 1536, 768], P('expert', None, 'tensor'), may hold values from -0.15625 to 0.15625
- w_up: bfloat16 [16, 1536, 768], P('expert', None, 'tensor'), may hold values from -0.15625 to 0.15625
- w_down: bfloat16 [16, 768, 1536], P('expert', 'tensor'), may hold values from -0.4375 to 0.4375
- gate_logits: float32 [8192, 4], P('expert'), may hold values from -3 to 3
- routes: int32 [8192, 4], P('expert'), may hold values from 0 to 15, all different within a row; in each aligned block of 512 rows (0 to 511, 512 to 1023, ...) at most 256 rows name the same one
- out_grad: bfloat16 [8192, 1536], P('expert'), may hold values from -6 to 6
Outputs:
- block_out: bfloat16 [8192, 1536], P('expert')
- grad_in: float32 [8192, 1536], P('expert')
- grad_attn_gain: float32 [1536], replicated
- grad_query: float32 [1536, 1536], P(None, 'tensor')
- grad_key: float32 [1536, 256], P(None, 'tensor')
- grad_value: float32 [1536, 256], P(None, 'tensor')
- grad_output: float32 [1536, 1536], P('tensor')
- grad_moe_gain: float32 [1536], replicated
- grad_gate: float32 [16, 1536, 768], P('expert', None, 'tensor')
- grad_up: float32 [16, 1536, 768], P('expert', None, 'tensor')
- grad_down: float32 [16, 768, 1536], P('expert', 'tensor')
The draws below stay inside these ranges and needn't reach their ends.
Inputs may be any that keep to these rules, and one draw needn't show every extreme that they name: `routes`: A row names 4 different experts. Among the 512 rows of one sequence, no expert is named by more than 256 rows, a bound that some block reaches.
All inputs are finite; a program needn't handle non-finite values.
Results may differ from the reference program's by a relative error of at most 0.018.
Values may be sent and summed in bfloat16 or wider, within the bound.
No kernel may reach another device: no remote copies, remote signals or barrier semaphores. Data moves between devices by JAX's collectives and lax.ppermute only.
A program may use at most 256 MiB of HBM per device.

```python
import math
import jax
import jax.numpy as jnp
import numpy as np
from jax import lax

D = 1536
HEADS = 12
KV = 2
HD = 128
FF = 768
TOP = 4
TOK_DEV = 512
EXPERTS = 16
CAP = 256
TOKENS = 8192
N_EXPERT = 16


def levels(stream_key, dims, split, smallest, largest):
    def one(dim, shards_of):
        draws = jax.random.uniform(jax.random.fold_in(jax.random.fold_in(stream_key, 6), dim), (shards_of,), jnp.float32, smallest / len(split), largest / len(split))
        return jnp.repeat(jnp.exp(draws), dims[dim] // shards_of).reshape((-1,) + (1,) * (len(dims) - dim - 1))

    loudness = one(*split[0])
    for cut in split[1:]:
        loudness = loudness * one(*cut)
    return loudness


def deal_out(rng, own, number, rows, amount, top, limit, slope):
    ranking = jax.random.permutation(rng, amount)
    crowded, ordinary = shares(amount, rows * top, limit, slope, True), shares(amount, rows * top, limit, slope, False)
    places = jnp.arange(amount)

    def named(sizes, offset_by):
        used = int((sizes > 0).sum())
        fixed = max(1, used // 4)
        moved = fixed + (places - fixed + offset_by * (used - fixed)) % max(1, amount - fixed)
        return jnp.zeros((amount,), jnp.int32).at[ranking[jnp.where(places < fixed, places, moved)]].set(jnp.asarray(sizes, jnp.int32))

    sizes = jnp.where(number % 4 == 0, named(crowded, number // 4), named(ordinary, number - number // 4 - 1))
    mixed = jax.random.permutation(jax.random.fold_in(own, 3), amount)
    donor, taker = mixed[0:amount // 2 * 2:2], mixed[1:amount // 2 * 2:2]
    room = jnp.minimum(sizes[donor] - 1, limit - sizes[taker]) // 2
    room = jnp.where((donor == ranking[0]) | (taker == ranking[0]) | (sizes[taker] == 0), 0, jnp.maximum(room, 0))
    moved = jax.random.randint(jax.random.fold_in(own, 4), (amount // 2,), 0, 1 << 20) % (room + 1)
    sizes = sizes.at[donor].add(-moved).at[taker].add(moved)
    items = jnp.searchsorted(jnp.cumsum(sizes), jnp.arange(rows * top), side="right").astype(jnp.int32)
    listing = items.reshape(top, rows).T
    listing = listing[jax.random.permutation(jax.random.fold_in(own, 1), rows)]
    offset_by = jax.random.randint(jax.random.fold_in(own, 2), (rows, 1), 0, top)
    return jnp.take_along_axis(listing, (jnp.arange(top)[None, :] + offset_by) % top, axis=1)


def shares(count, total, bound, slope, full):
    loads = [(1 << 20) // math.isqrt(grade ** slope) + 1 for grade in range(1, count + 1)]
    largest = bound if full else min(bound, max(-(-total // count), total * loads[0] // sum(loads)))
    least = 1 if total - largest >= count - 1 else 0
    holding, surplus = [largest] + [least] * (count - 1), total - largest - least * (count - 1)
    while surplus > 0:
        free = [i for i in range(1, count) if holding[i] < largest] or [i for i in range(1, count) if holding[i] < bound]
        pool, remaining = sum([loads[i] for i in free]), surplus
        for i in free:
            addition = min(bound - holding[i], max(1, remaining * loads[i] // pool), surplus)
            holding[i] = holding[i] + addition
            surplus = surplus - addition
    return np.array(holding)


def scatter_about(rng, dims, width, limit, cuts=(), kind=jnp.bfloat16):
    values = width * jax.random.normal(rng, dims, jnp.float32)
    if cuts:
        values = values * levels(rng, dims, cuts, -0.22, 0.18)
    return jnp.clip(values, -limit, limit).astype(kind)


def setup_inputs(seed: int = 0) -> dict:
    seeds = jax.random.split(jax.random.key(seed), 14)
    hidden_in = scatter_about(seeds[0], (TOKENS, D), 1.0, 6.0, ((0, 16),))
    attn_gain = jnp.clip(1.0 + 0.1 * jax.random.normal(seeds[1], (D,), jnp.float32), 0.5, 1.5)
    w_query = scatter_about(seeds[2], (D, HEADS * HD), D ** -0.5, 0.15625, ((1, 2),))
    w_key = scatter_about(seeds[3], (D, KV * HD), D ** -0.5, 0.15625, ((1, 2),))
    w_value = scatter_about(seeds[4], (D, KV * HD), D ** -0.5, 0.15625, ((1, 2),))
    w_output = scatter_about(seeds[5], (HEADS * HD, D), (HEADS * HD // 16) ** -0.5, 0.625, ((0, 2),))
    moe_gain = jnp.clip(1.0 + 0.1 * jax.random.normal(seeds[6], (D,), jnp.float32), 0.5, 1.5)
    w_gate = scatter_about(seeds[7], (EXPERTS, D, FF), D ** -0.5, 0.15625, ((0, 16), (2, 2)))
    w_up = scatter_about(seeds[8], (EXPERTS, D, FF), D ** -0.5, 0.15625, ((0, 16), (2, 2)))
    w_down = scatter_about(seeds[9], (EXPERTS, FF, D), (FF // 4) ** -0.5, 0.4375, ((0, 16), (1, 2)))
    gate_logits = scatter_about(seeds[10], (TOKENS, TOP), 0.5, 3.0, ((0, 16),), jnp.float32)
    routes_keys = jax.random.split(jax.random.fold_in(seeds[11], 1), TOKENS // TOK_DEV)
    routes_turns = jax.random.permutation(jax.random.fold_in(seeds[11], 3), TOKENS // TOK_DEV)
    routes = jax.vmap(lambda own, number: deal_out(jax.random.fold_in(seeds[11], 2), own, number, TOK_DEV, EXPERTS, TOP, CAP, 1))(routes_keys, routes_turns).reshape((TOKENS, TOP))
    out_grad = scatter_about(seeds[12], (TOKENS, D), 1.0, 6.0, ((0, 16),))
    return {"hidden_in": hidden_in, "attn_gain": attn_gain, "w_query": w_query, "w_key": w_key, "w_value": w_value, "w_output": w_output, "moe_gain": moe_gain, "w_gate": w_gate, "w_up": w_up, "w_down": w_down, "gate_logits": gate_logits, "routes": routes, "out_grad": out_grad}


epsilon = 1e-06
rope_base = 10000.0
masked_score = -1e+30
highest = lax.Precision.HIGHEST

@jax.custom_vjp
def low(v):
    return lax.optimization_barrier(v.astype(jnp.bfloat16)).astype(jnp.float32)

@jax.custom_vjp
def low_back(v):
    return v

def low_keep(v):
    return (low(v), None)

def low_pass(kept, grad):
    return (grad,)

def back_keep(v):
    return (v, None)

def back_low(kept, grad):
    return (low(grad),)
low.defvjp(low_keep, low_pass)
low_back.defvjp(back_keep, back_low)

def product(left, right):
    return jnp.dot(left, right, precision=highest, preferred_element_type=jnp.float32)

def rms_scaled(values, gain):
    factor = lax.rsqrt(lax.optimization_barrier(jnp.mean(values * values, axis=-1, keepdims=True)) + epsilon)
    return values * factor * gain

def rotate(values, places, sign):
    halfway = values.shape[-1] // 2
    frequency = rope_base ** (-jnp.arange(halfway, dtype=jnp.float32) / halfway)
    angles = places.astype(jnp.float32)[:, None] * frequency[None, :]
    cosine = jnp.cos(angles)[:, None, :]
    sine = sign * jnp.sin(angles)[:, None, :]
    first = values[..., :halfway]
    second = values[..., halfway:]
    return jnp.concatenate([first * cosine - second * sine, second * cosine + first * sine], axis=-1)

def attend(pieces):
    queries, keys_used, values_used = pieces
    length = queries.shape[0]
    raw_scores = jnp.einsum('qcgd,kcd->cgqk', queries, keys_used, precision=highest) * (1.0 / math.sqrt(HD))
    raw_scores = low_back(raw_scores)
    positions = jnp.arange(length)
    causal = positions[None, :] <= positions[:, None]
    raw_scores = jnp.where(causal, raw_scores, masked_score)
    weights = low(jax.nn.softmax(raw_scores, axis=-1))
    return jnp.einsum('cgqk,kcd->qcgd', weights, values_used, precision=highest)

def reference(hidden_in, attn_gain, w_query, w_key, w_value, w_output, moe_gain, w_gate, w_up, w_down, gate_logits, routes, out_grad):
    tokens = hidden_in.shape[0]
    sources = N_EXPERT
    route_count = tokens * TOP
    local_routes = routes.reshape(sources, TOK_DEV * TOP).astype(jnp.int32)
    route_hits = (local_routes[:, :, None] == jnp.arange(EXPERTS, dtype=jnp.int32)[None, None, :]).astype(jnp.int32)
    slot_index = lax.optimization_barrier(jnp.sum(jnp.cumsum(route_hits, axis=1) * route_hits, axis=-1)) - 1
    source_ids = jnp.arange(sources, dtype=jnp.int32)[:, None]
    flat_place = (local_routes * (sources * CAP) + source_ids * CAP + slot_index).reshape(-1).astype(jnp.int32)
    owners = jnp.full((EXPERTS * sources * CAP,), tokens, jnp.int32).at[flat_place].set((jnp.arange(route_count, dtype=jnp.int32) // TOP).astype(jnp.int32))
    owners = owners.reshape(EXPERTS, sources * CAP)
    gate_weights = jax.nn.softmax(gate_logits.astype(jnp.float32), axis=-1)
    places = jnp.arange(tokens, dtype=jnp.int32) % TOK_DEV
    groups = HEADS // KV
    sequences = tokens // TOK_DEV

    def forward(hidden, gain_one, query_w, key_w, value_w, output_w, gain_two, gate_w, up_w, down_w):
        normed = low(rms_scaled(hidden, gain_one))
        queries = low(rotate(low_back(product(normed, query_w)).reshape(tokens, HEADS, HD), places, 1.0))
        keys_used = low(rotate(low_back(product(normed, key_w)).reshape(tokens, KV, HD), places, 1.0))
        values_used = low_back(low(product(normed, value_w)))
        mixed_heads = lax.map(jax.checkpoint(attend), (queries.reshape(sequences, TOK_DEV, KV, groups, HD), keys_used.reshape(sequences, TOK_DEV, KV, HD), values_used.reshape(sequences, TOK_DEV, KV, HD)))
        mixed_heads = low_back(low(mixed_heads.reshape(tokens, HEADS * HD)))
        middle = hidden + low_back(product(mixed_heads, output_w))
        rows_in = low(rms_scaled(middle, gain_two))
        padded = jnp.concatenate([rows_in, jnp.zeros((1, rows_in.shape[1]), jnp.float32)], axis=0)

        def expert(pieces):
            gate_one, up_one, down_one, owner_rows = pieces
            arrived = low_back(padded[owner_rows])
            gate_pre = low_back(product(arrived, gate_one))
            up_pre = low_back(product(arrived, up_one))
            hidden_units = low(jax.nn.silu(gate_pre) * up_pre)
            return low_back(low(product(hidden_units, down_one)))
        produced = lax.map(jax.checkpoint(expert), (gate_w, up_w, down_w, owners))
        picked = produced.reshape(-1, produced.shape[-1])[flat_place].reshape(tokens, TOP, -1)
        return middle + lax.optimization_barrier(jnp.sum(gate_weights[:, :, None] * picked, axis=1))
    primals = (hidden_in.astype(jnp.float32), attn_gain.astype(jnp.float32), w_query.astype(jnp.float32), w_key.astype(jnp.float32), w_value.astype(jnp.float32), w_output.astype(jnp.float32), moe_gain.astype(jnp.float32), w_gate.astype(jnp.float32), w_up.astype(jnp.float32), w_down.astype(jnp.float32))
    result, pullback = jax.vjp(forward, *primals)
    grads = pullback(out_grad.astype(jnp.float32))
    return (result.astype(jnp.bfloat16), grads[0], grads[1], grads[2], grads[3], grads[4], grads[5], grads[6], grads[7], grads[8], grads[9])
```

```python
import math

import jax
import jax.numpy as jnp
from jax import lax
from jax.sharding import PartitionSpec as P

HD = 128


epsilon = 1e-06
rope_base = 10000.0
masked_score = -1e30


def rotate(values, places, sign):
    halfway = values.shape[-1] // 2
    frequency = rope_base ** (-jnp.arange(halfway, dtype=jnp.float32) / halfway)
    angles = places.astype(jnp.float32)[:, None] * frequency[None, :]
    cosine = jnp.cos(angles)[:, None, :]
    sine = sign * jnp.sin(angles)[:, None, :]
    first = values[..., :halfway]
    second = values[..., halfway:]
    return jnp.concatenate(
        [first * cosine - second * sine, second * cosine + first * sine], axis=-1
    )


def contract_rows(left, right):
    return lax.dot_general(
        left, right, (((0,), (0,)), ((), ())), preferred_element_type=jnp.float32
    )


def contract_cols(left, right):
    return lax.dot_general(
        left, right, (((1,), (1,)), ((), ())), preferred_element_type=jnp.float32
    )


def block_scores(query_block, keys_used, row_start, scale_factor):
    query_rows = query_block.shape[0]
    key_rows = keys_used.shape[0]
    raw_scores = (
        jnp.einsum("qcgd,kcd->cgqk", query_block, keys_used, preferred_element_type=jnp.float32)
        * scale_factor
    )
    row_ids = row_start + jnp.arange(query_rows)
    causal = jnp.arange(key_rows)[None, :] <= row_ids[:, None]
    return jnp.where(causal, raw_scores, masked_score)


def routed_slots(
    hidden_in,
    attn_gain,
    w_query,
    w_key,
    w_value,
    w_output,
    moe_gain,
    w_gate,
    w_up,
    w_down,
    gate_logits,
    routes,
    out_grad,
):
    tokens, model_width = hidden_in.shape
    experts = lax.axis_size("expert")
    tensor_ranks = lax.axis_size("tensor")
    tensor_rank = lax.axis_index("tensor")
    route_width = routes.shape[1]
    route_count = tokens * route_width
    capacity = 2 * route_count // experts
    half_slots = capacity // tensor_ranks
    heads_local = w_query.shape[1] // HD
    kv_local = w_key.shape[1] // HD
    groups = heads_local // kv_local
    scale_factor = 1.0 / math.sqrt(HD)
    block_rows = min(512, tokens)
    places = jnp.arange(tokens, dtype=jnp.int32)
    flat_routes = routes.reshape(-1)
    route_hits = (flat_routes[:, None] == jnp.arange(experts, dtype=jnp.int32)[None, :]).astype(
        jnp.int32
    )
    slot_index = jnp.sum(jnp.cumsum(route_hits, axis=0) * route_hits, axis=1) - 1
    which_route = (
        jnp.full((experts * capacity,), route_count, jnp.int32)
        .at[flat_routes * capacity + slot_index]
        .set(jnp.arange(route_count, dtype=jnp.int32))
    )
    which_token = which_route // route_width
    own_half = slot_index // half_slots == tensor_rank
    back_index = jnp.where(
        own_half, flat_routes * half_slots + slot_index % half_slots, experts * half_slots
    )
    gate_weights = jax.nn.softmax(gate_logits, axis=-1)
    full_gate, full_up, full_down = (w_gate[0], w_up[0], w_down[0])

    def deliver(buffer):
        arrived_all = lax.all_to_all(buffer, "expert", split_axis=0, concat_axis=0, tiled=True)
        return arrived_all.reshape(experts * capacity, model_width)

    def give_back(partial_value):
        summed_rows = lax.psum_scatter(
            partial_value.reshape(experts, capacity, model_width).astype(jnp.bfloat16),
            "tensor",
            scatter_dimension=1,
            tiled=True,
        )
        returned = lax.all_to_all(summed_rows, "expert", split_axis=0, concat_axis=0, tiled=True)
        return jnp.concatenate(
            [
                returned.reshape(experts * half_slots, model_width),
                jnp.zeros((1, model_width), jnp.bfloat16),
            ],
            axis=0,
        )

    def collect(returned, weights):
        picked = returned[back_index].astype(jnp.float32).reshape(tokens, route_width, model_width)
        return lax.psum(
            jnp.sum(picked * weights[:, :, None], axis=1).astype(jnp.bfloat16), "tensor"
        ).astype(jnp.float32)

    source = hidden_in.astype(jnp.float32)
    scale_one = lax.rsqrt(jnp.mean(source * source, axis=-1, keepdims=True) + epsilon)
    unit_one = source * scale_one
    normed = (unit_one * attn_gain).astype(jnp.bfloat16)
    query_pre = jnp.dot(normed, w_query, preferred_element_type=jnp.float32).reshape(
        tokens, heads_local, HD
    )
    queries = (
        rotate(query_pre, places, 1.0).astype(jnp.bfloat16).reshape(tokens, kv_local, groups, HD)
    )
    key_pre = jnp.dot(normed, w_key, preferred_element_type=jnp.float32).reshape(
        tokens, kv_local, HD
    )
    keys_used = rotate(key_pre, places, 1.0).astype(jnp.bfloat16)
    values_used = (
        jnp.dot(normed, w_value, preferred_element_type=jnp.float32)
        .astype(jnp.bfloat16)
        .reshape(tokens, kv_local, HD)
    )
    row_start = 0
    query_block = queries
    raw_scores = block_scores(query_block, keys_used, row_start, scale_factor)
    biggest = jnp.max(raw_scores, axis=-1, keepdims=True)
    exponent = jnp.exp(raw_scores - biggest)
    row_total = jnp.sum(exponent, axis=-1, keepdims=True)
    weights_low = (exponent / row_total).astype(jnp.bfloat16)
    logsums = [biggest + jnp.log(row_total)]
    attended = jnp.einsum(
        "cgqk,kcd->qcgd", weights_low, values_used, preferred_element_type=jnp.float32
    )
    mixed_blocks = attended.reshape(block_rows, heads_local * HD).astype(jnp.bfloat16)
    attn_part = jnp.dot(mixed_blocks, w_output, preferred_element_type=jnp.float32)
    middle = source + lax.psum(attn_part.astype(jnp.bfloat16), "tensor").astype(jnp.float32)
    scale_two = lax.rsqrt(jnp.mean(middle * middle, axis=-1, keepdims=True) + epsilon)
    unit_two = middle * scale_two
    rows_in = (unit_two * moe_gain).astype(jnp.bfloat16)
    padded_rows = jnp.concatenate([rows_in, jnp.zeros((1, model_width), jnp.bfloat16)], axis=0)
    arrived = deliver(padded_rows[which_token].reshape(experts, capacity, model_width))
    gate_pre = jnp.dot(arrived, full_gate, preferred_element_type=jnp.float32)
    up_pre = jnp.dot(arrived, full_up, preferred_element_type=jnp.float32)
    sigmoid = jax.nn.sigmoid(gate_pre)
    activated = gate_pre * sigmoid
    hidden_units = (activated * up_pre).astype(jnp.bfloat16)
    produced = jnp.dot(hidden_units, full_down, preferred_element_type=jnp.float32)
    moe_result = collect(give_back(produced), gate_weights)
    block_out = (middle + moe_result).astype(jnp.bfloat16)
    grad_out = out_grad.astype(jnp.float32)
    route_grads = (
        (gate_weights[:, :, None] * grad_out[:, None, :])
        .astype(jnp.bfloat16)
        .reshape(route_count, model_width)
    )
    padded_grads = jnp.concatenate([route_grads, jnp.zeros((1, model_width), jnp.bfloat16)], axis=0)
    grad_arrived = deliver(padded_grads[which_route].reshape(experts, capacity, model_width))
    grad_down = contract_rows(hidden_units, grad_arrived)
    grad_inner = contract_cols(grad_arrived, full_down)
    grad_gate_pre = (grad_inner * up_pre * sigmoid * (1.0 + gate_pre * (1.0 - sigmoid))).astype(
        jnp.bfloat16
    )
    grad_up_pre = (grad_inner * activated).astype(jnp.bfloat16)
    grad_gate = contract_rows(arrived, grad_gate_pre)
    grad_up = contract_rows(arrived, grad_up_pre)
    grad_arrived_rows = contract_cols(grad_gate_pre, full_gate) + contract_cols(
        grad_up_pre, full_up
    )
    grad_rows = collect(give_back(grad_arrived_rows), jnp.ones_like(gate_weights))
    grad_unit_two = grad_rows * moe_gain
    grad_moe_gain = jnp.sum(grad_rows * unit_two, axis=0)
    grad_middle = grad_out + scale_two * (
        grad_unit_two - unit_two * jnp.mean(grad_unit_two * unit_two, axis=-1, keepdims=True)
    )
    grad_attn = grad_middle.astype(jnp.bfloat16)
    grad_output = contract_rows(mixed_blocks, grad_attn)
    grad_mixed = (
        contract_cols(grad_attn, w_output)
        .astype(jnp.bfloat16)
        .reshape(tokens, kv_local, groups, HD)
    )
    grad_query_blocks = []
    grad_keys = jnp.zeros((tokens, kv_local, HD), jnp.float32)
    grad_values = jnp.zeros((tokens, kv_local, HD), jnp.float32)
    for block_number, row_start in enumerate(range(0, tokens, block_rows)):
        query_block = queries
        raw_scores = block_scores(query_block, keys_used, row_start, scale_factor)
        probs = jnp.exp(raw_scores - logsums[block_number])
        probs_low = probs.astype(jnp.bfloat16)
        grad_probs = jnp.einsum(
            "qcgd,kcd->cgqk", grad_mixed, values_used, preferred_element_type=jnp.float32
        )
        delta = jnp.sum(probs * grad_probs, axis=-1, keepdims=True)
        grad_scores = (probs * (grad_probs - delta)).astype(jnp.bfloat16)
        grad_query_blocks.append(
            jnp.einsum("cgqk,kcd->qcgd", grad_scores, keys_used, preferred_element_type=jnp.float32)
            * scale_factor
        )
        grad_keys = (
            jnp.einsum(
                "cgqk,qcgd->kcd", grad_scores, query_block, preferred_element_type=jnp.float32
            )
            * scale_factor
        )
        grad_values = jnp.einsum(
            "cgqk,qcgd->kcd", probs_low, grad_mixed, preferred_element_type=jnp.float32
        )
    grad_queries = grad_query_blocks[0].reshape(tokens, heads_local, HD)
    grad_query_pre = (
        rotate(grad_queries, places, -1.0).astype(jnp.bfloat16).reshape(tokens, heads_local * HD)
    )
    grad_key_pre = (
        rotate(grad_keys, places, -1.0).astype(jnp.bfloat16).reshape(tokens, kv_local * HD)
    )
    grad_value_pre = grad_values.astype(jnp.bfloat16).reshape(tokens, kv_local * HD)
    grad_query = contract_rows(normed, grad_query_pre)
    grad_key = contract_rows(normed, grad_key_pre)
    grad_value = contract_rows(normed, grad_value_pre)
    grad_normed_part = (
        contract_cols(grad_query_pre, w_query)
        + contract_cols(grad_key_pre, w_key)
        + contract_cols(grad_value_pre, w_value)
    )
    grad_normed = lax.psum(grad_normed_part.astype(jnp.bfloat16), "tensor").astype(jnp.float32)
    grad_unit_one = grad_normed * attn_gain
    grad_attn_gain = jnp.sum(grad_normed * unit_one, axis=0)
    grad_in = grad_middle + scale_one * (
        grad_unit_one - unit_one * jnp.mean(grad_unit_one * unit_one, axis=-1, keepdims=True)
    )
    summed = lax.psum(
        (grad_query, grad_key, grad_value, grad_output, grad_attn_gain, grad_moe_gain), "expert"
    )
    return (
        block_out,
        grad_in,
        summed[4],
        summed[0],
        summed[1],
        summed[2],
        summed[3],
        summed[5],
        grad_gate[None],
        grad_up[None],
        grad_down[None],
    )


def swap(value):
    return lax.ppermute(value, "tensor", [(0, 1), (1, 0)])


def flip(value, bit):
    places = lax.axis_size("expert")
    return lax.ppermute(value, "expert", [(i, i ^ bit) for i in range(places)])


def part(value, index, count):
    size = value.shape[0] // count
    return lax.dynamic_slice_in_dim(value, index * size, size, 0)


def ordered(own, other, place):
    return jnp.where(
        place == 0,
        jnp.concatenate([own, other], axis=0),
        jnp.concatenate([other, own], axis=0),
    )


def add_low(kept, arrived):
    return (kept.astype(jnp.float32) + arrived.astype(jnp.float32)).astype(jnp.bfloat16)


def plane_scatter(value, bit_x, bit_y):
    left, right = jnp.split(value, 2, axis=0)
    left = add_low(part(left, bit_x, 2), flip(part(left, 1 - bit_x, 2), 1))
    right = add_low(part(right, bit_y, 2), flip(part(right, 1 - bit_y, 2), 2))
    left = add_low(part(left, bit_y, 2), flip(part(left, 1 - bit_y, 2), 2))
    right = add_low(part(right, bit_x, 2), flip(part(right, 1 - bit_x, 2), 1))
    return left, right


def plane_gather(left, right, bit_x, bit_y):
    left = ordered(left, flip(left, 2), bit_y)
    right = ordered(right, flip(right, 1), bit_x)
    left = ordered(left, flip(left, 1), bit_x)
    right = ordered(right, flip(right, 2), bit_y)
    return jnp.concatenate([left, right], axis=0)


def sum_experts(value, columns, bit_x, bit_y):
    left, right = plane_scatter(value.astype(jnp.bfloat16), bit_x, bit_y)
    rows = left.shape[0]
    both = lax.psum(jnp.concatenate([left, right], axis=0), "expert", axis_index_groups=columns)
    return plane_gather(both[:rows], both[rows:], bit_x, bit_y).astype(jnp.float32)


def planes_of_four(
    hidden_in,
    attn_gain,
    w_query,
    w_key,
    w_value,
    w_output,
    moe_gain,
    w_gate,
    w_up,
    w_down,
    gate_logits,
    routes,
    out_grad,
):
    tokens, model_width = hidden_in.shape
    half_tokens = tokens // 2
    experts = lax.axis_size("expert")
    planes = experts // 4
    columns = [[4 * z + r for z in range(planes)] for r in range(4)]
    core = lax.axis_index("tensor")
    expert = lax.axis_index("expert")
    bit_x = expert % 2
    bit_y = (expert // 2) % 2
    heads_local = w_query.shape[1] // HD
    kv_local = w_key.shape[1] // HD
    groups = heads_local // kv_local
    scale_factor = 1.0 / math.sqrt(HD)
    places = jnp.arange(tokens, dtype=jnp.int32)
    hidden_local = w_down.shape[1]
    gathered = planes * half_tokens

    def column_gather(value):
        arrived = lax.all_gather(value, "expert", axis_index_groups=columns, axis=0, tiled=True)
        return jnp.concatenate([arrived, swap(arrived)], axis=0)

    def column_return(partial_value):
        own = add_low(partial_value[:gathered], swap(partial_value[gathered:].astype(jnp.bfloat16)))
        return lax.psum_scatter(
            own, "expert", axis_index_groups=columns, scatter_dimension=0, tiled=True
        ).astype(jnp.float32)

    gate_up = jnp.concatenate([w_gate[0], w_up[0]], axis=1)
    down = w_down[0]

    def plane_weights(own):
        beside_x = flip(own, 1)
        beside_y = flip(own, 2)
        middle_row = own.shape[0] // 2
        across = jnp.concatenate(
            [flip(beside_y[:middle_row], 1), flip(beside_x[middle_row:], 2)], axis=0
        )
        return [own, beside_x, beside_y, across]

    gate_up_all = plane_weights(gate_up)
    down_all = plane_weights(down)
    gates = jnp.concatenate([w[:, :hidden_local] for w in gate_up_all], axis=1)
    ups = jnp.concatenate([w[:, hidden_local:] for w in gate_up_all], axis=1)
    downs = jnp.concatenate(down_all, axis=0)

    gate_weights = jax.nn.softmax(gate_logits, axis=-1)
    names = jnp.arange(experts, dtype=jnp.int32)
    dense = jnp.sum(
        jnp.where(routes.T[:, None, :] == names[None, :, None], gate_weights.T[:, None, :], 0.0),
        axis=0,
    )
    dense_all = lax.all_gather(dense, "expert", axis_index_groups=columns, axis=0)
    mine = dense_all[:, expert ^ jnp.arange(4)]
    mine = mine.reshape(planes, 4, 2, half_tokens)[:, :, core ^ jnp.arange(2)]
    mine = mine.transpose(2, 0, 3, 1).reshape(2 * gathered, 4)
    route_weights = jnp.repeat(mine, hidden_local, axis=1)

    out_grad_half = part(out_grad, core, 2)
    grad_out_all = column_gather(out_grad_half)

    source = hidden_in.astype(jnp.float32)
    scale_one = lax.rsqrt(jnp.mean(source * source, axis=-1, keepdims=True) + epsilon)
    unit_one = source * scale_one
    normed = (unit_one * attn_gain).astype(jnp.bfloat16)
    query_pre = jnp.dot(normed, w_query, preferred_element_type=jnp.float32).reshape(
        tokens, heads_local, HD
    )
    queries = (
        rotate(query_pre, places, 1.0).astype(jnp.bfloat16).reshape(tokens, kv_local, groups, HD)
    )
    key_pre = jnp.dot(normed, w_key, preferred_element_type=jnp.float32).reshape(
        tokens, kv_local, HD
    )
    keys_used = rotate(key_pre, places, 1.0).astype(jnp.bfloat16)
    values_used = (
        jnp.dot(normed, w_value, preferred_element_type=jnp.float32)
        .astype(jnp.bfloat16)
        .reshape(tokens, kv_local, HD)
    )
    raw_scores = block_scores(queries, keys_used, 0, scale_factor)
    biggest = jnp.max(raw_scores, axis=-1, keepdims=True)
    exponent = jnp.exp(raw_scores - biggest)
    row_total = jnp.sum(exponent, axis=-1, keepdims=True)
    weights_low = (exponent / row_total).astype(jnp.bfloat16)
    logsum = biggest + jnp.log(row_total)
    attended = jnp.einsum(
        "cgqk,kcd->qcgd", weights_low, values_used, preferred_element_type=jnp.float32
    )
    mixed = attended.reshape(tokens, heads_local * HD).astype(jnp.bfloat16)
    attn_part = jnp.dot(mixed, w_output, preferred_element_type=jnp.float32).astype(jnp.bfloat16)

    source_half = part(source, core, 2)
    middle = source_half + (
        part(attn_part, core, 2).astype(jnp.float32)
        + swap(part(attn_part, 1 - core, 2)).astype(jnp.float32)
    )
    scale_two = lax.rsqrt(jnp.mean(middle * middle, axis=-1, keepdims=True) + epsilon)
    unit_two = middle * scale_two
    rows_in = (unit_two * moe_gain).astype(jnp.bfloat16)
    rows_all = column_gather(rows_in)

    gate_pre = jnp.dot(rows_all, gates, preferred_element_type=jnp.float32)
    up_pre = jnp.dot(rows_all, ups, preferred_element_type=jnp.float32)
    sigmoid = jax.nn.sigmoid(gate_pre)
    activated = gate_pre * sigmoid
    grad_inner = contract_cols(grad_out_all, downs) * route_weights
    grad_gate_pre = (grad_inner * up_pre * sigmoid * (1.0 + gate_pre * (1.0 - sigmoid))).astype(
        jnp.bfloat16
    )
    grad_up_pre = (grad_inner * activated).astype(jnp.bfloat16)
    inner = (activated * up_pre * route_weights).astype(jnp.bfloat16)
    grad_rows = column_return(contract_cols(grad_gate_pre, gates) + contract_cols(grad_up_pre, ups))
    moe_result = column_return(jnp.dot(inner, downs, preferred_element_type=jnp.float32))
    block_half = (middle + moe_result).astype(jnp.bfloat16)
    block_out = ordered(block_half, swap(block_half), core)

    grad_gate_all = contract_rows(rows_all, grad_gate_pre)
    grad_up_all = contract_rows(rows_all, grad_up_pre)
    grad_down_all = contract_rows(inner, grad_out_all)

    def plane_return(pieces):
        own, to_x, to_y, to_across = pieces
        middle_row = own.shape[0] // 2
        low_own = own
        first = flip(
            jnp.concatenate([to_x, to_across[:middle_row]], axis=0).astype(jnp.bfloat16), 1
        ).astype(jnp.float32)
        second = flip(
            jnp.concatenate([to_y, to_across[middle_row:]], axis=0).astype(jnp.bfloat16), 2
        ).astype(jnp.float32)
        rows = own.shape[0]
        on_y = flip(first[rows:].astype(jnp.bfloat16), 2).astype(jnp.float32)
        on_x = flip(second[rows:].astype(jnp.bfloat16), 1).astype(jnp.float32)
        return low_own + first[:rows] + second[:rows] + jnp.concatenate([on_y, on_x], axis=0)

    def pieces_of(value, axis):
        return jnp.split(value, 4, axis=axis)

    grad_gate = plane_return(pieces_of(grad_gate_all, 1))
    grad_up = plane_return(pieces_of(grad_up_all, 1))
    grad_down = plane_return(pieces_of(grad_down_all, 0))

    grad_out = out_grad_half.astype(jnp.float32)
    grad_unit_two = grad_rows * moe_gain
    grad_moe_gain = jnp.sum(grad_rows * unit_two, axis=0)
    grad_middle = grad_out + scale_two * (
        grad_unit_two - unit_two * jnp.mean(grad_unit_two * unit_two, axis=-1, keepdims=True)
    )
    grad_attn_half = grad_middle.astype(jnp.bfloat16)
    grad_attn = ordered(grad_attn_half, swap(grad_attn_half), core)
    grad_output = contract_rows(mixed, grad_attn)
    grad_mixed = (
        contract_cols(grad_attn, w_output)
        .astype(jnp.bfloat16)
        .reshape(tokens, kv_local, groups, HD)
    )
    raw_scores = block_scores(queries, keys_used, 0, scale_factor)
    probs = jnp.exp(raw_scores - logsum)
    probs_low = probs.astype(jnp.bfloat16)
    grad_probs = jnp.einsum(
        "qcgd,kcd->cgqk", grad_mixed, values_used, preferred_element_type=jnp.float32
    )
    delta = jnp.sum(probs * grad_probs, axis=-1, keepdims=True)
    grad_scores = (probs * (grad_probs - delta)).astype(jnp.bfloat16)
    grad_queries = (
        jnp.einsum("cgqk,kcd->qcgd", grad_scores, keys_used, preferred_element_type=jnp.float32)
        * scale_factor
    ).reshape(tokens, heads_local, HD)
    grad_keys = (
        jnp.einsum("cgqk,qcgd->kcd", grad_scores, queries, preferred_element_type=jnp.float32)
        * scale_factor
    )
    grad_values = jnp.einsum(
        "cgqk,qcgd->kcd", probs_low, grad_mixed, preferred_element_type=jnp.float32
    )
    grad_query_pre = (
        rotate(grad_queries, places, -1.0).astype(jnp.bfloat16).reshape(tokens, heads_local * HD)
    )
    grad_key_pre = (
        rotate(grad_keys, places, -1.0).astype(jnp.bfloat16).reshape(tokens, kv_local * HD)
    )
    grad_value_pre = grad_values.astype(jnp.bfloat16).reshape(tokens, kv_local * HD)
    grad_all_pre = jnp.concatenate([grad_query_pre, grad_key_pre, grad_value_pre], axis=1)
    w_all = jnp.concatenate([w_query, w_key, w_value], axis=1)
    grad_projections = contract_rows(normed, grad_all_pre)
    grad_normed_part = contract_cols(grad_all_pre, w_all).astype(jnp.bfloat16)
    grad_normed = part(grad_normed_part, core, 2).astype(jnp.float32) + swap(
        part(grad_normed_part, 1 - core, 2)
    ).astype(jnp.float32)
    grad_unit_one = grad_normed * attn_gain
    unit_half = part(unit_one, core, 2)
    scale_half = part(scale_one, core, 2)
    grad_attn_gain = jnp.sum(grad_normed * unit_half, axis=0)
    grad_in_half = grad_middle + scale_half * (
        grad_unit_one - unit_half * jnp.mean(grad_unit_one * unit_half, axis=-1, keepdims=True)
    )
    grad_in = ordered(grad_in_half, swap(grad_in_half), core)
    gains = lax.psum(jnp.stack([grad_attn_gain, grad_moe_gain]), ("expert", "tensor"))
    output_sum = sum_experts(grad_output, columns, bit_x, bit_y)
    projection_sum = sum_experts(grad_projections, columns, bit_x, bit_y)
    query_width = w_query.shape[1]
    key_width = w_key.shape[1]
    return (
        block_out,
        grad_in,
        gains[0],
        projection_sum[:, :query_width],
        projection_sum[:, query_width : query_width + key_width],
        projection_sum[:, query_width + key_width :],
        output_sum,
        gains[1],
        grad_gate[None],
        grad_up[None],
        grad_down[None],
    )


def solution(mesh):
    on_device = planes_of_four if mesh.shape["expert"] == 16 else routed_slots
    return jax.shard_map(
        on_device,
        mesh=mesh,
        in_specs=(
            P("expert", None),
            P(),
            P(None, "tensor"),
            P(None, "tensor"),
            P(None, "tensor"),
            P("tensor", None),
            P(),
            P("expert", None, "tensor"),
            P("expert", None, "tensor"),
            P("expert", "tensor", None),
            P("expert", None),
            P("expert", None),
            P("expert", None),
        ),
        out_specs=(
            P("expert", None),
            P("expert", None),
            P(),
            P(None, "tensor"),
            P(None, "tensor"),
            P(None, "tensor"),
            P("tensor", None),
            P(),
            P("expert", None, "tensor"),
            P("expert", None, "tensor"),
            P("expert", "tensor", None),
        ),
        check_vma=False,
    )
```

```python
import math

import jax
import jax.numpy as jnp
import numpy as np
from jax import lax
from jax.experimental import pallas as pl
from jax.experimental.pallas import tpu as pltpu
from jax.sharding import PartitionSpec as P

HD = 128


epsilon = 1e-06
rope_base = 10000.0
masked_score = -1e30


def rotate(values, places, sign):
    halfway = values.shape[-1] // 2
    frequency = rope_base ** (-jnp.arange(halfway, dtype=jnp.float32) / halfway)
    angles = places.astype(jnp.float32)[:, None] * frequency[None, :]
    cosine = jnp.cos(angles)[:, None, :]
    sine = sign * jnp.sin(angles)[:, None, :]
    first = values[..., :halfway]
    second = values[..., halfway:]
    return jnp.concatenate(
        [first * cosine - second * sine, second * cosine + first * sine], axis=-1
    )


def contract_rows(left, right):
    return lax.dot_general(
        left, right, (((0,), (0,)), ((), ())), preferred_element_type=jnp.float32
    )


def contract_cols(left, right):
    return lax.dot_general(
        left, right, (((1,), (1,)), ((), ())), preferred_element_type=jnp.float32
    )


def block_scores(query_block, keys_used, row_start, scale_factor):
    query_rows = query_block.shape[0]
    key_rows = keys_used.shape[0]
    raw_scores = (
        jnp.einsum("qcgd,kcd->cgqk", query_block, keys_used, preferred_element_type=jnp.float32)
        * scale_factor
    )
    row_ids = row_start + jnp.arange(query_rows)
    causal = jnp.arange(key_rows)[None, :] <= row_ids[:, None]
    return jnp.where(causal, raw_scores, masked_score)


def routed_slots(
    hidden_in,
    attn_gain,
    w_query,
    w_key,
    w_value,
    w_output,
    moe_gain,
    w_gate,
    w_up,
    w_down,
    gate_logits,
    routes,
    out_grad,
):
    tokens, model_width = hidden_in.shape
    experts = lax.axis_size("expert")
    tensor_ranks = lax.axis_size("tensor")
    tensor_rank = lax.axis_index("tensor")
    route_width = routes.shape[1]
    route_count = tokens * route_width
    capacity = 2 * route_count // experts
    half_slots = capacity // tensor_ranks
    heads_local = w_query.shape[1] // HD
    kv_local = w_key.shape[1] // HD
    groups = heads_local // kv_local
    scale_factor = 1.0 / math.sqrt(HD)
    block_rows = min(512, tokens)
    places = jnp.arange(tokens, dtype=jnp.int32)
    flat_routes = routes.reshape(-1)
    route_hits = (flat_routes[:, None] == jnp.arange(experts, dtype=jnp.int32)[None, :]).astype(
        jnp.int32
    )
    slot_index = jnp.sum(jnp.cumsum(route_hits, axis=0) * route_hits, axis=1) - 1
    which_route = (
        jnp.full((experts * capacity,), route_count, jnp.int32)
        .at[flat_routes * capacity + slot_index]
        .set(jnp.arange(route_count, dtype=jnp.int32))
    )
    which_token = which_route // route_width
    own_half = slot_index // half_slots == tensor_rank
    back_index = jnp.where(
        own_half, flat_routes * half_slots + slot_index % half_slots, experts * half_slots
    )
    gate_weights = jax.nn.softmax(gate_logits, axis=-1)
    full_gate, full_up, full_down = (w_gate[0], w_up[0], w_down[0])

    def deliver(buffer):
        arrived_all = lax.all_to_all(buffer, "expert", split_axis=0, concat_axis=0, tiled=True)
        return arrived_all.reshape(experts * capacity, model_width)

    def give_back(partial_value):
        summed_rows = lax.psum_scatter(
            partial_value.reshape(experts, capacity, model_width).astype(jnp.bfloat16),
            "tensor",
            scatter_dimension=1,
            tiled=True,
        )
        returned = lax.all_to_all(summed_rows, "expert", split_axis=0, concat_axis=0, tiled=True)
        return jnp.concatenate(
            [
                returned.reshape(experts * half_slots, model_width),
                jnp.zeros((1, model_width), jnp.bfloat16),
            ],
            axis=0,
        )

    def collect(returned, weights):
        picked = returned[back_index].astype(jnp.float32).reshape(tokens, route_width, model_width)
        return lax.psum(
            jnp.sum(picked * weights[:, :, None], axis=1).astype(jnp.bfloat16), "tensor"
        ).astype(jnp.float32)

    source = hidden_in.astype(jnp.float32)
    scale_one = lax.rsqrt(jnp.mean(source * source, axis=-1, keepdims=True) + epsilon)
    unit_one = source * scale_one
    normed = (unit_one * attn_gain).astype(jnp.bfloat16)
    query_pre = jnp.dot(normed, w_query, preferred_element_type=jnp.float32).reshape(
        tokens, heads_local, HD
    )
    queries = (
        rotate(query_pre, places, 1.0).astype(jnp.bfloat16).reshape(tokens, kv_local, groups, HD)
    )
    key_pre = jnp.dot(normed, w_key, preferred_element_type=jnp.float32).reshape(
        tokens, kv_local, HD
    )
    keys_used = rotate(key_pre, places, 1.0).astype(jnp.bfloat16)
    values_used = (
        jnp.dot(normed, w_value, preferred_element_type=jnp.float32)
        .astype(jnp.bfloat16)
        .reshape(tokens, kv_local, HD)
    )
    row_start = 0
    query_block = queries
    raw_scores = block_scores(query_block, keys_used, row_start, scale_factor)
    biggest = jnp.max(raw_scores, axis=-1, keepdims=True)
    exponent = jnp.exp(raw_scores - biggest)
    row_total = jnp.sum(exponent, axis=-1, keepdims=True)
    weights_low = (exponent / row_total).astype(jnp.bfloat16)
    logsums = [biggest + jnp.log(row_total)]
    attended = jnp.einsum(
        "cgqk,kcd->qcgd", weights_low, values_used, preferred_element_type=jnp.float32
    )
    mixed_blocks = attended.reshape(block_rows, heads_local * HD).astype(jnp.bfloat16)
    attn_part = jnp.dot(mixed_blocks, w_output, preferred_element_type=jnp.float32)
    middle = source + lax.psum(attn_part.astype(jnp.bfloat16), "tensor").astype(jnp.float32)
    scale_two = lax.rsqrt(jnp.mean(middle * middle, axis=-1, keepdims=True) + epsilon)
    unit_two = middle * scale_two
    rows_in = (unit_two * moe_gain).astype(jnp.bfloat16)
    padded_rows = jnp.concatenate([rows_in, jnp.zeros((1, model_width), jnp.bfloat16)], axis=0)
    arrived = deliver(padded_rows[which_token].reshape(experts, capacity, model_width))
    gate_pre = jnp.dot(arrived, full_gate, preferred_element_type=jnp.float32)
    up_pre = jnp.dot(arrived, full_up, preferred_element_type=jnp.float32)
    sigmoid = jax.nn.sigmoid(gate_pre)
    activated = gate_pre * sigmoid
    hidden_units = (activated * up_pre).astype(jnp.bfloat16)
    produced = jnp.dot(hidden_units, full_down, preferred_element_type=jnp.float32)
    moe_result = collect(give_back(produced), gate_weights)
    block_out = (middle + moe_result).astype(jnp.bfloat16)
    grad_out = out_grad.astype(jnp.float32)
    route_grads = (
        (gate_weights[:, :, None] * grad_out[:, None, :])
        .astype(jnp.bfloat16)
        .reshape(route_count, model_width)
    )
    padded_grads = jnp.concatenate([route_grads, jnp.zeros((1, model_width), jnp.bfloat16)], axis=0)
    grad_arrived = deliver(padded_grads[which_route].reshape(experts, capacity, model_width))
    grad_down = contract_rows(hidden_units, grad_arrived)
    grad_inner = contract_cols(grad_arrived, full_down)
    grad_gate_pre = (grad_inner * up_pre * sigmoid * (1.0 + gate_pre * (1.0 - sigmoid))).astype(
        jnp.bfloat16
    )
    grad_up_pre = (grad_inner * activated).astype(jnp.bfloat16)
    grad_gate = contract_rows(arrived, grad_gate_pre)
    grad_up = contract_rows(arrived, grad_up_pre)
    grad_arrived_rows = contract_cols(grad_gate_pre, full_gate) + contract_cols(
        grad_up_pre, full_up
    )
    grad_rows = collect(give_back(grad_arrived_rows), jnp.ones_like(gate_weights))
    grad_unit_two = grad_rows * moe_gain
    grad_moe_gain = jnp.sum(grad_rows * unit_two, axis=0)
    grad_middle = grad_out + scale_two * (
        grad_unit_two - unit_two * jnp.mean(grad_unit_two * unit_two, axis=-1, keepdims=True)
    )
    grad_attn = grad_middle.astype(jnp.bfloat16)
    grad_output = contract_rows(mixed_blocks, grad_attn)
    grad_mixed = (
        contract_cols(grad_attn, w_output)
        .astype(jnp.bfloat16)
        .reshape(tokens, kv_local, groups, HD)
    )
    grad_query_blocks = []
    grad_keys = jnp.zeros((tokens, kv_local, HD), jnp.float32)
    grad_values = jnp.zeros((tokens, kv_local, HD), jnp.float32)
    for block_number, row_start in enumerate(range(0, tokens, block_rows)):
        query_block = queries
        raw_scores = block_scores(query_block, keys_used, row_start, scale_factor)
        probs = jnp.exp(raw_scores - logsums[block_number])
        probs_low = probs.astype(jnp.bfloat16)
        grad_probs = jnp.einsum(
            "qcgd,kcd->cgqk", grad_mixed, values_used, preferred_element_type=jnp.float32
        )
        delta = jnp.sum(probs * grad_probs, axis=-1, keepdims=True)
        grad_scores = (probs * (grad_probs - delta)).astype(jnp.bfloat16)
        grad_query_blocks.append(
            jnp.einsum("cgqk,kcd->qcgd", grad_scores, keys_used, preferred_element_type=jnp.float32)
            * scale_factor
        )
        grad_keys = (
            jnp.einsum(
                "cgqk,qcgd->kcd", grad_scores, query_block, preferred_element_type=jnp.float32
            )
            * scale_factor
        )
        grad_values = jnp.einsum(
            "cgqk,qcgd->kcd", probs_low, grad_mixed, preferred_element_type=jnp.float32
        )
    grad_queries = grad_query_blocks[0].reshape(tokens, heads_local, HD)
    grad_query_pre = (
        rotate(grad_queries, places, -1.0).astype(jnp.bfloat16).reshape(tokens, heads_local * HD)
    )
    grad_key_pre = (
        rotate(grad_keys, places, -1.0).astype(jnp.bfloat16).reshape(tokens, kv_local * HD)
    )
    grad_value_pre = grad_values.astype(jnp.bfloat16).reshape(tokens, kv_local * HD)
    grad_query = contract_rows(normed, grad_query_pre)
    grad_key = contract_rows(normed, grad_key_pre)
    grad_value = contract_rows(normed, grad_value_pre)
    grad_normed_part = (
        contract_cols(grad_query_pre, w_query)
        + contract_cols(grad_key_pre, w_key)
        + contract_cols(grad_value_pre, w_value)
    )
    grad_normed = lax.psum(grad_normed_part.astype(jnp.bfloat16), "tensor").astype(jnp.float32)
    grad_unit_one = grad_normed * attn_gain
    grad_attn_gain = jnp.sum(grad_normed * unit_one, axis=0)
    grad_in = grad_middle + scale_one * (
        grad_unit_one - unit_one * jnp.mean(grad_unit_one * unit_one, axis=-1, keepdims=True)
    )
    summed = lax.psum(
        (grad_query, grad_key, grad_value, grad_output, grad_attn_gain, grad_moe_gain), "expert"
    )
    return (
        block_out,
        grad_in,
        summed[4],
        summed[0],
        summed[1],
        summed[2],
        summed[3],
        summed[5],
        grad_gate[None],
        grad_up[None],
        grad_down[None],
    )


VMEM_BYTES = 60 * 2**20


def small_cost(**_):
    return pl.CostEstimate(flops=1000, bytes_accessed=1000, transcendentals=0)


def dot(left, right):
    return jnp.dot(left, right, preferred_element_type=jnp.float32)


def whole(*shape):
    return pl.BlockSpec(shape, lambda *_: (0,) * len(shape), pipeline_mode=pl.Buffered(1))


def swap(value):
    return lax.ppermute(value, "tensor", [(0, 1), (1, 0)])


def flip(value, bit):
    places = lax.axis_size("expert")
    return lax.ppermute(value, "expert", [(i, i ^ bit) for i in range(places)])


def climb(value):
    places = lax.axis_size("expert")
    return lax.ppermute(value, "expert", [(i, i + 4) for i in range(places - 4)])


def descend(value):
    places = lax.axis_size("expert")
    return lax.ppermute(value, "expert", [(i + 4, i) for i in range(places - 4)])


def part(value, index, count):
    size = value.shape[0] // count
    return lax.dynamic_slice_in_dim(value, index * size, size, 0)


def ordered(own, other, place):
    return jnp.where(
        place == 0,
        jnp.concatenate([own, other], axis=0),
        jnp.concatenate([other, own], axis=0),
    )


def add_low(kept, arrived):
    return (kept.astype(jnp.float32) + arrived.astype(jnp.float32)).astype(jnp.bfloat16)


def plane_scatter_first(value, bit_x, bit_y):
    left, right = jnp.split(value, 2, axis=0)
    left = add_low(part(left, bit_x, 2), flip(part(left, 1 - bit_x, 2), 1))
    right = add_low(part(right, bit_y, 2), flip(part(right, 1 - bit_y, 2), 2))
    return left, right


def plane_scatter_second(halves, bit_x, bit_y):
    left, right = halves
    left = add_low(part(left, bit_y, 2), flip(part(left, 1 - bit_y, 2), 2))
    right = add_low(part(right, bit_x, 2), flip(part(right, 1 - bit_x, 2), 1))
    return left, right


def plane_gather(left, right, bit_x, bit_y):
    left = ordered(left, flip(left, 2), bit_y)
    right = ordered(right, flip(right, 1), bit_x)
    left = ordered(left, flip(left, 1), bit_x)
    right = ordered(right, flip(right, 2), bit_y)
    return jnp.concatenate([left, right], axis=0)


def rotary_tables(tokens):
    halfway = HD // 2
    frequency = rope_base ** (-np.arange(halfway, dtype=np.float64) / halfway)
    angles = np.arange(tokens)[:, None] * frequency[None, :]
    cosine, sine = np.cos(angles), np.sin(angles)
    return (
        np.concatenate([cosine, cosine], axis=1).astype(np.float32),
        np.concatenate([-sine, sine], axis=1).astype(np.float32),
    )


def causal_scores(query_block, keys, row_start, scale_factor):
    raw = contract_cols(query_block, keys) * scale_factor
    row_ids = row_start + lax.broadcasted_iota(jnp.int32, raw.shape, 0)
    return jnp.where(lax.broadcasted_iota(jnp.int32, raw.shape, 1) <= row_ids, raw, masked_score)


def softmax_rows(raw):
    exponent = jnp.exp(raw - jnp.max(raw, axis=-1, keepdims=True))
    return exponent / jnp.sum(exponent, axis=-1, keepdims=True)


def attention_forward(core, hidden, gain, w_query, w_key, w_value, w_output, cosine, sine):
    tokens, width = hidden.shape
    half = tokens // 2
    local = w_query.shape[1]
    heads = local // HD
    scale_factor = 1.0 / math.sqrt(HD)

    def kernel(
        core_ref, hidden_ref, gain_ref, wq_ref, wk_ref, wv_ref, wo_ref, cos_ref, sin_ref,
        normed_ref, query_ref, key_ref, value_ref, mixed_ref, keep_ref, send_ref, part_ref,
    ):
        for block in range(2):
            rows = pl.ds(block * half, half)
            source = hidden_ref[rows, :].astype(jnp.float32)
            scale = lax.rsqrt(jnp.mean(source * source, axis=-1, keepdims=True) + epsilon)
            normed = (source * scale * gain_ref[...]).astype(jnp.bfloat16)
            normed_ref[rows, :] = normed
            cos, sin = cos_ref[rows, :], sin_ref[rows, :]

            def turned(value):
                return (value * cos + pltpu.roll(value, HD // 2, 1) * sin).astype(jnp.bfloat16)

            query_pre = dot(normed, wq_ref[...])
            for head in range(heads):
                lanes = slice(head * HD, (head + 1) * HD)
                query_ref[rows, lanes] = turned(query_pre[:, lanes])
            key_ref[rows, :] = turned(dot(normed, wk_ref[...]))
            value_ref[rows, :] = dot(normed, wv_ref[...]).astype(jnp.bfloat16)
        for block in range(2):
            rows = pl.ds(block * half, half)
            seen = pl.ds(0, (block + 1) * half)
            keys, values = key_ref[seen, :], value_ref[seen, :]
            for head in range(heads):
                lanes = slice(head * HD, (head + 1) * HD)
                raw = causal_scores(query_ref[rows, lanes], keys, block * half, scale_factor)
                probs_low = softmax_rows(raw).astype(jnp.bfloat16)
                mixed_ref[rows, lanes] = dot(probs_low, values).astype(jnp.bfloat16)
            part_ref[rows, :] = dot(mixed_ref[rows, :], wo_ref[...])
        own = pl.ds(pl.multiple_of(core_ref[0] * half, half), half)
        other = pl.ds(pl.multiple_of((1 - core_ref[0]) * half, half), half)
        keep_ref[...] = hidden_ref[own, :].astype(jnp.float32) + part_ref[own, :]
        send_ref[...] = part_ref[other, :].astype(jnp.bfloat16)

    def low(rows, columns):
        return jax.ShapeDtypeStruct((rows, columns), jnp.bfloat16)

    shapes = [
        low(tokens, width), low(tokens, local), low(tokens, HD), low(tokens, HD),
        low(tokens, local), jax.ShapeDtypeStruct((half, width), jnp.float32), low(half, width),
    ]
    operands = [hidden, gain, w_query, w_key, w_value, w_output, cosine, sine]
    return pl.pallas_call(
        kernel,
        out_shape=shapes,
        in_specs=[pl.BlockSpec(memory_space=pltpu.SMEM)]
        + [pl.BlockSpec(memory_space=pltpu.VMEM) for _ in operands],
        out_specs=[pl.BlockSpec(memory_space=pltpu.VMEM) for _ in shapes],
        scratch_shapes=[pltpu.VMEM((tokens, width), jnp.float32)],
        compiler_params=pltpu.CompilerParams(vmem_limit_bytes=VMEM_BYTES),
        cost_estimate=small_cost(
            flops=40 * 10**9, bytes_accessed=16 * 10**6, transcendentals=2 * 10**6
        ),
        name="attention_forward",
    )(core, *operands)


def attention_backward(grad_mixed, queries, keys, values, cosine, sine):
    tokens, local = queries.shape
    half = tokens // 2
    heads = local // HD
    scale_factor = 1.0 / math.sqrt(HD)

    def kernel(gm_ref, query_ref, key_ref, value_ref, cos_ref, sin_ref, grad_ref, gk_ref, gv_ref):
        for block in range(2):
            rows = pl.ds(block * half, half)
            seen = pl.ds(0, (block + 1) * half)
            keys, values = key_ref[seen, :], value_ref[seen, :]
            cos, sin = cos_ref[rows, :], sin_ref[rows, :]
            grad_keys = jnp.zeros(((block + 1) * half, HD), jnp.float32)
            grad_values = grad_keys
            for head in range(heads):
                lanes = slice(head * HD, (head + 1) * HD)
                query, grad = query_ref[rows, lanes], gm_ref[rows, lanes]
                probs = softmax_rows(causal_scores(query, keys, block * half, scale_factor))
                grad_probs = contract_cols(grad, values)
                delta = jnp.sum(probs * grad_probs, axis=-1, keepdims=True)
                grad_scores = (probs * (grad_probs - delta)).astype(jnp.bfloat16)
                turned = dot(grad_scores, keys) * scale_factor
                grad_ref[rows, lanes] = (
                    turned * cos - pltpu.roll(turned, HD // 2, 1) * sin
                ).astype(jnp.bfloat16)
                grad_keys = grad_keys + contract_rows(grad_scores, query)
                grad_values = grad_values + contract_rows(probs.astype(jnp.bfloat16), grad)
            if block == 0:
                gk_ref[pl.ds(0, half), :] = grad_keys
                gv_ref[pl.ds(0, half), :] = grad_values
            else:
                first = pl.ds(0, half)
                gk_ref[first, :] = gk_ref[first, :] + grad_keys[:half]
                gv_ref[first, :] = gv_ref[first, :] + grad_values[:half]
                gk_ref[rows, :] = grad_keys[half:]
                gv_ref[rows, :] = grad_values[half:]
        turned = gk_ref[...] * scale_factor
        grad_ref[:, local : local + HD] = (
            turned * cos_ref[...] - pltpu.roll(turned, HD // 2, 1) * sin_ref[...]
        ).astype(jnp.bfloat16)
        grad_ref[:, local + HD :] = gv_ref[...].astype(jnp.bfloat16)

    return pl.pallas_call(
        kernel,
        out_shape=jax.ShapeDtypeStruct((tokens, local + 2 * HD), jnp.bfloat16),
        in_specs=[pl.BlockSpec(memory_space=pltpu.VMEM)] * 6,
        out_specs=pl.BlockSpec(memory_space=pltpu.VMEM),
        scratch_shapes=[pltpu.VMEM((tokens, HD), jnp.float32)] * 2,
        compiler_params=pltpu.CompilerParams(vmem_limit_bytes=VMEM_BYTES),
        cost_estimate=small_cost(
            flops=10 * 10**9, bytes_accessed=4 * 10**6, transcendentals=2 * 10**6
        ),
        name="attention_backward",
    )(grad_mixed, queries, keys, values, cosine, sine)


def expert_weights_of(expert_ref, packs, half):
    start = 2 * half
    count = packs[0].shape[0] - start
    row_ids = lax.broadcasted_iota(jnp.int32, (count, 128), 0)
    lane_ids = lax.broadcasted_iota(jnp.int32, (count, 128), 1)
    pick = (row_ids == (expert_ref[0] ^ lane_ids)).astype(jnp.bfloat16)
    sides = []
    for ref in packs:
        coarse, fine = ref[start:, :half], ref[start:, half : 2 * half]
        sides.append(contract_rows(coarse, pick) + contract_rows(fine, pick))
    return jnp.concatenate(sides, axis=0)


def expert_terms(expert, sequences, counts, pieces, first, keep):
    width = sequences[0][0].shape[1]
    half = sequences[0][0].shape[0] // 2 // 128 * 128
    stacked = not isinstance(pieces, list)
    number = pieces.shape[0] if stacked else len(pieces)
    flat_pieces = [pieces] if stacked else [piece for own in pieces for piece in own]
    columns = flat_pieces[0].shape[-1]
    hidden = columns // 3
    tokens = 2 * half
    total = len(sequences)
    flat = [array for sequence in sequences for array in sequence]

    loads = []
    if stacked:
        loads = [[(0, e, 0, width)] for e in range(number)]
    else:
        n = 0
        for own in pieces:
            loads.append([])
            place = 0
            for piece in own:
                loads[-1].append((n, None, place, piece.shape[0]))
                place += piece.shape[0]
                n += 1
    copy_count = sum(len(own) for own in loads)

    def kernel(expert_ref, *refs):
        sources, refs = refs[: len(flat)], refs[len(flat) :]
        piece_refs, refs = refs[: len(flat_pieces)], refs[len(flat_pieces) :]
        results, (w_ref, gate_all, semaphores) = refs[:-3], refs[-3:]
        e = pl.program_id(0)

        def copies_of(one):
            n = sum(len(own) for own in loads[:one])
            for which, index, place, rows in loads[one]:
                source = piece_refs[which] if index is None else piece_refs[which].at[index]
                yield pltpu.make_async_copy(
                    source, w_ref.at[one, pl.ds(place, rows), :], semaphores.at[n]
                )
                n += 1

        def kept(one):
            return pltpu.make_async_copy(
                w_ref.at[one], results[-1].at[one], semaphores.at[copy_count + one]
            )

        @pl.when(e == 0)
        def _():
            for one in range(number):
                for copy in copies_of(one):
                    copy.start()
            for s in range(total):
                gate_all[s * tokens : (s + 1) * tokens, :] = expert_weights_of(
                    expert_ref, sources[2 * s : 2 * s + 2], half
                )

        for one in range(number):

            @pl.when(e == one)
            def _(one=one):
                for copy in copies_of(one):
                    copy.wait()
                if keep:
                    kept(one).start()

        lanes = lax.broadcasted_iota(jnp.int32, (half, 128), 1)
        n = 0
        for joined, count in enumerate(counts):
            inner_ref, grad_ref = results[2 * joined : 2 * joined + 2]
            for s in range(count):
                for side in range(2):
                    pack = sources[2 * n + side]
                    here = pl.ds(s * tokens + side * half, half)
                    gate = gate_all[n * tokens + side * half : n * tokens + (side + 1) * half, :]
                    weight = jnp.sum(jnp.where(lanes == e + first, gate, 0.0), axis=1, keepdims=True)
                    both = dot(pack[:half, :], w_ref[e, :, : 2 * hidden])
                    grad_inner = dot(pack[half : 2 * half, :], w_ref[e, :, 2 * hidden :]) * weight
                    gate_pre, up_pre = both[:, :hidden], both[:, hidden:]
                    sigmoid = jax.nn.sigmoid(gate_pre)
                    activated = gate_pre * sigmoid
                    grad_gate = grad_inner * up_pre * sigmoid * (1.0 + gate_pre * (1.0 - sigmoid))
                    grad_ref[here, :hidden] = grad_gate.astype(jnp.bfloat16)
                    grad_ref[here, hidden:] = (grad_inner * activated).astype(jnp.bfloat16)
                    inner_ref[here, :] = (activated * up_pre * weight).astype(jnp.bfloat16)
                n += 1

        if keep:

            @pl.when(e == number - 1)
            def _():
                for one in range(number):
                    kept(one).wait()

    out_specs, out_shape = [], []
    for count in counts:
        for size in (hidden, 2 * hidden):
            out_specs.append(pl.BlockSpec((count * tokens, size), lambda e: (0, e)))
            out_shape.append(jax.ShapeDtypeStruct((count * tokens, number * size), jnp.bfloat16))
    if keep:
        out_specs.append(pl.BlockSpec(memory_space=pl.ANY))
        out_shape.append(jax.ShapeDtypeStruct((number, width, columns), jnp.bfloat16))
    results = pl.pallas_call(
        kernel,
        grid=(number,),
        in_specs=[pl.BlockSpec(memory_space=pltpu.SMEM)]
        + [whole(*array.shape) for array in flat]
        + [pl.BlockSpec(memory_space=pl.ANY)] * len(flat_pieces),
        out_specs=out_specs,
        out_shape=out_shape,
        scratch_shapes=[
            pltpu.VMEM((number, width, columns), jnp.bfloat16),
            pltpu.VMEM((total * tokens, 128), jnp.float32),
            pltpu.SemaphoreType.DMA((copy_count + number,)),
        ],
        compiler_params=pltpu.CompilerParams(vmem_limit_bytes=VMEM_BYTES),
        cost_estimate=small_cost(
            flops=total * number * 6 * tokens * width * hidden,
            bytes_accessed=(total + number) * 4 * 10**6,
            transcendentals=total * number * tokens * hidden,
        ),
        name="expert_terms",
    )(expert, *flat, *flat_pieces)
    terms = [tuple(results[2 * n : 2 * n + 2]) for n in range(len(counts))]
    return (*terms, results[-1]) if keep else tuple(terms)


def expert_sums(near, far, near_weights, far_weights, half):
    rows, columns = near[0].shape
    number, width = near_weights.shape[:2]
    hidden = columns // number
    count = rows // (2 * half)
    block = 256

    def kernel(inner_ref, grad_ref, inner_far, grad_far, w_ref, w_far, back_own, back_other, out_own, out_other):
        def added(near_ref, far_ref, size, lanes):
            total = contract_cols(far_ref[...], w_far[0, :, lanes])
            for e in range(number):
                total += contract_cols(near_ref[:, e * size : (e + 1) * size], w_ref[e, :, lanes])
            return total

        back = added(grad_ref, grad_far, 2 * hidden, slice(0, 2 * hidden))
        out = added(inner_ref, inner_far, hidden, slice(2 * hidden, 3 * hidden))
        for s in range(count):
            start = 2 * s * half
            back_own[s] = back[start : start + half]
            back_other[s] = back[start + half : start + 2 * half].astype(jnp.bfloat16)
            out_own[s] = out[start : start + half]
            out_other[s] = out[start + half : start + 2 * half].astype(jnp.bfloat16)

    wide = jax.ShapeDtypeStruct((count, half, width), jnp.float32)
    low = jax.ShapeDtypeStruct((count, half, width), jnp.bfloat16)
    return pl.pallas_call(
        kernel,
        grid=(width // block,),
        in_specs=[whole(*a.shape) for a in (*near, *far)]
        + [
            pl.BlockSpec((number, block, 3 * hidden), lambda n: (0, n, 0)),
            pl.BlockSpec((1, block, 3 * hidden), lambda n: (0, n, 0)),
        ],
        out_specs=[pl.BlockSpec((count, half, block), lambda n: (0, 0, n))] * 4,
        out_shape=[wide, low, wide, low],
        compiler_params=pltpu.CompilerParams(vmem_limit_bytes=VMEM_BYTES),
        cost_estimate=small_cost(
            flops=(number + 1) * 6 * rows * width * hidden,
            bytes_accessed=3 * 10**7,
            transcendentals=0,
        ),
        name="expert_sums",
    )(*near, *far, near_weights, far_weights)


def load_copies(sequence, half, sources, x_all, dy_all, semaphores):
    for n in range(4):
        target = x_all if n < 2 else dy_all
        yield pltpu.make_async_copy(
            sources[2 * sequence + n % 2].at[pl.ds((n // 2) * half, half), :],
            target.at[pl.ds((2 * sequence + n % 2) * half, half), :],
            semaphores.at[4 * sequence + n],
        )


def expert_weight_grads(sequences, terms, experts, hidden):
    width = sequences[0][0].shape[1]
    half = sequences[0][0].shape[0] // 2 // 128 * 128
    start, number = experts
    tokens = 2 * half
    counts = [pair[0].shape[0] // tokens for pair in terms]
    flat = [array for sequence in sequences for array in sequence]
    total = len(sequences)
    quarter = width // 4

    def kernel(*refs):
        sources, refs = refs[: len(flat)], refs[len(flat) :]
        term_refs, refs = refs[: 2 * len(counts)], refs[2 * len(counts) :]
        result_refs, (x_all, dy_all, semaphores) = refs[:-3], refs[-3:]
        e = pl.program_id(0)

        @pl.when(e == 0)
        def _():
            for s in range(total):
                for copy in load_copies(s, half, sources, x_all, dy_all, semaphores):
                    copy.start()

        gate_up = down = None
        first = 0
        for joined, count in enumerate(counts):

            @pl.when(e == 0)
            def _(first=first, count=count):
                for s in range(first, first + count):
                    for copy in load_copies(s, half, sources, x_all, dy_all, semaphores):
                        copy.wait()

            span = pl.ds(first * tokens, count * tokens)
            one = contract_rows(x_all[span, :], term_refs[2 * joined + 1][...])
            two = contract_rows(dy_all[span, :], term_refs[2 * joined][...])
            gate_up = one if gate_up is None else gate_up + one
            down = two if down is None else down + two
            first += count
        for n in range(number):

            @pl.when(e == n)
            def _(n=n):
                for q in range(4):
                    rows = slice(q * quarter, (q + 1) * quarter)
                    result_refs[4 * n + q][:, : 2 * hidden] = gate_up[rows].astype(jnp.bfloat16)
                    result_refs[4 * n + q][:, 2 * hidden :] = down[rows].astype(jnp.bfloat16)

    def beside(count, columns):
        return pl.BlockSpec((count * tokens, columns), lambda e: (0, e + start))

    return pl.pallas_call(
        kernel,
        grid=(number,),
        in_specs=[pl.BlockSpec(memory_space=pl.ANY)] * len(flat)
        + [beside(count, columns) for count in counts for columns in (hidden, 2 * hidden)],
        out_specs=[whole(quarter, 3 * hidden)] * (4 * number),
        scratch_shapes=[pltpu.VMEM((total * tokens, width), jnp.bfloat16)] * 2
        + [pltpu.SemaphoreType.DMA((4 * total,))],
        out_shape=[jax.ShapeDtypeStruct((quarter, 3 * hidden), jnp.bfloat16)] * (4 * number),
        compiler_params=pltpu.CompilerParams(vmem_limit_bytes=VMEM_BYTES),
        cost_estimate=small_cost(),
        name="expert_weight_grads",
    )(*flat, *(array for pair in terms for array in pair))


def own_weight_grads(sequences, terms, arrived, hidden):
    width = sequences[0][0].shape[1]
    half = sequences[0][0].shape[0] // 2 // 128 * 128
    tokens = 2 * half
    counts = [pair[0].shape[0] // tokens for pair in terms]
    flat = [array for sequence in sequences for array in sequence]
    total = len(sequences)
    quarter = width // 4

    def kernel(*refs):
        sources, refs = refs[: len(flat)], refs[len(flat) :]
        term_refs, refs = refs[: 2 * len(counts)], refs[2 * len(counts) :]
        arrived_refs, refs = refs[:6], refs[6:]
        gate_ref, up_ref, down_ref, x_all, dy_all, semaphores = refs
        for s in range(total):
            for copy in load_copies(s, half, sources, x_all, dy_all, semaphores):
                copy.start()
        gate_up = down = None
        first = 0
        for joined, count in enumerate(counts):
            for s in range(first, first + count):
                for copy in load_copies(s, half, sources, x_all, dy_all, semaphores):
                    copy.wait()
            span = pl.ds(first * tokens, count * tokens)
            one = contract_rows(x_all[span, :], term_refs[2 * joined + 1][...])
            two = contract_rows(term_refs[2 * joined][...], dy_all[span, :])
            gate_up = one if gate_up is None else gate_up + one
            down = two if down is None else down + two
            first += count
        for q in range(4):
            rows = slice(q * quarter, (q + 1) * quarter)
            inside = slice(q % 2 * quarter, (q % 2 + 1) * quarter)
            more = arrived_refs[q][...].astype(jnp.float32) + arrived_refs[4 + q // 2][
                inside, :
            ].astype(jnp.float32)
            both = gate_up[rows] + more[:, : 2 * hidden]
            gate_ref[0, rows, :] = both[:, :hidden]
            up_ref[0, rows, :] = both[:, hidden:]
            down_ref[0, :, rows] = down[:, rows] + more[:, 2 * hidden :].T

    def beside(count, columns):
        return pl.BlockSpec((count * tokens, columns), lambda e: (0, 0))

    tall = jax.ShapeDtypeStruct((1, width, hidden), jnp.float32)
    flat_down = jax.ShapeDtypeStruct((1, hidden, width), jnp.float32)
    return pl.pallas_call(
        kernel,
        grid=(1,),
        in_specs=[pl.BlockSpec(memory_space=pl.ANY)] * len(flat)
        + [beside(count, columns) for count in counts for columns in (hidden, 2 * hidden)]
        + [whole(quarter, 3 * hidden)] * 4
        + [whole(2 * quarter, 3 * hidden)] * 2,
        out_specs=[whole(*tall.shape), whole(*tall.shape), whole(*flat_down.shape)],
        scratch_shapes=[pltpu.VMEM((total * tokens, width), jnp.bfloat16)] * 2
        + [pltpu.SemaphoreType.DMA((4 * total,))],
        out_shape=[tall, tall, flat_down],
        compiler_params=pltpu.CompilerParams(vmem_limit_bytes=VMEM_BYTES),
        cost_estimate=small_cost(),
        name="own_weight_grads",
    )(*flat, *(array for pair in terms for array in pair), *arrived)


def planes_of_four(
    hidden_in,
    attn_gain,
    w_query,
    w_key,
    w_value,
    w_output,
    moe_gain,
    w_gate,
    w_up,
    w_down,
    gate_logits,
    routes,
    out_grad,
):
    tokens, width = hidden_in.shape
    half = tokens // 2
    experts = lax.axis_size("expert")
    columns = [[4 * z + r for z in range(4)] for r in range(4)]
    core = lax.axis_index("tensor")
    expert = lax.axis_index("expert")
    plane = expert // 4
    bit_x = expert % 2
    bit_y = (expert // 2) % 2
    hidden = w_down.shape[1]
    together = lax.optimization_barrier

    own_weights = jnp.concatenate([w_gate[0], w_up[0], w_down[0].T], axis=1)
    quarter = width // 4
    pieces = [own_weights[:quarter], own_weights[quarter : 2 * quarter], own_weights[2 * quarter :]]
    gate_weights = jax.nn.softmax(gate_logits, axis=-1)
    names = jnp.arange(experts, dtype=jnp.int32)
    dense = jnp.sum(
        jnp.where(routes.T[:, None, :] == names[None, :, None], gate_weights.T[:, None, :], 0.0),
        axis=0,
    )
    dense = lax.dynamic_slice_in_dim(dense, core * half, half, 1)
    coarse = dense.astype(jnp.bfloat16)
    fine = (dense - coarse.astype(jnp.float32)).astype(jnp.bfloat16)
    extra = jnp.pad(jnp.concatenate([coarse, fine], axis=1), ((0, 0), (0, width - 2 * half)))
    out_grad_half = part(out_grad, core, 2)
    dy_own = jnp.concatenate([out_grad_half, extra], axis=0)

    x0, y0 = flip(pieces[0], 1), flip(pieces[0], 2)
    dy_up_one, dy_down_one = climb(dy_own), descend(dy_own)
    cosine, sine = (jnp.asarray(table) for table in rotary_tables(tokens))
    normed, queries, keys, values, mixed, keep, send = attention_forward(
        core.reshape(1), hidden_in, attn_gain[None], w_query, w_key, w_value, w_output, cosine, sine
    )
    send, x0, y0, dy_up_one, dy_down_one, piece = together(
        (send, x0, y0, dy_up_one, dy_down_one, pieces[1])
    )
    x1, y1 = flip(piece, 1), flip(piece, 2)
    middle = keep + swap(send).astype(jnp.float32)
    scale_two = lax.rsqrt(jnp.mean(middle * middle, axis=-1, keepdims=True) + epsilon)
    unit_two = middle * scale_two
    rows_in = (unit_two * moe_gain).astype(jnp.bfloat16)
    up_one, down_one = climb(rows_in), descend(rows_in)
    x1, y1, up_one, down_one, dy_up_one, dy_down_one, piece = together(
        (x1, y1, up_one, down_one, dy_up_one, dy_down_one, pieces[2])
    )
    up_one = jnp.concatenate([up_one, dy_up_one], axis=0)
    down_one = jnp.concatenate([down_one, dy_down_one], axis=0)
    up_one, down_one, piece = together((up_one, down_one, piece))
    x2, y2 = flip(piece, 1), flip(piece, 2)
    up_two, down_two = climb(up_one), descend(down_one)
    own = jnp.concatenate([rows_in, dy_own], axis=0)
    first = jnp.where(plane == 0, down_one, up_one)
    own, first = (own, swap(own)), (first, swap(first))
    far_from_y = jnp.concatenate([y0, y1], axis=0)
    x2, y2, up_two, down_two, own, first, far_from_y = together(
        (x2, y2, up_two, down_two, own, first, far_from_y)
    )
    far_weights = [flip(far_from_y, 1), flip(x2, 2)]
    up_three, down_three = climb(up_two), descend(down_two)
    number = expert.reshape(1)
    near_early, near_weights = expert_terms(
        number, [own, first], [2], [[own_weights], [x0, x1, x2], [y0, y1, y2]], 0, True
    )
    second = jnp.where(plane == 0, down_two, jnp.where(plane == 3, up_two, down_one))
    second = (second, swap(second))
    far_weights, up_three, down_three, near_early, second = together(
        (far_weights, up_three, down_three, near_early, second)
    )
    third = jnp.where(
        plane == 0,
        down_three,
        jnp.where(plane == 1, down_two, jnp.where(plane == 2, up_two, up_three)),
    )
    third = (third, swap(third))
    sequences = [own, first, third, second]
    far_early, far_late, far_weights = expert_terms(
        number, sequences, [2, 2], [far_weights], 3, True
    )
    to_far = expert_weight_grads(sequences, [far_early, far_late], (0, 1), hidden)

    over_x, over_y = [flip(to_far[0], 1)], [flip(to_far[2], 2)]
    to_far, late = together((to_far, sequences[2:]))
    (near_late,) = expert_terms(number, late, [2], near_weights, 0, False)
    near_late, over_x, over_y, to_far = together((near_late, over_x, over_y, to_far))
    over_x, over_y = over_x + [flip(to_far[1], 1)], over_y + [flip(to_far[3], 2)]
    late_sums = expert_sums(near_late, far_late, near_weights, far_weights, half)
    late_sums, over_x, over_y, near_early, near_late = together(
        (late_sums, over_x, over_y, near_early, near_late)
    )
    back_late = add_low(late_sums[0], swap(late_sums[1]))
    second_back, third_back = back_late[1], back_late[0]

    falling, rising = descend(third_back), climb(third_back)
    third_back, near_early, near_late = together((third_back, near_early, near_late))
    beside = expert_weight_grads(sequences, [near_early, near_late], (1, 2), hidden)
    falling, rising, beside, near_early, far_early = together(
        (falling, rising, beside, near_early, far_early)
    )
    to_x, to_y = beside[:4], beside[4:]
    falling = add_low(jnp.where(plane == 3, second_back, third_back), falling)
    rising = add_low(jnp.where(plane == 0, second_back, third_back), rising)
    falling, rising, near_early, far_early = together((falling, rising, near_early, far_early))
    falling, rising = descend(falling), climb(rising)
    from_x, from_y = [flip(to_x[0], 1)], [flip(to_y[2], 2)]
    early_sums = expert_sums(near_early, far_early, near_weights, far_weights, half)
    falling, rising, early_sums, from_x, from_y, to_x, to_y = together(
        (falling, rising, early_sums, from_x, from_y, to_x, to_y)
    )
    back_early = add_low(early_sums[0], swap(early_sums[1]))
    own_back, first_back = back_early[0], back_early[1]
    falling = add_low(first_back, falling)
    rising = add_low(jnp.where(plane == 0, first_back, second_back), rising)
    falling, rising = descend(falling), climb(rising)
    from_x, from_y = from_x + [flip(to_x[1], 1)], from_y + [flip(to_y[3], 2)]
    with_x = jnp.concatenate([add_low(to_y[n], over_x[n]) for n in range(2)], axis=0)
    with_y = jnp.concatenate([add_low(to_x[2 + n], over_y[n]) for n in range(2)], axis=0)
    out_late = add_low(late_sums[2], swap(late_sums[3]))
    out_early = add_low(early_sums[2], swap(early_sums[3]))
    own_out, first_out, second_out, third_out = out_early[0], out_early[1], out_late[1], out_late[0]
    by_plane = [
        jnp.where(plane == 0, own_out, jnp.where(plane == 1, first_out, third_out)),
        jnp.where(plane == 1, own_out, jnp.where(plane == 3, second_out, first_out)),
        jnp.where(plane == 2, own_out, jnp.where(plane == 3, first_out, second_out)),
        jnp.where(plane == 3, own_out, jnp.where(plane == 2, second_out, third_out)),
    ]
    results = jnp.concatenate(by_plane, axis=0)
    falling, rising, results, from_x, from_y, with_x, with_y = together(
        (falling, rising, results, from_x, from_y, with_x, with_y)
    )
    moe_result = lax.psum_scatter(
        results, "expert", axis_index_groups=columns, scatter_dimension=0, tiled=True
    )
    grad_rows = (
        own_back.astype(jnp.float32) + falling.astype(jnp.float32) + rising.astype(jnp.float32)
    )
    grad_out = out_grad_half.astype(jnp.float32)
    grad_unit_two = grad_rows * moe_gain
    grad_moe_gain = jnp.sum(grad_rows * unit_two, axis=0)
    grad_middle = grad_out + scale_two * (
        grad_unit_two - unit_two * jnp.mean(grad_unit_two * unit_two, axis=-1, keepdims=True)
    )
    grad_attn_half = grad_middle.astype(jnp.bfloat16)
    grad_attn = ordered(grad_attn_half, swap(grad_attn_half), core)
    grad_mixed = contract_cols(grad_attn, w_output).astype(jnp.bfloat16)
    grad_output = contract_rows(mixed, grad_attn).astype(jnp.bfloat16)
    grad_mixed, grad_output = together((grad_mixed, grad_output))
    output_parts = plane_scatter_first(grad_output, bit_x, bit_y)
    grad_all_pre = attention_backward(grad_mixed, queries, keys, values, cosine, sine)
    grad_all_pre, output_parts = together((grad_all_pre, output_parts))
    grad_projections = contract_rows(normed, grad_all_pre).astype(jnp.bfloat16)
    output_parts = plane_scatter_second(output_parts, bit_x, bit_y)
    projection_parts = plane_scatter_first(grad_projections, bit_x, bit_y)
    w_all = jnp.concatenate([w_query, w_key, w_value], axis=1)
    grad_normed_part = contract_cols(grad_all_pre, w_all).astype(jnp.bfloat16)
    grad_normed = part(grad_normed_part, core, 2).astype(jnp.float32) + swap(
        part(grad_normed_part, 1 - core, 2)
    ).astype(jnp.float32)
    source_half = part(hidden_in, core, 2).astype(jnp.float32)
    scale_half = lax.rsqrt(jnp.mean(source_half * source_half, axis=-1, keepdims=True) + epsilon)
    unit_half = source_half * scale_half
    grad_unit_one = grad_normed * attn_gain
    grad_attn_gain = jnp.sum(grad_normed * unit_half, axis=0)
    grad_in_half = grad_middle + scale_half * (
        grad_unit_one - unit_half * jnp.mean(grad_unit_one * unit_half, axis=-1, keepdims=True)
    )
    gains = jnp.stack([grad_attn_gain, grad_moe_gain])
    projection_parts, output_parts, gains, grad_in_half = together(
        (projection_parts, output_parts, gains, grad_in_half)
    )
    projection_parts = plane_scatter_second(projection_parts, bit_x, bit_y)
    gains = (gains + swap(gains)).reshape(-1, grad_projections.shape[1])
    gain_rows = gains.shape[0]
    gains = jnp.pad(gains, ((0, 16 - gain_rows), (0, 0))).astype(jnp.bfloat16)
    grad_in = ordered(grad_in_half, swap(grad_in_half), core)
    output_both = jnp.concatenate(output_parts, axis=0)
    projection_both = jnp.concatenate([*projection_parts, gains], axis=0)
    projection_both, output_both, grad_in, moe_result, with_x, with_y = together(
        (projection_both, output_both, grad_in, moe_result, with_x, with_y)
    )
    output_both, projection_both = lax.psum(
        (output_both, projection_both), "expert", axis_index_groups=columns
    )
    block_half = (middle + moe_result.astype(jnp.float32)).astype(jnp.bfloat16)
    block_out = ordered(block_half, swap(block_half), core)
    then_y, then_x = flip(with_x, 2), flip(with_y, 1)
    arrived = (*from_x, *from_y, then_y, then_x)
    expert_grads = own_weight_grads(sequences, [near_early, near_late], arrived, hidden)
    output_both, projection_both, expert_grads, block_out = together(
        (output_both, projection_both, expert_grads, block_out)
    )
    output_sum = plane_gather(*jnp.split(output_both, 2), bit_x, bit_y)
    gains = projection_both[-16:].astype(jnp.float32)
    gains = gains + flip(gains, 1)
    gains = gains + flip(gains, 2)
    gains_sum = gains[:gain_rows].reshape(2, width)
    projection_both = projection_both[:-16]
    grad_gate, grad_up, grad_down = expert_grads
    projections = plane_gather(*jnp.split(projection_both, 2), bit_x, bit_y).astype(jnp.float32)
    query_width = w_query.shape[1]
    key_width = w_key.shape[1]
    return (
        block_out,
        grad_in,
        gains_sum[0],
        projections[:, :query_width],
        projections[:, query_width : query_width + key_width],
        projections[:, query_width + key_width :],
        output_sum.astype(jnp.float32),
        gains_sum[1],
        grad_gate,
        grad_up,
        grad_down,
    )


def solution(mesh):
    on_device = planes_of_four if mesh.shape["expert"] == 16 else routed_slots
    return jax.shard_map(
        on_device,
        mesh=mesh,
        in_specs=(
            P("expert", None),
            P(),
            P(None, "tensor"),
            P(None, "tensor"),
            P(None, "tensor"),
            P("tensor", None),
            P(),
            P("expert", None, "tensor"),
            P("expert", None, "tensor"),
            P("expert", "tensor", None),
            P("expert", None),
            P("expert", None),
            P("expert", None),
        ),
        out_specs=(
            P("expert", None),
            P("expert", None),
            P(),
            P(None, "tensor"),
            P(None, "tensor"),
            P(None, "tensor"),
            P("tensor", None),
            P(),
            P("expert", None, "tensor"),
            P("expert", None, "tensor"),
            P("expert", "tensor", None),
        ),
        check_vma=False,
    )
```

```python
import math

import jax
import jax.numpy as jnp
import numpy as np
from jax import lax
from jax.experimental import pallas as pl
from jax.experimental.pallas import tpu as pltpu
from jax.sharding import PartitionSpec as P

HD = 128


epsilon = 1e-06
rope_base = 10000.0
masked_score = -1e30


def rotate(values, places, sign):
    halfway = values.shape[-1] // 2
    frequency = rope_base ** (-jnp.arange(halfway, dtype=jnp.float32) / halfway)
    angles = places.astype(jnp.float32)[:, None] * frequency[None, :]
    cosine = jnp.cos(angles)[:, None, :]
    sine = sign * jnp.sin(angles)[:, None, :]
    first = values[..., :halfway]
    second = values[..., halfway:]
    return jnp.concatenate(
        [first * cosine - second * sine, second * cosine + first * sine], axis=-1
    )


def contract_rows(left, right):
    return lax.dot_general(
        left, right, (((0,), (0,)), ((), ())), preferred_element_type=jnp.float32
    )


def contract_cols(left, right):
    return lax.dot_general(
        left, right, (((1,), (1,)), ((), ())), preferred_element_type=jnp.float32
    )


def block_scores(query_block, keys_used, row_start, scale_factor):
    query_rows = query_block.shape[0]
    key_rows = keys_used.shape[0]
    raw_scores = (
        jnp.einsum("qcgd,kcd->cgqk", query_block, keys_used, preferred_element_type=jnp.float32)
        * scale_factor
    )
    row_ids = row_start + jnp.arange(query_rows)
    causal = jnp.arange(key_rows)[None, :] <= row_ids[:, None]
    return jnp.where(causal, raw_scores, masked_score)


def routed_slots(
    hidden_in,
    attn_gain,
    w_query,
    w_key,
    w_value,
    w_output,
    moe_gain,
    w_gate,
    w_up,
    w_down,
    gate_logits,
    routes,
    out_grad,
):
    tokens, model_width = hidden_in.shape
    experts = lax.axis_size("expert")
    tensor_ranks = lax.axis_size("tensor")
    tensor_rank = lax.axis_index("tensor")
    route_width = routes.shape[1]
    route_count = tokens * route_width
    capacity = 2 * route_count // experts
    half_slots = capacity // tensor_ranks
    heads_local = w_query.shape[1] // HD
    kv_local = w_key.shape[1] // HD
    groups = heads_local // kv_local
    scale_factor = 1.0 / math.sqrt(HD)
    block_rows = min(512, tokens)
    places = jnp.arange(tokens, dtype=jnp.int32)
    flat_routes = routes.reshape(-1)
    route_hits = (flat_routes[:, None] == jnp.arange(experts, dtype=jnp.int32)[None, :]).astype(
        jnp.int32
    )
    slot_index = jnp.sum(jnp.cumsum(route_hits, axis=0) * route_hits, axis=1) - 1
    which_route = (
        jnp.full((experts * capacity,), route_count, jnp.int32)
        .at[flat_routes * capacity + slot_index]
        .set(jnp.arange(route_count, dtype=jnp.int32))
    )
    which_token = which_route // route_width
    own_half = slot_index // half_slots == tensor_rank
    back_index = jnp.where(
        own_half, flat_routes * half_slots + slot_index % half_slots, experts * half_slots
    )
    gate_weights = jax.nn.softmax(gate_logits, axis=-1)
    full_gate, full_up, full_down = (w_gate[0], w_up[0], w_down[0])

    def deliver(buffer):
        arrived_all = lax.all_to_all(buffer, "expert", split_axis=0, concat_axis=0, tiled=True)
        return arrived_all.reshape(experts * capacity, model_width)

    def give_back(partial_value):
        summed_rows = lax.psum_scatter(
            partial_value.reshape(experts, capacity, model_width).astype(jnp.bfloat16),
            "tensor",
            scatter_dimension=1,
            tiled=True,
        )
        returned = lax.all_to_all(summed_rows, "expert", split_axis=0, concat_axis=0, tiled=True)
        return jnp.concatenate(
            [
                returned.reshape(experts * half_slots, model_width),
                jnp.zeros((1, model_width), jnp.bfloat16),
            ],
            axis=0,
        )

    def collect(returned, weights):
        picked = returned[back_index].astype(jnp.float32).reshape(tokens, route_width, model_width)
        return lax.psum(
            jnp.sum(picked * weights[:, :, None], axis=1).astype(jnp.bfloat16), "tensor"
        ).astype(jnp.float32)

    source = hidden_in.astype(jnp.float32)
    scale_one = lax.rsqrt(jnp.mean(source * source, axis=-1, keepdims=True) + epsilon)
    unit_one = source * scale_one
    normed = (unit_one * attn_gain).astype(jnp.bfloat16)
    query_pre = jnp.dot(normed, w_query, preferred_element_type=jnp.float32).reshape(
        tokens, heads_local, HD
    )
    queries = (
        rotate(query_pre, places, 1.0).astype(jnp.bfloat16).reshape(tokens, kv_local, groups, HD)
    )
    key_pre = jnp.dot(normed, w_key, preferred_element_type=jnp.float32).reshape(
        tokens, kv_local, HD
    )
    keys_used = rotate(key_pre, places, 1.0).astype(jnp.bfloat16)
    values_used = (
        jnp.dot(normed, w_value, preferred_element_type=jnp.float32)
        .astype(jnp.bfloat16)
        .reshape(tokens, kv_local, HD)
    )
    row_start = 0
    query_block = queries
    raw_scores = block_scores(query_block, keys_used, row_start, scale_factor)
    biggest = jnp.max(raw_scores, axis=-1, keepdims=True)
    exponent = jnp.exp(raw_scores - biggest)
    row_total = jnp.sum(exponent, axis=-1, keepdims=True)
    weights_low = (exponent / row_total).astype(jnp.bfloat16)
    logsums = [biggest + jnp.log(row_total)]
    attended = jnp.einsum(
        "cgqk,kcd->qcgd", weights_low, values_used, preferred_element_type=jnp.float32
    )
    mixed_blocks = attended.reshape(block_rows, heads_local * HD).astype(jnp.bfloat16)
    attn_part = jnp.dot(mixed_blocks, w_output, preferred_element_type=jnp.float32)
    middle = source + lax.psum(attn_part.astype(jnp.bfloat16), "tensor").astype(jnp.float32)
    scale_two = lax.rsqrt(jnp.mean(middle * middle, axis=-1, keepdims=True) + epsilon)
    unit_two = middle * scale_two
    rows_in = (unit_two * moe_gain).astype(jnp.bfloat16)
    padded_rows = jnp.concatenate([rows_in, jnp.zeros((1, model_width), jnp.bfloat16)], axis=0)
    arrived = deliver(padded_rows[which_token].reshape(experts, capacity, model_width))
    gate_pre = jnp.dot(arrived, full_gate, preferred_element_type=jnp.float32)
    up_pre = jnp.dot(arrived, full_up, preferred_element_type=jnp.float32)
    sigmoid = jax.nn.sigmoid(gate_pre)
    activated = gate_pre * sigmoid
    hidden_units = (activated * up_pre).astype(jnp.bfloat16)
    produced = jnp.dot(hidden_units, full_down, preferred_element_type=jnp.float32)
    moe_result = collect(give_back(produced), gate_weights)
    block_out = (middle + moe_result).astype(jnp.bfloat16)
    grad_out = out_grad.astype(jnp.float32)
    route_grads = (
        (gate_weights[:, :, None] * grad_out[:, None, :])
        .astype(jnp.bfloat16)
        .reshape(route_count, model_width)
    )
    padded_grads = jnp.concatenate([route_grads, jnp.zeros((1, model_width), jnp.bfloat16)], axis=0)
    grad_arrived = deliver(padded_grads[which_route].reshape(experts, capacity, model_width))
    grad_down = contract_rows(hidden_units, grad_arrived)
    grad_inner = contract_cols(grad_arrived, full_down)
    grad_gate_pre = (grad_inner * up_pre * sigmoid * (1.0 + gate_pre * (1.0 - sigmoid))).astype(
        jnp.bfloat16
    )
    grad_up_pre = (grad_inner * activated).astype(jnp.bfloat16)
    grad_gate = contract_rows(arrived, grad_gate_pre)
    grad_up = contract_rows(arrived, grad_up_pre)
    grad_arrived_rows = contract_cols(grad_gate_pre, full_gate) + contract_cols(
        grad_up_pre, full_up
    )
    grad_rows = collect(give_back(grad_arrived_rows), jnp.ones_like(gate_weights))
    grad_unit_two = grad_rows * moe_gain
    grad_moe_gain = jnp.sum(grad_rows * unit_two, axis=0)
    grad_middle = grad_out + scale_two * (
        grad_unit_two - unit_two * jnp.mean(grad_unit_two * unit_two, axis=-1, keepdims=True)
    )
    grad_attn = grad_middle.astype(jnp.bfloat16)
    grad_output = contract_rows(mixed_blocks, grad_attn)
    grad_mixed = (
        contract_cols(grad_attn, w_output)
        .astype(jnp.bfloat16)
        .reshape(tokens, kv_local, groups, HD)
    )
    grad_query_blocks = []
    grad_keys = jnp.zeros((tokens, kv_local, HD), jnp.float32)
    grad_values = jnp.zeros((tokens, kv_local, HD), jnp.float32)
    for block_number, row_start in enumerate(range(0, tokens, block_rows)):
        query_block = queries
        raw_scores = block_scores(query_block, keys_used, row_start, scale_factor)
        probs = jnp.exp(raw_scores - logsums[block_number])
        probs_low = probs.astype(jnp.bfloat16)
        grad_probs = jnp.einsum(
            "qcgd,kcd->cgqk", grad_mixed, values_used, preferred_element_type=jnp.float32
        )
        delta = jnp.sum(probs * grad_probs, axis=-1, keepdims=True)
        grad_scores = (probs * (grad_probs - delta)).astype(jnp.bfloat16)
        grad_query_blocks.append(
            jnp.einsum("cgqk,kcd->qcgd", grad_scores, keys_used, preferred_element_type=jnp.float32)
            * scale_factor
        )
        grad_keys = (
            jnp.einsum(
                "cgqk,qcgd->kcd", grad_scores, query_block, preferred_element_type=jnp.float32
            )
            * scale_factor
        )
        grad_values = jnp.einsum(
            "cgqk,qcgd->kcd", probs_low, grad_mixed, preferred_element_type=jnp.float32
        )
    grad_queries = grad_query_blocks[0].reshape(tokens, heads_local, HD)
    grad_query_pre = (
        rotate(grad_queries, places, -1.0).astype(jnp.bfloat16).reshape(tokens, heads_local * HD)
    )
    grad_key_pre = (
        rotate(grad_keys, places, -1.0).astype(jnp.bfloat16).reshape(tokens, kv_local * HD)
    )
    grad_value_pre = grad_values.astype(jnp.bfloat16).reshape(tokens, kv_local * HD)
    grad_query = contract_rows(normed, grad_query_pre)
    grad_key = contract_rows(normed, grad_key_pre)
    grad_value = contract_rows(normed, grad_value_pre)
    grad_normed_part = (
        contract_cols(grad_query_pre, w_query)
        + contract_cols(grad_key_pre, w_key)
        + contract_cols(grad_value_pre, w_value)
    )
    grad_normed = lax.psum(grad_normed_part.astype(jnp.bfloat16), "tensor").astype(jnp.float32)
    grad_unit_one = grad_normed * attn_gain
    grad_attn_gain = jnp.sum(grad_normed * unit_one, axis=0)
    grad_in = grad_middle + scale_one * (
        grad_unit_one - unit_one * jnp.mean(grad_unit_one * unit_one, axis=-1, keepdims=True)
    )
    summed = lax.psum(
        (grad_query, grad_key, grad_value, grad_output, grad_attn_gain, grad_moe_gain), "expert"
    )
    return (
        block_out,
        grad_in,
        summed[4],
        summed[0],
        summed[1],
        summed[2],
        summed[3],
        summed[5],
        grad_gate[None],
        grad_up[None],
        grad_down[None],
    )


VMEM_BYTES = 60 * 2**20


def small_cost(**_):
    return pl.CostEstimate(flops=1000, bytes_accessed=1000, transcendentals=0)


def dot(left, right):
    return jnp.dot(left, right, preferred_element_type=jnp.float32)


def whole(*shape):
    return pl.BlockSpec(shape, lambda *_: (0,) * len(shape), pipeline_mode=pl.Buffered(1))


def swap(value):
    return lax.ppermute(value, "tensor", [(0, 1), (1, 0)])


def flip(value, bit):
    places = lax.axis_size("expert")
    return lax.ppermute(value, "expert", [(i, i ^ bit) for i in range(places)])


def climb(value):
    places = lax.axis_size("expert")
    return lax.ppermute(value, "expert", [(i, i + 4) for i in range(places - 4)])


def descend(value):
    places = lax.axis_size("expert")
    return lax.ppermute(value, "expert", [(i + 4, i) for i in range(places - 4)])


def part(value, index, count):
    size = value.shape[0] // count
    return lax.dynamic_slice_in_dim(value, index * size, size, 0)


def ordered(own, other, place):
    return jnp.where(
        place == 0,
        jnp.concatenate([own, other], axis=0),
        jnp.concatenate([other, own], axis=0),
    )


def add_low(kept, arrived):
    return (kept.astype(jnp.float32) + arrived.astype(jnp.float32)).astype(jnp.bfloat16)


def plane_scatter_first(value, bit_x, bit_y):
    left, right = jnp.split(value, 2, axis=0)
    left = add_low(part(left, bit_x, 2), flip(part(left, 1 - bit_x, 2), 1))
    right = add_low(part(right, bit_y, 2), flip(part(right, 1 - bit_y, 2), 2))
    return left, right


def plane_scatter_second(halves, bit_x, bit_y):
    left, right = halves
    left = add_low(part(left, bit_y, 2), flip(part(left, 1 - bit_y, 2), 2))
    right = add_low(part(right, bit_x, 2), flip(part(right, 1 - bit_x, 2), 1))
    return left, right


def plane_gather_first(left, right, bit_x, bit_y):
    return ordered(left, flip(left, 2), bit_y), ordered(right, flip(right, 1), bit_x)


def plane_gather_second(halves, bit_x, bit_y):
    left, right = halves
    return left, flip(left, 1), right, flip(right, 2)


def lay_out(bits, pieces, widths):
    rows, columns = pieces[0].shape
    def kernel(bits_ref, *refs):
        sources, results = refs[:4], refs[4:]
        for side in range(2):
            bit = bits_ref[side]
            for n in range(2):
                value = sources[2 * side + n][...].astype(jnp.float32)
                place = pl.multiple_of((2 * side + jnp.where(bit == n, 0, 1)) * rows, rows)
                start = 0
                for result, size in zip(results, widths, strict=True):
                    result[pl.ds(place, rows), :] = value[:, start : start + size]
                    start += size

    return pl.pallas_call(
        kernel,
        in_specs=[pl.BlockSpec(memory_space=pltpu.SMEM)]
        + [pl.BlockSpec(memory_space=pltpu.VMEM)] * 4,
        out_specs=[pl.BlockSpec(memory_space=pltpu.VMEM)] * len(widths),
        out_shape=[jax.ShapeDtypeStruct((4 * rows, size), jnp.float32) for size in widths],
        compiler_params=pltpu.CompilerParams(vmem_limit_bytes=VMEM_BYTES),
        cost_estimate=small_cost(),
        name="lay_out",
    )(bits, *pieces)


def rotary_tables(tokens):
    halfway = HD // 2
    frequency = rope_base ** (-np.arange(halfway, dtype=np.float64) / halfway)
    angles = np.arange(tokens)[:, None] * frequency[None, :]
    cosine, sine = np.cos(angles), np.sin(angles)
    return (
        np.concatenate([cosine, cosine], axis=1).astype(np.float32),
        np.concatenate([-sine, sine], axis=1).astype(np.float32),
    )


def causal_scores(query_block, keys, row_start, scale_factor):
    raw = contract_cols(query_block, keys) * scale_factor
    row_ids = row_start + lax.broadcasted_iota(jnp.int32, raw.shape, 0)
    return jnp.where(lax.broadcasted_iota(jnp.int32, raw.shape, 1) <= row_ids, raw, masked_score)


def softmax_rows(raw):
    exponent = jnp.exp(raw - jnp.max(raw, axis=-1, keepdims=True))
    return exponent / jnp.sum(exponent, axis=-1, keepdims=True)


def attention_forward(core, hidden, gain, w_query, w_key, w_value, w_output, cosine, sine):
    tokens, width = hidden.shape
    half = tokens // 2
    local = w_query.shape[1]
    heads = local // HD
    scale_factor = 1.0 / math.sqrt(HD)

    def kernel(
        core_ref, hidden_ref, gain_ref, wq_ref, wk_ref, wv_ref, wo_ref, cos_ref, sin_ref,
        normed_ref, query_ref, key_ref, value_ref, mixed_ref, keep_ref, send_ref, part_ref,
    ):
        for block in range(2):
            rows = pl.ds(block * half, half)
            source = hidden_ref[rows, :].astype(jnp.float32)
            scale = lax.rsqrt(jnp.mean(source * source, axis=-1, keepdims=True) + epsilon)
            normed = (source * scale * gain_ref[...]).astype(jnp.bfloat16)
            normed_ref[rows, :] = normed
            cos, sin = cos_ref[rows, :], sin_ref[rows, :]

            def turned(value):
                return (value * cos + pltpu.roll(value, HD // 2, 1) * sin).astype(jnp.bfloat16)

            query_pre = dot(normed, wq_ref[...])
            for head in range(heads):
                lanes = slice(head * HD, (head + 1) * HD)
                query_ref[rows, lanes] = turned(query_pre[:, lanes])
            key_ref[rows, :] = turned(dot(normed, wk_ref[...]))
            value_ref[rows, :] = dot(normed, wv_ref[...]).astype(jnp.bfloat16)
        for block in range(2):
            rows = pl.ds(block * half, half)
            seen = pl.ds(0, (block + 1) * half)
            keys, values = key_ref[seen, :], value_ref[seen, :]
            for head in range(heads):
                lanes = slice(head * HD, (head + 1) * HD)
                raw = causal_scores(query_ref[rows, lanes], keys, block * half, scale_factor)
                probs_low = softmax_rows(raw).astype(jnp.bfloat16)
                mixed_ref[rows, lanes] = dot(probs_low, values).astype(jnp.bfloat16)
            part_ref[rows, :] = dot(mixed_ref[rows, :], wo_ref[...])
        own = pl.ds(pl.multiple_of(core_ref[0] * half, half), half)
        other = pl.ds(pl.multiple_of((1 - core_ref[0]) * half, half), half)
        keep_ref[...] = hidden_ref[own, :].astype(jnp.float32) + part_ref[own, :]
        send_ref[...] = part_ref[other, :].astype(jnp.bfloat16)

    def low(rows, columns):
        return jax.ShapeDtypeStruct((rows, columns), jnp.bfloat16)

    shapes = [
        low(tokens, width), low(tokens, local), low(tokens, HD), low(tokens, HD),
        low(tokens, local), jax.ShapeDtypeStruct((half, width), jnp.float32), low(half, width),
    ]
    operands = [hidden, gain, w_query, w_key, w_value, w_output, cosine, sine]
    return pl.pallas_call(
        kernel,
        out_shape=shapes,
        in_specs=[pl.BlockSpec(memory_space=pltpu.SMEM)]
        + [pl.BlockSpec(memory_space=pltpu.VMEM) for _ in operands],
        out_specs=[pl.BlockSpec(memory_space=pltpu.VMEM) for _ in shapes],
        scratch_shapes=[pltpu.VMEM((tokens, width), jnp.float32)],
        compiler_params=pltpu.CompilerParams(vmem_limit_bytes=VMEM_BYTES),
        cost_estimate=small_cost(
            flops=40 * 10**9, bytes_accessed=16 * 10**6, transcendentals=2 * 10**6
        ),
        name="attention_forward",
    )(core, *operands)


def attention_backward(grad_attn, w_output, queries, keys, values, cosine, sine):
    tokens, local = queries.shape
    half = tokens // 2
    heads = local // HD
    scale_factor = 1.0 / math.sqrt(HD)

    def kernel(
        ga_ref, wo_ref, query_ref, key_ref, value_ref, cos_ref, sin_ref, grad_ref, gk_ref, gv_ref, gm_ref
    ):
        gm_ref[...] = contract_cols(ga_ref[...], wo_ref[...]).astype(jnp.bfloat16)
        for block in range(2):
            rows = pl.ds(block * half, half)
            seen = pl.ds(0, (block + 1) * half)
            keys, values = key_ref[seen, :], value_ref[seen, :]
            cos, sin = cos_ref[rows, :], sin_ref[rows, :]
            grad_keys = jnp.zeros(((block + 1) * half, HD), jnp.float32)
            grad_values = grad_keys
            for head in range(heads):
                lanes = slice(head * HD, (head + 1) * HD)
                query, grad = query_ref[rows, lanes], gm_ref[rows, lanes]
                probs = softmax_rows(causal_scores(query, keys, block * half, scale_factor))
                grad_probs = contract_cols(grad, values)
                delta = jnp.sum(probs * grad_probs, axis=-1, keepdims=True)
                grad_scores = (probs * (grad_probs - delta)).astype(jnp.bfloat16)
                turned = dot(grad_scores, keys) * scale_factor
                grad_ref[rows, lanes] = (
                    turned * cos - pltpu.roll(turned, HD // 2, 1) * sin
                ).astype(jnp.bfloat16)
                grad_keys = grad_keys + contract_rows(grad_scores, query)
                grad_values = grad_values + contract_rows(probs.astype(jnp.bfloat16), grad)
            if block == 0:
                gk_ref[pl.ds(0, half), :] = grad_keys
                gv_ref[pl.ds(0, half), :] = grad_values
            else:
                first = pl.ds(0, half)
                gk_ref[first, :] = gk_ref[first, :] + grad_keys[:half]
                gv_ref[first, :] = gv_ref[first, :] + grad_values[:half]
                gk_ref[rows, :] = grad_keys[half:]
                gv_ref[rows, :] = grad_values[half:]
        turned = gk_ref[...] * scale_factor
        grad_ref[:, local : local + HD] = (
            turned * cos_ref[...] - pltpu.roll(turned, HD // 2, 1) * sin_ref[...]
        ).astype(jnp.bfloat16)
        grad_ref[:, local + HD :] = gv_ref[...].astype(jnp.bfloat16)

    return pl.pallas_call(
        kernel,
        out_shape=jax.ShapeDtypeStruct((tokens, local + 2 * HD), jnp.bfloat16),
        in_specs=[pl.BlockSpec(memory_space=pltpu.VMEM)] * 7,
        out_specs=pl.BlockSpec(memory_space=pltpu.VMEM),
        scratch_shapes=[pltpu.VMEM((tokens, HD), jnp.float32)] * 2
        + [pltpu.VMEM((tokens, local), jnp.bfloat16)],
        compiler_params=pltpu.CompilerParams(vmem_limit_bytes=VMEM_BYTES),
        cost_estimate=small_cost(
            flops=10 * 10**9, bytes_accessed=4 * 10**6, transcendentals=2 * 10**6
        ),
        name="attention_backward",
    )(grad_attn, w_output, queries, keys, values, cosine, sine)


def expert_weights_of(expert_ref, packs, half):
    start = 2 * half
    count = packs[0].shape[0] - start
    row_ids = lax.broadcasted_iota(jnp.int32, (count, 128), 0)
    lane_ids = lax.broadcasted_iota(jnp.int32, (count, 128), 1)
    pick = (row_ids == (expert_ref[0] ^ lane_ids)).astype(jnp.bfloat16)
    sides = []
    for ref in packs:
        coarse, fine = ref[start:, :half], ref[start:, half : 2 * half]
        sides.append(contract_rows(coarse, pick) + contract_rows(fine, pick))
    return jnp.concatenate(sides, axis=0)


def expert_terms(expert, joins, pieces, first, keep):
    sequences = [sequence for own, _ in joins for sequence in own]
    width = sequences[0][0].shape[1]
    half = sequences[0][0].shape[0] // 2 // 128 * 128
    number = len(pieces)
    arrays = [array for own in pieces for array, _ in own]
    columns = arrays[0].shape[-1]
    hidden = columns // 3
    tokens = 2 * half
    total = len(sequences)
    flat = [array for sequence in sequences for array in sequence]

    loads = []
    n = 0
    for own in pieces:
        loads.append([])
        place = 0
        for array, index in own:
            loads[-1].append((n, index, place, array.shape[-2]))
            place += array.shape[-2]
            n += 1
    copy_count = n

    def kernel(expert_ref, *refs):
        sources, refs = refs[: len(flat)], refs[len(flat) :]
        piece_refs, refs = refs[: len(arrays)], refs[len(arrays) :]
        results, (w_ref, packs, gate_all, semaphores) = refs[:-4], refs[-4:]
        e = pl.program_id(0)

        def copies_of(one):
            for which, index, place, rows in loads[one]:
                source = piece_refs[which] if index is None else piece_refs[which].at[index]
                yield pltpu.make_async_copy(
                    source, w_ref.at[one, pl.ds(place, rows), :], semaphores.at[which]
                )

        def kept(one):
            return pltpu.make_async_copy(
                w_ref.at[one], results[-1].at[one], semaphores.at[copy_count + one]
            )

        def pack_copy(n):
            return pltpu.make_async_copy(
                sources[n], packs.at[n], semaphores.at[copy_count + number + n]
            )

        @pl.when(e == 0)
        def _():
            for copy in copies_of(0):
                copy.start()
            for n in range(2 * total):
                pack_copy(n).start()
            for one in range(1, number):
                for copy in copies_of(one):
                    copy.start()

        for one in range(number):

            @pl.when(e == one)
            def _(one=one):
                for copy in copies_of(one):
                    copy.wait()
                if keep:
                    kept(one).start()

        lanes = lax.broadcasted_iota(jnp.int32, (half, 128), 1)
        n = 0
        for join, (own, start) in enumerate(joins):
            inner_ref, grad_ref = results[2 * join : 2 * join + 2]
            for s in range(len(own)):

                @pl.when(e == 0)
                def _(n=n):
                    for side in range(2):
                        pack_copy(2 * n + side).wait()
                    gate_all[n * tokens : (n + 1) * tokens, :] = expert_weights_of(
                        expert_ref, [packs.at[2 * n], packs.at[2 * n + 1]], half
                    )

                def run(n=n, s=s, inner_ref=inner_ref, grad_ref=grad_ref):
                    for side in range(2):
                        pack = packs.at[2 * n + side]
                        here = pl.ds(s * tokens + side * half, half)
                        gate = gate_all[n * tokens + side * half : n * tokens + (side + 1) * half, :]
                        weight = jnp.sum(
                            jnp.where(lanes == e + first, gate, 0.0), axis=1, keepdims=True
                        )
                        both = dot(pack[:half, :], w_ref[e, :, : 2 * hidden])
                        grad_inner = dot(pack[half : 2 * half, :], w_ref[e, :, 2 * hidden :]) * weight
                        gate_pre, up_pre = both[:, :hidden], both[:, hidden:]
                        sigmoid = jax.nn.sigmoid(gate_pre)
                        activated = gate_pre * sigmoid
                        grad_gate = (
                            grad_inner * up_pre * sigmoid * (1.0 + gate_pre * (1.0 - sigmoid))
                        )
                        grad_ref[here, :hidden] = grad_gate.astype(jnp.bfloat16)
                        grad_ref[here, hidden:] = (grad_inner * activated).astype(jnp.bfloat16)
                        inner_ref[here, :] = (activated * up_pre * weight).astype(jnp.bfloat16)

                if start:
                    pl.when(e >= start)(run)
                else:
                    run()
                n += 1

        if keep:

            @pl.when(e == number - 1)
            def _():
                for one in range(number):
                    kept(one).wait()

    out_specs, out_shape = [], []
    for own, start in joins:
        for size in (hidden, 2 * hidden):
            out_specs.append(
                pl.BlockSpec(
                    (len(own) * tokens, size), lambda e, start=start: (0, jnp.maximum(e - start, 0))
                )
            )
            out_shape.append(
                jax.ShapeDtypeStruct((len(own) * tokens, (number - start) * size), jnp.bfloat16)
            )
    if keep:
        out_specs.append(pl.BlockSpec(memory_space=pl.ANY))
        out_shape.append(jax.ShapeDtypeStruct((number, width, columns), jnp.bfloat16))
    results = pl.pallas_call(
        kernel,
        grid=(number,),
        in_specs=[pl.BlockSpec(memory_space=pltpu.SMEM)]
        + [pl.BlockSpec(memory_space=pl.ANY)] * (len(flat) + len(arrays)),
        out_specs=out_specs,
        out_shape=out_shape,
        scratch_shapes=[
            pltpu.VMEM((number, width, columns), jnp.bfloat16),
            pltpu.VMEM((2 * total, *flat[0].shape), jnp.bfloat16),
            pltpu.VMEM((total * tokens, 128), jnp.float32),
            pltpu.SemaphoreType.DMA((copy_count + number + 2 * total,)),
        ],
        compiler_params=pltpu.CompilerParams(vmem_limit_bytes=VMEM_BYTES),
        cost_estimate=small_cost(),
        name="expert_terms",
    )(expert, *flat, *arrays)
    terms = [tuple(results[2 * n : 2 * n + 2]) for n in range(len(joins))]
    return (*terms, results[-1]) if keep else tuple(terms)


def expert_sums(groups, weights, half):
    number, width = weights.shape[:2]
    hidden = weights.shape[2] // 3
    counts = [group[0][0].shape[0] // (2 * half) for group in groups]
    total = sum(counts)
    flat = [array for group in groups for part in group for array in part[:2]]
    block = 256

    def kernel(*refs):
        terms, refs = refs[: len(flat)], refs[len(flat) :]
        w_ref, back_own, back_other, out_own, out_other = refs
        n = place = 0
        for group, count in zip(groups, counts, strict=True):
            back = out = None
            for inner, _, start in group:
                for e in range(inner.shape[1] // hidden):
                    grad = terms[n + 1][:, 2 * e * hidden : 2 * (e + 1) * hidden]
                    one = contract_cols(grad, w_ref[start + e, :, : 2 * hidden])
                    back = one if back is None else back + one
                n += 2
            n -= 2 * len(group)
            for inner, _, start in group:
                for e in range(inner.shape[1] // hidden):
                    one = contract_cols(
                        terms[n][:, e * hidden : (e + 1) * hidden], w_ref[start + e, :, 2 * hidden :]
                    )
                    out = one if out is None else out + one
                n += 2
            for s in range(count):
                start = 2 * s * half
                back_own[place + s] = back[start : start + half].astype(jnp.bfloat16)
                back_other[place + s] = back[start + half : start + 2 * half].astype(jnp.bfloat16)
                out_own[place + s] = out[start : start + half].astype(jnp.bfloat16)
                out_other[place + s] = out[start + half : start + 2 * half].astype(jnp.bfloat16)
            place += count

    low = jax.ShapeDtypeStruct((total, half, width), jnp.bfloat16)
    return pl.pallas_call(
        kernel,
        grid=(width // block,),
        in_specs=[whole(*a.shape) for a in flat]
        + [pl.BlockSpec((number, block, 3 * hidden), lambda n: (0, n, 0))],
        out_specs=[pl.BlockSpec((total, half, block), lambda n: (0, 0, n))] * 4,
        out_shape=[low] * 4,
        compiler_params=pltpu.CompilerParams(vmem_limit_bytes=VMEM_BYTES),
        cost_estimate=small_cost(),
        name="expert_sums",
    )(*flat, weights)


def load_copies(sequence, half, sources, x_all, dy_all, semaphores):
    for n in range(4):
        target = x_all if n < 2 else dy_all
        yield pltpu.make_async_copy(
            sources[2 * sequence + n % 2].at[pl.ds((n // 2) * half, half), :],
            target.at[pl.ds((2 * sequence + n % 2) * half, half), :],
            semaphores.at[4 * sequence + n],
        )


def expert_weight_grads(sequences, terms, number, hidden):
    width = sequences[0][0].shape[1]
    half = sequences[0][0].shape[0] // 2 // 128 * 128
    tokens = 2 * half
    flat = [array for sequence in sequences for array in sequence]
    total = len(sequences)
    quarter = width // 4
    per_load = 4 * total

    def kernel(*refs):
        sources, refs = refs[: len(flat)], refs[len(flat) :]
        term_refs, refs = refs[: 2 * len(terms)], refs[2 * len(terms) :]
        result_refs, refs = refs[: 4 * number], refs[4 * number :]
        x_all, dy_all, inner_all, grad_all, result, semaphores, term_semaphores, out_semaphores = refs

        def row_copies(of_gradients):
            for s in range(total):
                copies = list(load_copies(s, half, sources, x_all, dy_all, semaphores))
                yield from copies[2:] if of_gradients else copies[:2]

        def term_copies(e, of_products):
            place = 0
            for n, (inner, _, start) in enumerate(terms):
                rows = inner.shape[0]
                size = 2 * hidden if of_products else hidden
                yield pltpu.make_async_copy(
                    term_refs[2 * n + of_products].at[:, pl.ds((start + e) * size, size)],
                    (grad_all if of_products else inner_all).at[e, pl.ds(place, rows), :],
                    term_semaphores.at[2 * len(terms) * e + 2 * n + of_products],
                )
                place += rows

        def out_copies(e):
            for q in range(4):
                yield pltpu.make_async_copy(
                    result.at[e, pl.ds(q * quarter, quarter), :],
                    result_refs[4 * e + q],
                    out_semaphores.at[4 * e + q],
                )

        first = [*row_copies(True), *term_copies(0, 0)]
        second = [*row_copies(False), *term_copies(0, 1)]
        later = [[*term_copies(e, 0), *term_copies(e, 1)] for e in range(1, number)]
        for copy in [*first, *second, *(copy for one in later for copy in one)]:
            copy.start()
        for e in range(number):
            for copy in first if e == 0 else later[e - 1]:
                copy.wait()
            result[e, :, 2 * hidden :] = contract_rows(dy_all[...], inner_all[e]).astype(jnp.bfloat16)
            if e == 0:
                for copy in second:
                    copy.wait()
            result[e, :, : 2 * hidden] = contract_rows(x_all[...], grad_all[e]).astype(jnp.bfloat16)
            for copy in out_copies(e):
                copy.start()
        for e in range(number):
            for copy in out_copies(e):
                copy.wait()

    anywhere = pl.BlockSpec(memory_space=pl.ANY)
    return pl.pallas_call(
        kernel,
        in_specs=[anywhere] * (len(flat) + 2 * len(terms)),
        out_specs=[anywhere] * (4 * number),
        scratch_shapes=[pltpu.VMEM((total * tokens, width), jnp.bfloat16)] * 2
        + [
            pltpu.VMEM((number, total * tokens, hidden), jnp.bfloat16),
            pltpu.VMEM((number, total * tokens, 2 * hidden), jnp.bfloat16),
            pltpu.VMEM((number, width, 3 * hidden), jnp.bfloat16),
            pltpu.SemaphoreType.DMA((per_load,)),
            pltpu.SemaphoreType.DMA((2 * len(terms) * number,)),
            pltpu.SemaphoreType.DMA((4 * number,)),
        ],
        out_shape=[jax.ShapeDtypeStruct((quarter, 3 * hidden), jnp.bfloat16)] * (4 * number),
        compiler_params=pltpu.CompilerParams(vmem_limit_bytes=VMEM_BYTES),
        cost_estimate=small_cost(),
        name="expert_weight_grads",
    )(*flat, *(array for term in terms for array in term[:2]))


def own_weight_grads(sequences, terms, arrived, hidden):
    width = sequences[0][0].shape[1]
    half = sequences[0][0].shape[0] // 2 // 128 * 128
    tokens = 2 * half
    counts = [pair[0].shape[0] // tokens for pair in terms]
    flat = [array for sequence in sequences for array in sequence]
    total = len(sequences)
    quarter = width // 4

    def kernel(*refs):
        sources, refs = refs[: len(flat)], refs[len(flat) :]
        term_refs, refs = refs[: 2 * len(counts)], refs[2 * len(counts) :]
        arrived_refs, refs = refs[:6], refs[6:]
        gate_ref, up_ref, down_ref, x_all, dy_all, semaphores = refs
        for s in range(total):
            for copy in load_copies(s, half, sources, x_all, dy_all, semaphores):
                copy.start()
        gate_up = down = None
        first = 0
        for joined, count in enumerate(counts):
            for s in range(first, first + count):
                for copy in load_copies(s, half, sources, x_all, dy_all, semaphores):
                    copy.wait()
            span = pl.ds(first * tokens, count * tokens)
            one = contract_rows(x_all[span, :], term_refs[2 * joined + 1][...])
            two = contract_rows(term_refs[2 * joined][...], dy_all[span, :])
            gate_up = one if gate_up is None else gate_up + one
            down = two if down is None else down + two
            first += count
        for q in range(4):
            rows = slice(q * quarter, (q + 1) * quarter)
            inside = slice(q % 2 * quarter, (q % 2 + 1) * quarter)
            more = arrived_refs[q][...].astype(jnp.float32) + arrived_refs[4 + q // 2][
                inside, :
            ].astype(jnp.float32)
            both = gate_up[rows] + more[:, : 2 * hidden]
            gate_ref[0, rows, :] = both[:, :hidden]
            up_ref[0, rows, :] = both[:, hidden:]
            down_ref[0, :, rows] = down[:, rows] + more[:, 2 * hidden :].T

    def beside(count, columns):
        return pl.BlockSpec((count * tokens, columns), lambda e: (0, 0))

    tall = jax.ShapeDtypeStruct((1, width, hidden), jnp.float32)
    flat_down = jax.ShapeDtypeStruct((1, hidden, width), jnp.float32)
    return pl.pallas_call(
        kernel,
        grid=(1,),
        in_specs=[pl.BlockSpec(memory_space=pl.ANY)] * len(flat)
        + [beside(count, columns) for count in counts for columns in (hidden, 2 * hidden)]
        + [whole(quarter, 3 * hidden)] * 4
        + [whole(2 * quarter, 3 * hidden)] * 2,
        out_specs=[whole(*tall.shape), whole(*tall.shape), whole(*flat_down.shape)],
        scratch_shapes=[pltpu.VMEM((total * tokens, width), jnp.bfloat16)] * 2
        + [pltpu.SemaphoreType.DMA((4 * total,))],
        out_shape=[tall, tall, flat_down],
        compiler_params=pltpu.CompilerParams(vmem_limit_bytes=VMEM_BYTES),
        cost_estimate=small_cost(),
        name="own_weight_grads",
    )(*flat, *(array for pair in terms for array in pair), *arrived)


def planes_of_four(
    hidden_in,
    attn_gain,
    w_query,
    w_key,
    w_value,
    w_output,
    moe_gain,
    w_gate,
    w_up,
    w_down,
    gate_logits,
    routes,
    out_grad,
):
    tokens, width = hidden_in.shape
    half = tokens // 2
    experts = lax.axis_size("expert")
    columns = [[4 * z + r for z in range(4)] for r in range(4)]
    core = lax.axis_index("tensor")
    expert = lax.axis_index("expert")
    plane = expert // 4
    bit_x = expert % 2
    bit_y = (expert // 2) % 2
    hidden = w_down.shape[1]
    together = lax.optimization_barrier

    own_weights = jnp.concatenate([w_gate[0], w_up[0], w_down[0].T], axis=1)
    quarter = width // 4
    pieces = [own_weights[:quarter], own_weights[quarter : 2 * quarter], own_weights[2 * quarter :]]
    gate_weights = jax.nn.softmax(gate_logits, axis=-1)
    names = jnp.arange(experts, dtype=jnp.int32)
    dense = jnp.sum(
        jnp.where(routes.T[:, None, :] == names[None, :, None], gate_weights.T[:, None, :], 0.0),
        axis=0,
    )
    dense = lax.dynamic_slice_in_dim(dense, core * half, half, 1)
    coarse = dense.astype(jnp.bfloat16)
    fine = (dense - coarse.astype(jnp.float32)).astype(jnp.bfloat16)
    extra = jnp.pad(jnp.concatenate([coarse, fine], axis=1), ((0, 0), (0, width - 2 * half)))
    out_grad_half = part(out_grad, core, 2)
    dy_own = jnp.concatenate([out_grad_half, extra], axis=0)

    x0, y0 = flip(pieces[0], 1), flip(pieces[0], 2)
    dy_up_one, dy_down_one = climb(dy_own), descend(dy_own)
    cosine, sine = (jnp.asarray(table) for table in rotary_tables(tokens))
    normed, queries, keys, values, mixed, keep, send = attention_forward(
        core.reshape(1), hidden_in, attn_gain[None], w_query, w_key, w_value, w_output, cosine, sine
    )
    send, x0, y0, dy_up_one, dy_down_one, piece = together(
        (send, x0, y0, dy_up_one, dy_down_one, pieces[1])
    )
    x1, y1 = flip(piece, 1), flip(piece, 2)
    middle = keep + swap(send).astype(jnp.float32)
    scale_two = lax.rsqrt(jnp.mean(middle * middle, axis=-1, keepdims=True) + epsilon)
    unit_two = middle * scale_two
    rows_in = (unit_two * moe_gain).astype(jnp.bfloat16)
    up_one, down_one = climb(rows_in), descend(rows_in)
    x1, y1, up_one, down_one, dy_up_one, dy_down_one, piece = together(
        (x1, y1, up_one, down_one, dy_up_one, dy_down_one, pieces[2])
    )
    up_one = jnp.concatenate([up_one, dy_up_one], axis=0)
    down_one = jnp.concatenate([down_one, dy_down_one], axis=0)
    up_one, down_one, piece = together((up_one, down_one, piece))
    x2, y2 = flip(piece, 1), flip(piece, 2)
    up_two, down_two = climb(up_one), descend(down_one)
    own = jnp.concatenate([rows_in, dy_own], axis=0)
    first = jnp.where(plane == 0, down_one, up_one)
    own, first = (own, swap(own)), (first, swap(first))
    far_from_y = jnp.concatenate([y0, y1], axis=0)
    x2, y2, up_two, down_two, own, first, far_from_y = together(
        (x2, y2, up_two, down_two, own, first, far_from_y)
    )
    far_weights = [flip(far_from_y, 1), flip(x2, 2)]
    up_three, down_three = climb(up_two), descend(down_two)
    number = expert.reshape(1)
    second = jnp.where(plane == 0, down_two, jnp.where(plane == 3, up_two, down_one))
    second = (second, swap(second))
    near_pieces = [[own_weights], [x0, x1, x2], [y0, y1, y2]]
    near_early, near_second, near_weights = expert_terms(
        number,
        [([own, first], 0), ([second], 0)],
        [[(piece, None) for piece in one] for one in near_pieces],
        0,
        True,
    )
    far_weights, up_three, down_three, near_early, near_second, second = together(
        (far_weights, up_three, down_three, near_early, near_second, second)
    )
    third = jnp.where(
        plane == 0,
        down_three,
        jnp.where(plane == 1, down_two, jnp.where(plane == 2, up_two, up_three)),
    )
    third = (third, swap(third))
    far_pieces = [(piece, None) for piece in far_weights]
    all_third, far_second, weights = expert_terms(
        number,
        [([third], 0), ([second], 3)],
        [[(near_weights, 0)], [(near_weights, 1)], [(near_weights, 2)], far_pieces],
        0,
        True,
    )
    (far_early,) = expert_terms(number, [([own, first], 0)], [[(weights, 3)]], 3, False)
    to_far = expert_weight_grads(
        [third, second, own, first], [(*all_third, 3), (*far_second, 0), (*far_early, 0)], 1, hidden
    )
    over_x, over_y = [flip(to_far[0], 1)], [flip(to_far[2], 2)]
    to_far, near_second, far_second = together((to_far, near_second, far_second))
    late_sums = expert_sums(
        [[(*all_third, 0)], [(*near_second, 0), (*far_second, 3)]], weights, half
    )
    late_sums, over_x, over_y, to_far = together((late_sums, over_x, over_y, to_far))
    back_late = add_low(late_sums[0], swap(late_sums[1]))
    back_late, near_early, all_third = together((back_late, near_early, all_third))
    second_back, third_back = back_late[1], back_late[0]

    falling, rising = descend(third_back), climb(third_back)
    over_x, over_y = over_x + [flip(to_far[1], 1)], over_y + [flip(to_far[3], 2)]
    beside = expert_weight_grads(
        [own, first, second, third],
        [(*near_early, 1), (*near_second, 1), (*all_third, 1)],
        2,
        hidden,
    )
    falling, rising, beside, over_x, over_y, far_early = together(
        (falling, rising, beside, over_x, over_y, far_early)
    )
    to_x, to_y = beside[:4], beside[4:]
    falling = add_low(jnp.where(plane == 3, second_back, third_back), falling)
    rising = add_low(jnp.where(plane == 0, second_back, third_back), rising)
    falling, rising, far_early = together((falling, rising, far_early))
    falling, rising = descend(falling), climb(rising)
    from_x, from_y = [flip(to_x[0], 1)], [flip(to_y[2], 2)]
    early_sums = expert_sums([[(*near_early, 0), (*far_early, 3)]], weights, half)
    falling, rising, early_sums, from_x, from_y, to_x, to_y = together(
        (falling, rising, early_sums, from_x, from_y, to_x, to_y)
    )
    back_early = add_low(early_sums[0], swap(early_sums[1]))
    own_back, first_back = back_early[0], back_early[1]
    falling = add_low(first_back, falling)
    rising = add_low(jnp.where(plane == 0, first_back, second_back), rising)
    falling, rising, early_sums, late_sums, over_x = together(
        (falling, rising, early_sums, late_sums, over_x)
    )
    falling, rising = descend(falling), climb(rising)
    from_x, from_y = from_x + [flip(to_x[1], 1)], from_y + [flip(to_y[3], 2)]
    with_x = jnp.concatenate([add_low(to_y[n], over_x[n]) for n in range(2)], axis=0)
    with_y = jnp.concatenate([add_low(to_x[2 + n], over_y[n]) for n in range(2)], axis=0)
    out_late = add_low(late_sums[2], swap(late_sums[3]))
    out_early = add_low(early_sums[2], swap(early_sums[3]))
    own_out, first_out, second_out, third_out = out_early[0], out_early[1], out_late[1], out_late[0]
    by_plane = [
        jnp.where(plane == 0, own_out, jnp.where(plane == 1, first_out, third_out)),
        jnp.where(plane == 1, own_out, jnp.where(plane == 3, second_out, first_out)),
        jnp.where(plane == 2, own_out, jnp.where(plane == 3, first_out, second_out)),
        jnp.where(plane == 3, own_out, jnp.where(plane == 2, second_out, third_out)),
    ]
    results = jnp.concatenate(by_plane, axis=0)
    falling, rising, results, from_x, from_y, with_x, with_y = together(
        (falling, rising, results, from_x, from_y, with_x, with_y)
    )
    moe_result = lax.psum_scatter(
        results, "expert", axis_index_groups=columns, scatter_dimension=0, tiled=True
    )
    grad_rows = (
        own_back.astype(jnp.float32) + falling.astype(jnp.float32) + rising.astype(jnp.float32)
    )
    grad_out = out_grad_half.astype(jnp.float32)
    grad_unit_two = grad_rows * moe_gain
    grad_moe_gain = jnp.sum(grad_rows * unit_two, axis=0)
    grad_middle = grad_out + scale_two * (
        grad_unit_two - unit_two * jnp.mean(grad_unit_two * unit_two, axis=-1, keepdims=True)
    )
    grad_attn_half = grad_middle.astype(jnp.bfloat16)
    grad_attn = ordered(grad_attn_half, swap(grad_attn_half), core)
    grad_output = contract_rows(mixed, grad_attn).astype(jnp.bfloat16)
    grad_attn, grad_output = together((grad_attn, grad_output))
    output_parts = plane_scatter_first(grad_output, bit_x, bit_y)
    grad_all_pre = attention_backward(grad_attn, w_output, queries, keys, values, cosine, sine)
    grad_all_pre, output_parts = together((grad_all_pre, output_parts))
    grad_projections = contract_rows(normed, grad_all_pre).astype(jnp.bfloat16)
    output_parts = plane_scatter_second(output_parts, bit_x, bit_y)
    grad_projections, output_parts = together((grad_projections, output_parts))
    projection_parts = plane_scatter_first(grad_projections, bit_x, bit_y)
    w_all = jnp.concatenate([w_query, w_key, w_value], axis=1)
    grad_normed_part = contract_cols(grad_all_pre, w_all).astype(jnp.bfloat16)
    grad_normed = part(grad_normed_part, core, 2).astype(jnp.float32) + swap(
        part(grad_normed_part, 1 - core, 2)
    ).astype(jnp.float32)
    source_half = part(hidden_in, core, 2).astype(jnp.float32)
    scale_half = lax.rsqrt(jnp.mean(source_half * source_half, axis=-1, keepdims=True) + epsilon)
    unit_half = source_half * scale_half
    grad_unit_one = grad_normed * attn_gain
    grad_attn_gain = jnp.sum(grad_normed * unit_half, axis=0)
    grad_in_half = grad_middle + scale_half * (
        grad_unit_one - unit_half * jnp.mean(grad_unit_one * unit_half, axis=-1, keepdims=True)
    )
    gains = jnp.stack([grad_attn_gain, grad_moe_gain])
    projection_parts, gains, grad_in_half = together((projection_parts, gains, grad_in_half))
    projection_parts = plane_scatter_second(projection_parts, bit_x, bit_y)
    gains = (gains + swap(gains)).reshape(-1, grad_projections.shape[1])
    gain_rows = gains.shape[0]
    gains = jnp.pad(gains, ((0, 16 - gain_rows), (0, 0))).astype(jnp.bfloat16)
    grad_in = ordered(grad_in_half, swap(grad_in_half), core)
    output_both = jnp.concatenate(output_parts, axis=0)
    projection_both = jnp.concatenate([*projection_parts, gains], axis=0)
    projection_both, output_both, grad_in, moe_result, with_x, with_y = together(
        (projection_both, output_both, grad_in, moe_result, with_x, with_y)
    )
    output_both, projection_both = lax.psum(
        (output_both, projection_both), "expert", axis_index_groups=columns
    )
    block_half = (middle + moe_result.astype(jnp.float32)).astype(jnp.bfloat16)
    block_out = ordered(block_half, swap(block_half), core)
    then_y, then_x = flip(with_x, 2), flip(with_y, 1)
    output_both, projection_both, block_out, then_x, then_y = together(
        (output_both, projection_both, block_out, then_x, then_y)
    )
    gains, projection_both = projection_both[-16:].astype(jnp.float32), projection_both[:-16]
    output_halves = plane_gather_first(*jnp.split(output_both, 2), bit_x, bit_y)
    projection_halves = plane_gather_first(*jnp.split(projection_both, 2), bit_x, bit_y)
    output_halves, projection_halves, gains, then_x, then_y = together(
        (output_halves, projection_halves, gains, then_x, then_y)
    )
    arrived = (*from_x, *from_y, then_y, then_x)
    expert_grads = own_weight_grads(
        [own, first, second, third], [near_early, near_second, all_third], arrived, hidden
    )
    output_pieces = plane_gather_second(output_halves, bit_x, bit_y)
    projection_pieces = plane_gather_second(projection_halves, bit_x, bit_y)
    expert_grads, output_pieces, projection_pieces, gains = together(
        (expert_grads, output_pieces, projection_pieces, gains)
    )
    gains = (gains + flip(gains, 1)) + (flip(gains, 2) + flip(gains, 3))
    gains_sum = gains[:gain_rows].reshape(2, width)
    grad_gate, grad_up, grad_down = expert_grads
    bits = jnp.stack([bit_x, bit_y])
    (output_sum,) = lay_out(bits, output_pieces, (width,))
    projections = lay_out(bits, projection_pieces, [w.shape[1] for w in (w_query, w_key, w_value)])
    return (
        block_out,
        grad_in,
        gains_sum[0],
        *projections,
        output_sum,
        gains_sum[1],
        grad_gate,
        grad_up,
        grad_down,
    )


def solution(mesh):
    on_device = planes_of_four if mesh.shape["expert"] == 16 else routed_slots
    return jax.shard_map(
        on_device,
        mesh=mesh,
        in_specs=(
            P("expert", None),
            P(),
            P(None, "tensor"),
            P(None, "tensor"),
            P(None, "tensor"),
            P("tensor", None),
            P(),
            P("expert", None, "tensor"),
            P("expert", None, "tensor"),
            P("expert", "tensor", None),
            P("expert", None),
            P("expert", None),
            P("expert", None),
        ),
        out_specs=(
            P("expert", None),
            P("expert", None),
            P(),
            P(None, "tensor"),
            P(None, "tensor"),
            P(None, "tensor"),
            P("tensor", None),
            P(),
            P("expert", None, "tensor"),
            P("expert", None, "tensor"),
            P("expert", "tensor", None),
        ),
        check_vma=False,
    )
```

```python
import math

import jax
import jax.numpy as jnp
import numpy as np
from jax import lax
from jax.experimental import pallas as pl
from jax.experimental.pallas import tpu as pltpu
from jax.sharding import PartitionSpec as P

HD = 128


epsilon = 1e-06
rope_base = 10000.0
masked_score = -1e30


def rotate(values, places, sign):
    halfway = values.shape[-1] // 2
    frequency = rope_base ** (-jnp.arange(halfway, dtype=jnp.float32) / halfway)
    angles = places.astype(jnp.float32)[:, None] * frequency[None, :]
    cosine = jnp.cos(angles)[:, None, :]
    sine = sign * jnp.sin(angles)[:, None, :]
    first = values[..., :halfway]
    second = values[..., halfway:]
    return jnp.concatenate(
        [first * cosine - second * sine, second * cosine + first * sine], axis=-1
    )


def contract_rows(left, right):
    return lax.dot_general(
        left, right, (((0,), (0,)), ((), ())), preferred_element_type=jnp.float32
    )


def contract_cols(left, right):
    return lax.dot_general(
        left, right, (((1,), (1,)), ((), ())), preferred_element_type=jnp.float32
    )


def block_scores(query_block, keys_used, row_start, scale_factor):
    query_rows = query_block.shape[0]
    key_rows = keys_used.shape[0]
    raw_scores = (
        jnp.einsum("qcgd,kcd->cgqk", query_block, keys_used, preferred_element_type=jnp.float32)
        * scale_factor
    )
    row_ids = row_start + jnp.arange(query_rows)
    causal = jnp.arange(key_rows)[None, :] <= row_ids[:, None]
    return jnp.where(causal, raw_scores, masked_score)


def routed_slots(
    hidden_in,
    attn_gain,
    w_query,
    w_key,
    w_value,
    w_output,
    moe_gain,
    w_gate,
    w_up,
    w_down,
    gate_logits,
    routes,
    out_grad,
):
    tokens, model_width = hidden_in.shape
    experts = lax.axis_size("expert")
    tensor_ranks = lax.axis_size("tensor")
    tensor_rank = lax.axis_index("tensor")
    route_width = routes.shape[1]
    route_count = tokens * route_width
    capacity = 2 * route_count // experts
    half_slots = capacity // tensor_ranks
    heads_local = w_query.shape[1] // HD
    kv_local = w_key.shape[1] // HD
    groups = heads_local // kv_local
    scale_factor = 1.0 / math.sqrt(HD)
    block_rows = min(512, tokens)
    places = jnp.arange(tokens, dtype=jnp.int32)
    flat_routes = routes.reshape(-1)
    route_hits = (flat_routes[:, None] == jnp.arange(experts, dtype=jnp.int32)[None, :]).astype(
        jnp.int32
    )
    slot_index = jnp.sum(jnp.cumsum(route_hits, axis=0) * route_hits, axis=1) - 1
    which_route = (
        jnp.full((experts * capacity,), route_count, jnp.int32)
        .at[flat_routes * capacity + slot_index]
        .set(jnp.arange(route_count, dtype=jnp.int32))
    )
    which_token = which_route // route_width
    own_half = slot_index // half_slots == tensor_rank
    back_index = jnp.where(
        own_half, flat_routes * half_slots + slot_index % half_slots, experts * half_slots
    )
    gate_weights = jax.nn.softmax(gate_logits, axis=-1)
    full_gate, full_up, full_down = (w_gate[0], w_up[0], w_down[0])

    def deliver(buffer):
        arrived_all = lax.all_to_all(buffer, "expert", split_axis=0, concat_axis=0, tiled=True)
        return arrived_all.reshape(experts * capacity, model_width)

    def give_back(partial_value):
        summed_rows = lax.psum_scatter(
            partial_value.reshape(experts, capacity, model_width).astype(jnp.bfloat16),
            "tensor",
            scatter_dimension=1,
            tiled=True,
        )
        returned = lax.all_to_all(summed_rows, "expert", split_axis=0, concat_axis=0, tiled=True)
        return jnp.concatenate(
            [
                returned.reshape(experts * half_slots, model_width),
                jnp.zeros((1, model_width), jnp.bfloat16),
            ],
            axis=0,
        )

    def collect(returned, weights):
        picked = returned[back_index].astype(jnp.float32).reshape(tokens, route_width, model_width)
        return lax.psum(
            jnp.sum(picked * weights[:, :, None], axis=1).astype(jnp.bfloat16), "tensor"
        ).astype(jnp.float32)

    source = hidden_in.astype(jnp.float32)
    scale_one = lax.rsqrt(jnp.mean(source * source, axis=-1, keepdims=True) + epsilon)
    unit_one = source * scale_one
    normed = (unit_one * attn_gain).astype(jnp.bfloat16)
    query_pre = jnp.dot(normed, w_query, preferred_element_type=jnp.float32).reshape(
        tokens, heads_local, HD
    )
    queries = (
        rotate(query_pre, places, 1.0).astype(jnp.bfloat16).reshape(tokens, kv_local, groups, HD)
    )
    key_pre = jnp.dot(normed, w_key, preferred_element_type=jnp.float32).reshape(
        tokens, kv_local, HD
    )
    keys_used = rotate(key_pre, places, 1.0).astype(jnp.bfloat16)
    values_used = (
        jnp.dot(normed, w_value, preferred_element_type=jnp.float32)
        .astype(jnp.bfloat16)
        .reshape(tokens, kv_local, HD)
    )
    row_start = 0
    query_block = queries
    raw_scores = block_scores(query_block, keys_used, row_start, scale_factor)
    biggest = jnp.max(raw_scores, axis=-1, keepdims=True)
    exponent = jnp.exp(raw_scores - biggest)
    row_total = jnp.sum(exponent, axis=-1, keepdims=True)
    weights_low = (exponent / row_total).astype(jnp.bfloat16)
    logsums = [biggest + jnp.log(row_total)]
    attended = jnp.einsum(
        "cgqk,kcd->qcgd", weights_low, values_used, preferred_element_type=jnp.float32
    )
    mixed_blocks = attended.reshape(block_rows, heads_local * HD).astype(jnp.bfloat16)
    attn_part = jnp.dot(mixed_blocks, w_output, preferred_element_type=jnp.float32)
    middle = source + lax.psum(attn_part.astype(jnp.bfloat16), "tensor").astype(jnp.float32)
    scale_two = lax.rsqrt(jnp.mean(middle * middle, axis=-1, keepdims=True) + epsilon)
    unit_two = middle * scale_two
    rows_in = (unit_two * moe_gain).astype(jnp.bfloat16)
    padded_rows = jnp.concatenate([rows_in, jnp.zeros((1, model_width), jnp.bfloat16)], axis=0)
    arrived = deliver(padded_rows[which_token].reshape(experts, capacity, model_width))
    gate_pre = jnp.dot(arrived, full_gate, preferred_element_type=jnp.float32)
    up_pre = jnp.dot(arrived, full_up, preferred_element_type=jnp.float32)
    sigmoid = jax.nn.sigmoid(gate_pre)
    activated = gate_pre * sigmoid
    hidden_units = (activated * up_pre).astype(jnp.bfloat16)
    produced = jnp.dot(hidden_units, full_down, preferred_element_type=jnp.float32)
    moe_result = collect(give_back(produced), gate_weights)
    block_out = (middle + moe_result).astype(jnp.bfloat16)
    grad_out = out_grad.astype(jnp.float32)
    route_grads = (
        (gate_weights[:, :, None] * grad_out[:, None, :])
        .astype(jnp.bfloat16)
        .reshape(route_count, model_width)
    )
    padded_grads = jnp.concatenate([route_grads, jnp.zeros((1, model_width), jnp.bfloat16)], axis=0)
    grad_arrived = deliver(padded_grads[which_route].reshape(experts, capacity, model_width))
    grad_down = contract_rows(hidden_units, grad_arrived)
    grad_inner = contract_cols(grad_arrived, full_down)
    grad_gate_pre = (grad_inner * up_pre * sigmoid * (1.0 + gate_pre * (1.0 - sigmoid))).astype(
        jnp.bfloat16
    )
    grad_up_pre = (grad_inner * activated).astype(jnp.bfloat16)
    grad_gate = contract_rows(arrived, grad_gate_pre)
    grad_up = contract_rows(arrived, grad_up_pre)
    grad_arrived_rows = contract_cols(grad_gate_pre, full_gate) + contract_cols(
        grad_up_pre, full_up
    )
    grad_rows = collect(give_back(grad_arrived_rows), jnp.ones_like(gate_weights))
    grad_unit_two = grad_rows * moe_gain
    grad_moe_gain = jnp.sum(grad_rows * unit_two, axis=0)
    grad_middle = grad_out + scale_two * (
        grad_unit_two - unit_two * jnp.mean(grad_unit_two * unit_two, axis=-1, keepdims=True)
    )
    grad_attn = grad_middle.astype(jnp.bfloat16)
    grad_output = contract_rows(mixed_blocks, grad_attn)
    grad_mixed = (
        contract_cols(grad_attn, w_output)
        .astype(jnp.bfloat16)
        .reshape(tokens, kv_local, groups, HD)
    )
    grad_query_blocks = []
    grad_keys = jnp.zeros((tokens, kv_local, HD), jnp.float32)
    grad_values = jnp.zeros((tokens, kv_local, HD), jnp.float32)
    for block_number, row_start in enumerate(range(0, tokens, block_rows)):
        query_block = queries
        raw_scores = block_scores(query_block, keys_used, row_start, scale_factor)
        probs = jnp.exp(raw_scores - logsums[block_number])
        probs_low = probs.astype(jnp.bfloat16)
        grad_probs = jnp.einsum(
            "qcgd,kcd->cgqk", grad_mixed, values_used, preferred_element_type=jnp.float32
        )
        delta = jnp.sum(probs * grad_probs, axis=-1, keepdims=True)
        grad_scores = (probs * (grad_probs - delta)).astype(jnp.bfloat16)
        grad_query_blocks.append(
            jnp.einsum("cgqk,kcd->qcgd", grad_scores, keys_used, preferred_element_type=jnp.float32)
            * scale_factor
        )
        grad_keys = (
            jnp.einsum(
                "cgqk,qcgd->kcd", grad_scores, query_block, preferred_element_type=jnp.float32
            )
            * scale_factor
        )
        grad_values = jnp.einsum(
            "cgqk,qcgd->kcd", probs_low, grad_mixed, preferred_element_type=jnp.float32
        )
    grad_queries = grad_query_blocks[0].reshape(tokens, heads_local, HD)
    grad_query_pre = (
        rotate(grad_queries, places, -1.0).astype(jnp.bfloat16).reshape(tokens, heads_local * HD)
    )
    grad_key_pre = (
        rotate(grad_keys, places, -1.0).astype(jnp.bfloat16).reshape(tokens, kv_local * HD)
    )
    grad_value_pre = grad_values.astype(jnp.bfloat16).reshape(tokens, kv_local * HD)
    grad_query = contract_rows(normed, grad_query_pre)
    grad_key = contract_rows(normed, grad_key_pre)
    grad_value = contract_rows(normed, grad_value_pre)
    grad_normed_part = (
        contract_cols(grad_query_pre, w_query)
        + contract_cols(grad_key_pre, w_key)
        + contract_cols(grad_value_pre, w_value)
    )
    grad_normed = lax.psum(grad_normed_part.astype(jnp.bfloat16), "tensor").astype(jnp.float32)
    grad_unit_one = grad_normed * attn_gain
    grad_attn_gain = jnp.sum(grad_normed * unit_one, axis=0)
    grad_in = grad_middle + scale_one * (
        grad_unit_one - unit_one * jnp.mean(grad_unit_one * unit_one, axis=-1, keepdims=True)
    )
    summed = lax.psum(
        (grad_query, grad_key, grad_value, grad_output, grad_attn_gain, grad_moe_gain), "expert"
    )
    return (
        block_out,
        grad_in,
        summed[4],
        summed[0],
        summed[1],
        summed[2],
        summed[3],
        summed[5],
        grad_gate[None],
        grad_up[None],
        grad_down[None],
    )


VMEM_BYTES = 60 * 2**20


def small_cost(**_):
    return pl.CostEstimate(flops=1000, bytes_accessed=1000, transcendentals=0)


def dot(left, right):
    return jnp.dot(left, right, preferred_element_type=jnp.float32)


def whole(*shape):
    return pl.BlockSpec(shape, lambda *_: (0,) * len(shape), pipeline_mode=pl.Buffered(1))


def swap(value):
    return lax.ppermute(value, "tensor", [(0, 1), (1, 0)])


def flip(value, bit):
    places = lax.axis_size("expert")
    return lax.ppermute(value, "expert", [(i, i ^ bit) for i in range(places)])


def climb(value):
    places = lax.axis_size("expert")
    return lax.ppermute(value, "expert", [(i, i + 4) for i in range(places - 4)])


def descend(value):
    places = lax.axis_size("expert")
    return lax.ppermute(value, "expert", [(i + 4, i) for i in range(places - 4)])


def part(value, index, count):
    size = value.shape[0] // count
    return lax.dynamic_slice_in_dim(value, index * size, size, 0)


def ordered(own, other, place):
    return jnp.where(
        place == 0,
        jnp.concatenate([own, other], axis=0),
        jnp.concatenate([other, own], axis=0),
    )


def add_low(kept, arrived):
    return (kept.astype(jnp.float32) + arrived.astype(jnp.float32)).astype(jnp.bfloat16)


def plane_scatter_first(value, bit_x, bit_y):
    left, right = jnp.split(value, 2, axis=0)
    left = add_low(part(left, bit_x, 2), flip(part(left, 1 - bit_x, 2), 1))
    right = add_low(part(right, bit_y, 2), flip(part(right, 1 - bit_y, 2), 2))
    return left, right


def plane_scatter_second(halves, bit_x, bit_y):
    left, right = halves
    left = add_low(part(left, bit_y, 2), flip(part(left, 1 - bit_y, 2), 2))
    right = add_low(part(right, bit_x, 2), flip(part(right, 1 - bit_x, 2), 1))
    return left, right


def plane_gather_first(left, right, bit_x, bit_y):
    return ordered(left, flip(left, 2), bit_y), ordered(right, flip(right, 1), bit_x)


def plane_gather_second(left, right):
    return flip(left, 1), flip(right, 2)


def lay_out(bits, halves, widths, arrived, earlier=()):
    rows, columns = halves[0].shape

    def kernel(bits_ref, *refs):
        sources, refs = refs[:2], refs[2 + len(earlier) :]
        results, (wide, semaphores) = refs[: len(widths)], refs[len(widths) :]
        copies = []
        for side in range(2):
            wide[side] = sources[side][...].astype(jnp.float32)
            bit = bits_ref[side]
            place = pl.multiple_of((2 * side + (1 - bit if arrived else bit)) * rows, rows)
            start = 0
            for n, (result, size) in enumerate(zip(results, widths, strict=True)):
                copies.append(
                    pltpu.make_async_copy(
                        wide.at[side, :, pl.ds(start, size)],
                        result.at[pl.ds(place, rows), :],
                        semaphores.at[side, n],
                    )
                )
                copies[-1].start()
                start += size
        for copy in copies:
            copy.wait()

    anywhere = pl.BlockSpec(memory_space=pl.ANY)
    return pl.pallas_call(
        kernel,
        in_specs=[pl.BlockSpec(memory_space=pltpu.SMEM)]
        + [pl.BlockSpec(memory_space=pltpu.VMEM)] * 2
        + [anywhere] * len(earlier),
        out_specs=[anywhere] * len(widths),
        out_shape=[jax.ShapeDtypeStruct((4 * rows, size), jnp.float32) for size in widths],
        scratch_shapes=[
            pltpu.VMEM((2, rows, columns), jnp.float32),
            pltpu.SemaphoreType.DMA((2, len(widths))),
        ],
        input_output_aliases={3 + n: n for n in range(len(earlier))},
        compiler_params=pltpu.CompilerParams(vmem_limit_bytes=VMEM_BYTES),
        cost_estimate=small_cost(),
        name="lay_out",
    )(bits, *halves, *earlier)


def rotary_tables(tokens):
    halfway = HD // 2
    frequency = rope_base ** (-np.arange(halfway, dtype=np.float64) / halfway)
    angles = np.arange(tokens)[:, None] * frequency[None, :]
    cosine, sine = np.cos(angles), np.sin(angles)
    return (
        np.concatenate([cosine, cosine], axis=1).astype(np.float32),
        np.concatenate([-sine, sine], axis=1).astype(np.float32),
    )


def causal_scores(query_block, keys, row_start, scale_factor):
    raw = contract_cols(query_block, keys) * scale_factor
    row_ids = row_start + lax.broadcasted_iota(jnp.int32, raw.shape, 0)
    return jnp.where(lax.broadcasted_iota(jnp.int32, raw.shape, 1) <= row_ids, raw, masked_score)


def softmax_rows(raw):
    exponent = jnp.exp(raw - jnp.max(raw, axis=-1, keepdims=True))
    return exponent / jnp.sum(exponent, axis=-1, keepdims=True)


def attention_forward(core, hidden, gain, w_query, w_key, w_value, w_output, cosine, sine):
    tokens, width = hidden.shape
    half = tokens // 2
    local = w_query.shape[1]
    heads = local // HD
    scale_factor = 1.0 / math.sqrt(HD)

    def kernel(
        core_ref, hidden_ref, gain_ref, wq_ref, wk_ref, wv_ref, wo_ref, cos_ref, sin_ref,
        normed_ref, query_ref, key_ref, value_ref, mixed_ref, keep_ref, send_ref, part_ref,
    ):
        for block in range(2):
            rows = pl.ds(block * half, half)
            source = hidden_ref[rows, :].astype(jnp.float32)
            scale = lax.rsqrt(jnp.mean(source * source, axis=-1, keepdims=True) + epsilon)
            normed = (source * scale * gain_ref[...]).astype(jnp.bfloat16)
            normed_ref[rows, :] = normed
            cos, sin = cos_ref[rows, :], sin_ref[rows, :]

            def turned(value):
                return (value * cos + pltpu.roll(value, HD // 2, 1) * sin).astype(jnp.bfloat16)

            query_pre = dot(normed, wq_ref[...])
            for head in range(heads):
                lanes = slice(head * HD, (head + 1) * HD)
                query_ref[rows, lanes] = turned(query_pre[:, lanes])
            key_ref[rows, :] = turned(dot(normed, wk_ref[...]))
            value_ref[rows, :] = dot(normed, wv_ref[...]).astype(jnp.bfloat16)
        for block in range(2):
            rows = pl.ds(block * half, half)
            seen = pl.ds(0, (block + 1) * half)
            keys, values = key_ref[seen, :], value_ref[seen, :]
            for head in range(heads):
                lanes = slice(head * HD, (head + 1) * HD)
                raw = causal_scores(query_ref[rows, lanes], keys, block * half, scale_factor)
                probs_low = softmax_rows(raw).astype(jnp.bfloat16)
                mixed_ref[rows, lanes] = dot(probs_low, values).astype(jnp.bfloat16)
            part_ref[rows, :] = dot(mixed_ref[rows, :], wo_ref[...])
        own = pl.ds(pl.multiple_of(core_ref[0] * half, half), half)
        other = pl.ds(pl.multiple_of((1 - core_ref[0]) * half, half), half)
        keep_ref[...] = hidden_ref[own, :].astype(jnp.float32) + part_ref[own, :]
        send_ref[...] = part_ref[other, :].astype(jnp.bfloat16)

    def low(rows, columns):
        return jax.ShapeDtypeStruct((rows, columns), jnp.bfloat16)

    shapes = [
        low(tokens, width), low(tokens, local), low(tokens, HD), low(tokens, HD),
        low(tokens, local), jax.ShapeDtypeStruct((half, width), jnp.float32), low(half, width),
    ]
    operands = [hidden, gain, w_query, w_key, w_value, w_output, cosine, sine]
    return pl.pallas_call(
        kernel,
        out_shape=shapes,
        in_specs=[pl.BlockSpec(memory_space=pltpu.SMEM)]
        + [pl.BlockSpec(memory_space=pltpu.VMEM) for _ in operands],
        out_specs=[pl.BlockSpec(memory_space=pltpu.VMEM) for _ in shapes],
        scratch_shapes=[pltpu.VMEM((tokens, width), jnp.float32)],
        compiler_params=pltpu.CompilerParams(vmem_limit_bytes=VMEM_BYTES),
        cost_estimate=small_cost(
            flops=40 * 10**9, bytes_accessed=16 * 10**6, transcendentals=2 * 10**6
        ),
        name="attention_forward",
    )(core, *operands)


def output_gradient(places, mixed, own, other):
    half, width = own.shape
    local = mixed.shape[1]
    piece = local // 4

    def kernel(places_ref, mixed_ref, own_ref, other_ref, *refs):
        pieces, (whole_ref, result) = refs[:4], refs[4:]
        core = places_ref[0]
        whole_ref[pl.ds(pl.multiple_of(core * half, half), half), :] = own_ref[...]
        whole_ref[pl.ds(pl.multiple_of((1 - core) * half, half), half), :] = other_ref[...]
        result[...] = contract_rows(mixed_ref[...], whole_ref[...]).astype(jnp.bfloat16)
        give_pieces(places_ref, result, pieces, piece)

    low = jax.ShapeDtypeStruct((piece, width), jnp.bfloat16)
    results = pl.pallas_call(
        kernel,
        in_specs=[pl.BlockSpec(memory_space=pltpu.SMEM)]
        + [pl.BlockSpec(memory_space=pltpu.VMEM)] * 3,
        out_specs=[pl.BlockSpec(memory_space=pltpu.VMEM)] * 5,
        out_shape=[low] * 4 + [jax.ShapeDtypeStruct((2 * half, width), jnp.bfloat16)],
        scratch_shapes=[pltpu.VMEM((local, width), jnp.bfloat16)],
        compiler_params=pltpu.CompilerParams(vmem_limit_bytes=VMEM_BYTES),
        cost_estimate=small_cost(),
        name="output_gradient",
    )(places, mixed, own, other)
    return results[:4], results[4]


def give_pieces(places_ref, result, pieces, rows):
    for side in range(2):
        bit = places_ref[1 + side]
        for n, place in enumerate((bit, 1 - bit)):
            start = pl.multiple_of((2 * side + place) * rows, rows)
            pieces[2 * side + n][...] = result[pl.ds(start, rows), :]


def attention_backward(grad_attn, w_output, queries, keys, values, cosine, sine):
    tokens, local = queries.shape
    half = tokens // 2
    heads = local // HD
    scale_factor = 1.0 / math.sqrt(HD)

    def kernel(
        ga_ref, wo_ref, query_ref, key_ref, value_ref, cos_ref, sin_ref, grad_ref, gk_ref, gv_ref, gm_ref
    ):
        gm_ref[...] = contract_cols(ga_ref[...], wo_ref[...]).astype(jnp.bfloat16)
        for block in range(2):
            rows = pl.ds(block * half, half)
            seen = pl.ds(0, (block + 1) * half)
            keys, values = key_ref[seen, :], value_ref[seen, :]
            cos, sin = cos_ref[rows, :], sin_ref[rows, :]
            grad_keys = jnp.zeros(((block + 1) * half, HD), jnp.float32)
            grad_values = grad_keys
            for head in range(heads):
                lanes = slice(head * HD, (head + 1) * HD)
                query, grad = query_ref[rows, lanes], gm_ref[rows, lanes]
                probs = softmax_rows(causal_scores(query, keys, block * half, scale_factor))
                grad_probs = contract_cols(grad, values)
                delta = jnp.sum(probs * grad_probs, axis=-1, keepdims=True)
                grad_scores = (probs * (grad_probs - delta)).astype(jnp.bfloat16)
                turned = dot(grad_scores, keys) * scale_factor
                grad_ref[rows, lanes] = (
                    turned * cos - pltpu.roll(turned, HD // 2, 1) * sin
                ).astype(jnp.bfloat16)
                grad_keys = grad_keys + contract_rows(grad_scores, query)
                grad_values = grad_values + contract_rows(probs.astype(jnp.bfloat16), grad)
            if block == 0:
                gk_ref[pl.ds(0, half), :] = grad_keys
                gv_ref[pl.ds(0, half), :] = grad_values
            else:
                first = pl.ds(0, half)
                gk_ref[first, :] = gk_ref[first, :] + grad_keys[:half]
                gv_ref[first, :] = gv_ref[first, :] + grad_values[:half]
                gk_ref[rows, :] = grad_keys[half:]
                gv_ref[rows, :] = grad_values[half:]
        turned = gk_ref[...] * scale_factor
        grad_ref[:, local : local + HD] = (
            turned * cos_ref[...] - pltpu.roll(turned, HD // 2, 1) * sin_ref[...]
        ).astype(jnp.bfloat16)
        grad_ref[:, local + HD :] = gv_ref[...].astype(jnp.bfloat16)

    return pl.pallas_call(
        kernel,
        out_shape=jax.ShapeDtypeStruct((tokens, local + 2 * HD), jnp.bfloat16),
        in_specs=[pl.BlockSpec(memory_space=pltpu.VMEM)] * 7,
        out_specs=pl.BlockSpec(memory_space=pltpu.VMEM),
        scratch_shapes=[pltpu.VMEM((tokens, HD), jnp.float32)] * 2
        + [pltpu.VMEM((tokens, local), jnp.bfloat16)],
        compiler_params=pltpu.CompilerParams(vmem_limit_bytes=VMEM_BYTES),
        cost_estimate=small_cost(
            flops=10 * 10**9, bytes_accessed=4 * 10**6, transcendentals=2 * 10**6
        ),
        name="attention_backward",
    )(grad_attn, w_output, queries, keys, values, cosine, sine)


def expert_weights_of(expert_ref, packs, half):
    start = 2 * half
    count = packs[0].shape[0] - start
    row_ids = lax.broadcasted_iota(jnp.int32, (count, 128), 0)
    lane_ids = lax.broadcasted_iota(jnp.int32, (count, 128), 1)
    pick = (row_ids == (expert_ref[0] ^ lane_ids)).astype(jnp.bfloat16)
    sides = []
    for ref in packs:
        coarse, fine = ref[start:, :half], ref[start:, half : 2 * half]
        sides.append(contract_rows(coarse, pick) + contract_rows(fine, pick))
    return jnp.concatenate(sides, axis=0)


def expert_terms(expert, joins, pieces, first, keep):
    sequences = [sequence for own, _ in joins for sequence in own]
    width = sequences[0][0].shape[1]
    half = sequences[0][0].shape[0] // 2 // 128 * 128
    number = len(pieces)
    arrays = [array for own in pieces for array, _ in own]
    columns = arrays[0].shape[-1]
    hidden = columns // 3
    tokens = 2 * half
    total = len(sequences)
    flat = [array for sequence in sequences for array in sequence]

    loads = []
    n = 0
    for own in pieces:
        loads.append([])
        place = 0
        for array, index in own:
            loads[-1].append((n, index, place, array.shape[-2]))
            place += array.shape[-2]
            n += 1
    copy_count = n

    def kernel(expert_ref, *refs):
        sources, refs = refs[: len(flat)], refs[len(flat) :]
        piece_refs, refs = refs[: len(arrays)], refs[len(arrays) :]
        results, (w_ref, packs, gate_all, semaphores) = refs[:-4], refs[-4:]
        e = pl.program_id(0)

        def copies_of(one):
            for which, index, place, rows in loads[one]:
                source = piece_refs[which] if index is None else piece_refs[which].at[index]
                yield pltpu.make_async_copy(
                    source, w_ref.at[one, pl.ds(place, rows), :], semaphores.at[which]
                )

        def kept(one):
            return pltpu.make_async_copy(
                w_ref.at[one], results[-1].at[one], semaphores.at[copy_count + one]
            )

        def pack_copy(n):
            return pltpu.make_async_copy(
                sources[n], packs.at[n], semaphores.at[copy_count + number + n]
            )

        @pl.when(e == 0)
        def _():
            for copy in copies_of(0):
                copy.start()
            for n in range(2 * total):
                pack_copy(n).start()
            for one in range(1, number):
                for copy in copies_of(one):
                    copy.start()

        for one in range(number):

            @pl.when(e == one)
            def _(one=one):
                for copy in copies_of(one):
                    copy.wait()
                if keep:
                    kept(one).start()

        lanes = lax.broadcasted_iota(jnp.int32, (half, 128), 1)
        n = 0
        for join, (own, start) in enumerate(joins):
            inner_ref, grad_ref = results[2 * join : 2 * join + 2]
            for s in range(len(own)):

                @pl.when(e == 0)
                def _(n=n):
                    for side in range(2):
                        pack_copy(2 * n + side).wait()
                    gate_all[n * tokens : (n + 1) * tokens, :] = expert_weights_of(
                        expert_ref, [packs.at[2 * n], packs.at[2 * n + 1]], half
                    )

                def run(n=n, s=s, inner_ref=inner_ref, grad_ref=grad_ref):
                    for side in range(2):
                        pack = packs.at[2 * n + side]
                        here = pl.ds(s * tokens + side * half, half)
                        gate = gate_all[n * tokens + side * half : n * tokens + (side + 1) * half, :]
                        weight = jnp.sum(
                            jnp.where(lanes == e + first, gate, 0.0), axis=1, keepdims=True
                        )
                        both = dot(pack[:half, :], w_ref[e, :, : 2 * hidden])
                        grad_inner = dot(pack[half : 2 * half, :], w_ref[e, :, 2 * hidden :]) * weight
                        gate_pre, up_pre = both[:, :hidden], both[:, hidden:]
                        sigmoid = jax.nn.sigmoid(gate_pre)
                        activated = gate_pre * sigmoid
                        grad_gate = (
                            grad_inner * up_pre * sigmoid * (1.0 + gate_pre * (1.0 - sigmoid))
                        )
                        grad_ref[here, :hidden] = grad_gate.astype(jnp.bfloat16)
                        grad_ref[here, hidden:] = (grad_inner * activated).astype(jnp.bfloat16)
                        inner_ref[here, :] = (activated * up_pre * weight).astype(jnp.bfloat16)

                if start:
                    pl.when(e >= start)(run)
                else:
                    run()
                n += 1

        if keep:

            @pl.when(e == number - 1)
            def _():
                for one in range(number):
                    kept(one).wait()

    out_specs, out_shape = [], []
    for own, start in joins:
        for size in (hidden, 2 * hidden):
            out_specs.append(
                pl.BlockSpec(
                    (len(own) * tokens, size), lambda e, start=start: (0, jnp.maximum(e - start, 0))
                )
            )
            out_shape.append(
                jax.ShapeDtypeStruct((len(own) * tokens, (number - start) * size), jnp.bfloat16)
            )
    if keep:
        out_specs.append(pl.BlockSpec(memory_space=pl.ANY))
        out_shape.append(jax.ShapeDtypeStruct((number, width, columns), jnp.bfloat16))
    results = pl.pallas_call(
        kernel,
        grid=(number,),
        in_specs=[pl.BlockSpec(memory_space=pltpu.SMEM)]
        + [pl.BlockSpec(memory_space=pl.ANY)] * (len(flat) + len(arrays)),
        out_specs=out_specs,
        out_shape=out_shape,
        scratch_shapes=[
            pltpu.VMEM((number, width, columns), jnp.bfloat16),
            pltpu.VMEM((2 * total, *flat[0].shape), jnp.bfloat16),
            pltpu.VMEM((total * tokens, 128), jnp.float32),
            pltpu.SemaphoreType.DMA((copy_count + number + 2 * total,)),
        ],
        compiler_params=pltpu.CompilerParams(vmem_limit_bytes=VMEM_BYTES),
        cost_estimate=small_cost(),
        name="expert_terms",
    )(expert, *flat, *arrays)
    terms = [tuple(results[2 * n : 2 * n + 2]) for n in range(len(joins))]
    return (*terms, results[-1]) if keep else tuple(terms)


def expert_sums(groups, weights, half):
    number, width = weights.shape[:2]
    hidden = weights.shape[2] // 3
    counts = [group[0][0].shape[0] // (2 * half) for group in groups]
    total = sum(counts)
    flat = [array for group in groups for part in group for array in part[:2]]
    block = 512

    def kernel(*refs):
        terms, refs = refs[: len(flat)], refs[len(flat) :]
        w_ref, back_own, back_other, out_own, out_other = refs
        n = place = 0
        for group, count in zip(groups, counts, strict=True):
            back = out = None
            for inner, _, start in group:
                for e in range(inner.shape[1] // hidden):
                    grad = terms[n + 1][:, 2 * e * hidden : 2 * (e + 1) * hidden]
                    one = contract_cols(grad, w_ref[start + e, :, : 2 * hidden])
                    back = one if back is None else back + one
                n += 2
            n -= 2 * len(group)
            for inner, _, start in group:
                for e in range(inner.shape[1] // hidden):
                    one = contract_cols(
                        terms[n][:, e * hidden : (e + 1) * hidden], w_ref[start + e, :, 2 * hidden :]
                    )
                    out = one if out is None else out + one
                n += 2
            for s in range(count):
                start = 2 * s * half
                back_own[place + s] = back[start : start + half].astype(jnp.bfloat16)
                back_other[place + s] = back[start + half : start + 2 * half].astype(jnp.bfloat16)
                out_own[place + s] = out[start : start + half].astype(jnp.bfloat16)
                out_other[place + s] = out[start + half : start + 2 * half].astype(jnp.bfloat16)
            place += count

    low = jax.ShapeDtypeStruct((total, half, width), jnp.bfloat16)
    return pl.pallas_call(
        kernel,
        grid=(width // block,),
        in_specs=[whole(*a.shape) for a in flat]
        + [pl.BlockSpec((number, block, 3 * hidden), lambda n: (0, n, 0))],
        out_specs=[pl.BlockSpec((total, half, block), lambda n: (0, 0, n))] * 4,
        out_shape=[low] * 4,
        compiler_params=pltpu.CompilerParams(vmem_limit_bytes=VMEM_BYTES),
        cost_estimate=small_cost(),
        name="expert_sums",
    )(*flat, weights)


def load_copies(sequence, half, sources, x_all, dy_all, semaphores, which=range(4)):
    for n in which:
        target = x_all if n < 2 else dy_all
        yield pltpu.make_async_copy(
            sources[2 * sequence + n % 2].at[pl.ds((n // 2) * half, half), :],
            target.at[pl.ds((2 * sequence + n % 2) * half, half), :],
            semaphores.at[4 * sequence + n],
        )


def expert_weight_grads(sequences, terms, number, hidden):
    width = sequences[0][0].shape[1]
    half = sequences[0][0].shape[0] // 2 // 128 * 128
    tokens = 2 * half
    flat = [array for sequence in sequences for array in sequence]
    total = len(sequences)
    quarter = width // 4
    per_load = 4 * total

    def kernel(*refs):
        sources, refs = refs[: len(flat)], refs[len(flat) :]
        term_refs, refs = refs[: 2 * len(terms)], refs[2 * len(terms) :]
        result_refs, refs = refs[: 4 * number], refs[4 * number :]
        x_all, dy_all, inner_all, grad_all, result, semaphores, term_semaphores, out_semaphores = refs

        def row_copies(of_gradients):
            for s in range(total):
                yield from load_copies(
                    s, half, sources, x_all, dy_all, semaphores, (2, 3) if of_gradients else (0, 1)
                )

        def term_copies(e, of_products):
            place = 0
            for n, (inner, _, start) in enumerate(terms):
                rows = inner.shape[0]
                size = 2 * hidden if of_products else hidden
                yield pltpu.make_async_copy(
                    term_refs[2 * n + of_products].at[:, pl.ds((start + e) * size, size)],
                    (grad_all if of_products else inner_all).at[e, pl.ds(place, rows), :],
                    term_semaphores.at[2 * len(terms) * e + 2 * n + of_products],
                )
                place += rows

        def out_copies(e):
            for q in range(4):
                yield pltpu.make_async_copy(
                    result.at[e, pl.ds(q * quarter, quarter), :],
                    result_refs[4 * e + q],
                    out_semaphores.at[4 * e + q],
                )

        first = [*row_copies(True), *term_copies(0, 0)]
        second = [*row_copies(False), *term_copies(0, 1)]
        later = [[*term_copies(e, 0), *term_copies(e, 1)] for e in range(1, number)]
        for copy in [*first, *second, *(copy for one in later for copy in one)]:
            copy.start()
        for e in range(number):
            for copy in first if e == 0 else later[e - 1]:
                copy.wait()
            result[e, :, 2 * hidden :] = contract_rows(dy_all[...], inner_all[e]).astype(jnp.bfloat16)
            if e == 0:
                for copy in second:
                    copy.wait()
            result[e, :, : 2 * hidden] = contract_rows(x_all[...], grad_all[e]).astype(jnp.bfloat16)
            for copy in out_copies(e):
                copy.start()
        for e in range(number):
            for copy in out_copies(e):
                copy.wait()

    anywhere = pl.BlockSpec(memory_space=pl.ANY)
    return pl.pallas_call(
        kernel,
        in_specs=[anywhere] * (len(flat) + 2 * len(terms)),
        out_specs=[anywhere] * (4 * number),
        scratch_shapes=[pltpu.VMEM((total * tokens, width), jnp.bfloat16)] * 2
        + [
            pltpu.VMEM((number, total * tokens, hidden), jnp.bfloat16),
            pltpu.VMEM((number, total * tokens, 2 * hidden), jnp.bfloat16),
            pltpu.VMEM((number, width, 3 * hidden), jnp.bfloat16),
            pltpu.SemaphoreType.DMA((per_load,)),
            pltpu.SemaphoreType.DMA((2 * len(terms) * number,)),
            pltpu.SemaphoreType.DMA((4 * number,)),
        ],
        out_shape=[jax.ShapeDtypeStruct((quarter, 3 * hidden), jnp.bfloat16)] * (4 * number),
        compiler_params=pltpu.CompilerParams(vmem_limit_bytes=VMEM_BYTES),
        cost_estimate=small_cost(),
        name="expert_weight_grads",
    )(*flat, *(array for term in terms for array in term[:2]))


def own_weight_grads(sequences, terms, arrived, hidden):
    width = sequences[0][0].shape[1]
    half = sequences[0][0].shape[0] // 2 // 128 * 128
    tokens = 2 * half
    counts = [pair[0].shape[0] // tokens for pair in terms]
    flat = [array for sequence in sequences for array in sequence]
    total = len(sequences)
    quarter = width // 4

    def kernel(*refs):
        sources, refs = refs[: len(flat)], refs[len(flat) :]
        term_refs, refs = refs[: 2 * len(counts)], refs[2 * len(counts) :]
        arrived_refs, refs = refs[:6], refs[6:]
        gate_ref, up_ref, down_ref, x_all, dy_all, semaphores = refs
        for s in range(total):
            for copy in load_copies(s, half, sources, x_all, dy_all, semaphores):
                copy.start()
        gate_up = down = None
        first = 0
        for joined, count in enumerate(counts):
            for s in range(first, first + count):
                for copy in load_copies(s, half, sources, x_all, dy_all, semaphores):
                    copy.wait()
            span = pl.ds(first * tokens, count * tokens)
            one = contract_rows(x_all[span, :], term_refs[2 * joined + 1][...])
            two = contract_rows(term_refs[2 * joined][...], dy_all[span, :])
            gate_up = one if gate_up is None else gate_up + one
            down = two if down is None else down + two
            first += count
        for q in range(4):
            rows = slice(q * quarter, (q + 1) * quarter)
            inside = slice(q % 2 * quarter, (q % 2 + 1) * quarter)
            more = arrived_refs[q][...].astype(jnp.float32) + arrived_refs[4 + q // 2][
                inside, :
            ].astype(jnp.float32)
            both = gate_up[rows] + more[:, : 2 * hidden]
            gate_ref[0, rows, :] = both[:, :hidden]
            up_ref[0, rows, :] = both[:, hidden:]
            down_ref[0, :, rows] = down[:, rows] + more[:, 2 * hidden :].T

    def beside(count, columns):
        return pl.BlockSpec((count * tokens, columns), lambda e: (0, 0))

    tall = jax.ShapeDtypeStruct((1, width, hidden), jnp.float32)
    flat_down = jax.ShapeDtypeStruct((1, hidden, width), jnp.float32)
    return pl.pallas_call(
        kernel,
        grid=(1,),
        in_specs=[pl.BlockSpec(memory_space=pl.ANY)] * len(flat)
        + [beside(count, columns) for count in counts for columns in (hidden, 2 * hidden)]
        + [whole(quarter, 3 * hidden)] * 4
        + [whole(2 * quarter, 3 * hidden)] * 2,
        out_specs=[whole(*tall.shape), whole(*tall.shape), whole(*flat_down.shape)],
        scratch_shapes=[pltpu.VMEM((total * tokens, width), jnp.bfloat16)] * 2
        + [pltpu.SemaphoreType.DMA((4 * total,))],
        out_shape=[tall, tall, flat_down],
        compiler_params=pltpu.CompilerParams(vmem_limit_bytes=VMEM_BYTES),
        cost_estimate=small_cost(),
        name="own_weight_grads",
    )(*flat, *(array for pair in terms for array in pair), *arrived)


def planes_of_four(
    hidden_in,
    attn_gain,
    w_query,
    w_key,
    w_value,
    w_output,
    moe_gain,
    w_gate,
    w_up,
    w_down,
    gate_logits,
    routes,
    out_grad,
):
    tokens, width = hidden_in.shape
    half = tokens // 2
    experts = lax.axis_size("expert")
    columns = [[4 * z + r for z in range(4)] for r in range(4)]
    core = lax.axis_index("tensor")
    expert = lax.axis_index("expert")
    plane = expert // 4
    bit_x = expert % 2
    bit_y = (expert // 2) % 2
    hidden = w_down.shape[1]
    together = lax.optimization_barrier

    own_weights = jnp.concatenate([w_gate[0], w_up[0], w_down[0].T], axis=1)
    quarter = width // 4
    pieces = [own_weights[:quarter], own_weights[quarter : 2 * quarter], own_weights[2 * quarter :]]
    gate_weights = jax.nn.softmax(gate_logits, axis=-1)
    names = jnp.arange(experts, dtype=jnp.int32)
    dense = jnp.sum(
        jnp.where(routes.T[:, None, :] == names[None, :, None], gate_weights.T[:, None, :], 0.0),
        axis=0,
    )
    dense = lax.dynamic_slice_in_dim(dense, core * half, half, 1)
    coarse = dense.astype(jnp.bfloat16)
    fine = (dense - coarse.astype(jnp.float32)).astype(jnp.bfloat16)
    extra = jnp.pad(jnp.concatenate([coarse, fine], axis=1), ((0, 0), (0, width - 2 * half)))
    out_grad_half = part(out_grad, core, 2)
    dy_own = jnp.concatenate([out_grad_half, extra], axis=0)

    x0, y0 = flip(pieces[0], 1), flip(pieces[0], 2)
    dy_up_one, dy_down_one = climb(dy_own), descend(dy_own)
    cosine, sine = (jnp.asarray(table) for table in rotary_tables(tokens))
    normed, queries, keys, values, mixed, keep, send = attention_forward(
        core.reshape(1), hidden_in, attn_gain[None], w_query, w_key, w_value, w_output, cosine, sine
    )
    send, x0, y0, dy_up_one, dy_down_one, piece = together(
        (send, x0, y0, dy_up_one, dy_down_one, pieces[1])
    )
    x1, y1 = flip(piece, 1), flip(piece, 2)
    middle = keep + swap(send).astype(jnp.float32)
    scale_two = lax.rsqrt(jnp.mean(middle * middle, axis=-1, keepdims=True) + epsilon)
    unit_two = middle * scale_two
    rows_in = (unit_two * moe_gain).astype(jnp.bfloat16)
    up_one, down_one = climb(rows_in), descend(rows_in)
    x1, y1, up_one, down_one, dy_up_one, dy_down_one, piece = together(
        (x1, y1, up_one, down_one, dy_up_one, dy_down_one, pieces[2])
    )
    up_one = jnp.concatenate([up_one, dy_up_one], axis=0)
    down_one = jnp.concatenate([down_one, dy_down_one], axis=0)
    up_one, down_one, piece = together((up_one, down_one, piece))
    x2, y2 = flip(piece, 1), flip(piece, 2)
    up_two, down_two = climb(up_one), descend(down_one)
    own = jnp.concatenate([rows_in, dy_own], axis=0)
    first = jnp.where(plane == 0, down_one, up_one)
    own, first = (own, swap(own)), (first, swap(first))
    far_from_y = jnp.concatenate([y0, y1], axis=0)
    x2, y2, up_two, down_two, own, first, far_from_y = together(
        (x2, y2, up_two, down_two, own, first, far_from_y)
    )
    far_weights = [flip(far_from_y, 1), flip(x2, 2)]
    up_three, down_three = climb(up_two), descend(down_two)
    number = expert.reshape(1)
    second = jnp.where(plane == 0, down_two, jnp.where(plane == 3, up_two, down_one))
    second = (second, swap(second))
    near_pieces = [[own_weights], [x0, x1, x2], [y0, y1, y2]]
    near_early, near_second, near_weights = expert_terms(
        number,
        [([own, first], 0), ([second], 0)],
        [[(piece, None) for piece in one] for one in near_pieces],
        0,
        True,
    )
    far_weights, up_three, down_three, near_early, near_second, second = together(
        (far_weights, up_three, down_three, near_early, near_second, second)
    )
    third = jnp.where(
        plane == 0,
        down_three,
        jnp.where(plane == 1, down_two, jnp.where(plane == 2, up_two, up_three)),
    )
    third = (third, swap(third))
    far_pieces = [(piece, None) for piece in far_weights]
    all_third, far_second, far_early, weights = expert_terms(
        number,
        [([third], 0), ([second], 3), ([own, first], 3)],
        [[(near_weights, 0)], [(near_weights, 1)], [(near_weights, 2)], far_pieces],
        0,
        True,
    )
    to_far = expert_weight_grads(
        [third, second, own, first], [(*all_third, 3), (*far_second, 0), (*far_early, 0)], 1, hidden
    )
    over_x, over_y = [flip(to_far[0], 1)], [flip(to_far[2], 2)]
    to_far, near_second, far_second = together((to_far, near_second, far_second))
    late_sums = expert_sums(
        [[(*all_third, 0)], [(*near_second, 0), (*far_second, 3)]], weights, half
    )
    late_sums, over_x, over_y, to_far = together((late_sums, over_x, over_y, to_far))
    back_late = add_low(late_sums[0], swap(late_sums[1]))
    back_late, near_early, all_third = together((back_late, near_early, all_third))
    second_back, third_back = back_late[1], back_late[0]

    falling, rising = descend(third_back), climb(third_back)
    over_x, over_y = over_x + [flip(to_far[1], 1)], over_y + [flip(to_far[3], 2)]
    beside = expert_weight_grads(
        [own, first, second, third],
        [(*near_early, 1), (*near_second, 1), (*all_third, 1)],
        2,
        hidden,
    )
    falling, rising, beside, over_x, over_y, far_early = together(
        (falling, rising, beside, over_x, over_y, far_early)
    )
    to_x, to_y = beside[:4], beside[4:]
    falling = add_low(jnp.where(plane == 3, second_back, third_back), falling)
    rising = add_low(jnp.where(plane == 0, second_back, third_back), rising)
    falling, rising, far_early = together((falling, rising, far_early))
    falling, rising = descend(falling), climb(rising)
    from_x, from_y = [flip(to_x[0], 1)], [flip(to_y[2], 2)]
    early_sums = expert_sums([[(*near_early, 0), (*far_early, 3)]], weights, half)
    falling, rising, early_sums, from_x, from_y, to_x, to_y = together(
        (falling, rising, early_sums, from_x, from_y, to_x, to_y)
    )
    back_early = add_low(early_sums[0], swap(early_sums[1]))
    own_back, first_back = back_early[0], back_early[1]
    falling = add_low(first_back, falling)
    rising = add_low(jnp.where(plane == 0, first_back, second_back), rising)
    falling, rising, early_sums, late_sums, over_x = together(
        (falling, rising, early_sums, late_sums, over_x)
    )
    falling, rising = descend(falling), climb(rising)
    from_x, from_y = from_x + [flip(to_x[1], 1)], from_y + [flip(to_y[3], 2)]
    with_x = jnp.concatenate([add_low(to_y[n], over_x[n]) for n in range(2)], axis=0)
    with_y = jnp.concatenate([add_low(to_x[2 + n], over_y[n]) for n in range(2)], axis=0)
    out_late = add_low(late_sums[2], swap(late_sums[3]))
    out_early = add_low(early_sums[2], swap(early_sums[3]))
    own_out, first_out, second_out, third_out = out_early[0], out_early[1], out_late[1], out_late[0]
    by_plane = [
        jnp.where(plane == 0, own_out, jnp.where(plane == 1, first_out, third_out)),
        jnp.where(plane == 1, own_out, jnp.where(plane == 3, second_out, first_out)),
        jnp.where(plane == 2, own_out, jnp.where(plane == 3, first_out, second_out)),
        jnp.where(plane == 3, own_out, jnp.where(plane == 2, second_out, third_out)),
    ]
    results = jnp.concatenate(by_plane, axis=0)
    falling, rising, results, from_x, from_y, with_x, with_y = together(
        (falling, rising, results, from_x, from_y, with_x, with_y)
    )
    moe_result = lax.psum_scatter(
        results, "expert", axis_index_groups=columns, scatter_dimension=0, tiled=True
    )
    grad_rows = (
        own_back.astype(jnp.float32) + falling.astype(jnp.float32) + rising.astype(jnp.float32)
    )
    grad_out = out_grad_half.astype(jnp.float32)
    grad_unit_two = grad_rows * moe_gain
    grad_moe_gain = jnp.sum(grad_rows * unit_two, axis=0)
    grad_middle = grad_out + scale_two * (
        grad_unit_two - unit_two * jnp.mean(grad_unit_two * unit_two, axis=-1, keepdims=True)
    )
    grad_attn_half = grad_middle.astype(jnp.bfloat16)
    places = jnp.stack([core, bit_x, bit_y])
    output_pieces, grad_attn = output_gradient(places, mixed, grad_attn_half, swap(grad_attn_half))
    output_pieces, grad_attn = together((output_pieces, grad_attn))
    left, to_x_side, right, to_y_side = output_pieces
    output_parts = add_low(left, flip(to_x_side, 1)), add_low(right, flip(to_y_side, 2))
    grad_all_pre = attention_backward(grad_attn, w_output, queries, keys, values, cosine, sine)
    grad_all_pre, output_parts = together((grad_all_pre, output_parts))
    grad_projections = contract_rows(normed, grad_all_pre).astype(jnp.bfloat16)
    output_parts = plane_scatter_second(output_parts, bit_x, bit_y)
    grad_projections, output_parts = together((grad_projections, output_parts))
    projection_parts = plane_scatter_first(grad_projections, bit_x, bit_y)
    w_all = jnp.concatenate([w_query, w_key, w_value], axis=1)
    grad_normed_part = contract_cols(grad_all_pre, w_all).astype(jnp.bfloat16)
    grad_normed = part(grad_normed_part, core, 2).astype(jnp.float32) + swap(
        part(grad_normed_part, 1 - core, 2)
    ).astype(jnp.float32)
    source_half = part(hidden_in, core, 2).astype(jnp.float32)
    scale_half = lax.rsqrt(jnp.mean(source_half * source_half, axis=-1, keepdims=True) + epsilon)
    unit_half = source_half * scale_half
    grad_unit_one = grad_normed * attn_gain
    grad_attn_gain = jnp.sum(grad_normed * unit_half, axis=0)
    grad_in_half = grad_middle + scale_half * (
        grad_unit_one - unit_half * jnp.mean(grad_unit_one * unit_half, axis=-1, keepdims=True)
    )
    gains = jnp.stack([grad_attn_gain, grad_moe_gain])
    projection_parts, gains, grad_in_half = together((projection_parts, gains, grad_in_half))
    projection_parts = plane_scatter_second(projection_parts, bit_x, bit_y)
    gains = (gains + swap(gains)).reshape(-1, grad_projections.shape[1])
    gain_rows = gains.shape[0]
    gains = jnp.pad(gains, ((0, 16 - gain_rows), (0, 0))).astype(jnp.bfloat16)
    grad_in_other = swap(grad_in_half)
    output_both = jnp.concatenate(output_parts, axis=0)
    projection_both = jnp.concatenate([*projection_parts, gains], axis=0)
    projection_both, output_both, moe_result, with_x, with_y = together(
        (projection_both, output_both, moe_result, with_x, with_y)
    )
    output_both, projection_both = lax.psum(
        (output_both, projection_both), "expert", axis_index_groups=columns
    )
    block_half = (middle + moe_result.astype(jnp.float32)).astype(jnp.bfloat16)
    block_out = ordered(block_half, swap(block_half), core)
    then_y, then_x = flip(with_x, 2), flip(with_y, 1)
    output_both, projection_both, block_out, then_x, then_y = together(
        (output_both, projection_both, block_out, then_x, then_y)
    )
    gains, projection_both = projection_both[-16:].astype(jnp.float32), projection_both[:-16]
    output_halves = plane_gather_first(*jnp.split(output_both, 2), bit_x, bit_y)
    projection_halves = plane_gather_first(*jnp.split(projection_both, 2), bit_x, bit_y)
    output_halves, projection_halves, gains, then_x, then_y, grad_in_half, grad_in_other = together(
        (output_halves, projection_halves, gains, then_x, then_y, grad_in_half, grad_in_other)
    )
    arrived = (*from_x, *from_y, then_y, then_x)
    expert_grads = own_weight_grads(
        [own, first, second, third], [near_early, near_second, all_third], arrived, hidden
    )
    grad_in = ordered(grad_in_half, grad_in_other, core)
    bits = jnp.stack([bit_x, bit_y])
    projection_widths = [w.shape[1] for w in (w_query, w_key, w_value)]
    output_early = lay_out(bits, output_halves, (width,), False)
    projections_early = lay_out(bits, projection_halves, projection_widths, False)
    output_pieces = plane_gather_second(*output_halves)
    projection_pieces = plane_gather_second(*projection_halves)
    early_ones = (output_early, projections_early, grad_in)
    expert_grads, output_pieces, projection_pieces, gains, early_ones = together(
        (expert_grads, output_pieces, projection_pieces, gains, early_ones)
    )
    output_early, projections_early, grad_in = early_ones
    gains = (gains + flip(gains, 1)) + (flip(gains, 2) + flip(gains, 3))
    gains_sum = gains[:gain_rows].reshape(2, width)
    grad_gate, grad_up, grad_down = expert_grads
    projections = lay_out(bits, projection_pieces, projection_widths, True, projections_early)
    (output_sum,) = lay_out(bits, output_pieces, (width,), True, output_early)
    return (
        block_out,
        grad_in,
        gains_sum[0],
        *projections,
        output_sum,
        gains_sum[1],
        grad_gate,
        grad_up,
        grad_down,
    )


def solution(mesh):
    on_device = planes_of_four if mesh.shape["expert"] == 16 else routed_slots
    return jax.shard_map(
        on_device,
        mesh=mesh,
        in_specs=(
            P("expert", None),
            P(),
            P(None, "tensor"),
            P(None, "tensor"),
            P(None, "tensor"),
            P("tensor", None),
            P(),
            P("expert", None, "tensor"),
            P("expert", None, "tensor"),
            P("expert", "tensor", None),
            P("expert", None),
            P("expert", None),
            P("expert", None),
        ),
        out_specs=(
            P("expert", None),
            P("expert", None),
            P(),
            P(None, "tensor"),
            P(None, "tensor"),
            P(None, "tensor"),
            P("tensor", None),
            P(),
            P("expert", None, "tensor"),
            P("expert", None, "tensor"),
            P("expert", "tensor", None),
        ),
        check_vma=False,
    )
```

```python
import math

import jax
import jax.numpy as jnp
import numpy as np
from jax import lax
from jax.experimental import pallas as pl
from jax.experimental.pallas import tpu as pltpu
from jax.sharding import PartitionSpec as P

HD = 128


epsilon = 1e-06
rope_base = 10000.0
masked_score = -1e30


def rotate(values, places, sign):
    halfway = values.shape[-1] // 2
    frequency = rope_base ** (-jnp.arange(halfway, dtype=jnp.float32) / halfway)
    angles = places.astype(jnp.float32)[:, None] * frequency[None, :]
    cosine = jnp.cos(angles)[:, None, :]
    sine = sign * jnp.sin(angles)[:, None, :]
    first = values[..., :halfway]
    second = values[..., halfway:]
    return jnp.concatenate(
        [first * cosine - second * sine, second * cosine + first * sine], axis=-1
    )


def contract_rows(left, right):
    return lax.dot_general(
        left, right, (((0,), (0,)), ((), ())), preferred_element_type=jnp.float32
    )


def contract_cols(left, right):
    return lax.dot_general(
        left, right, (((1,), (1,)), ((), ())), preferred_element_type=jnp.float32
    )


def block_scores(query_block, keys_used, row_start, scale_factor):
    query_rows = query_block.shape[0]
    key_rows = keys_used.shape[0]
    raw_scores = (
        jnp.einsum("qcgd,kcd->cgqk", query_block, keys_used, preferred_element_type=jnp.float32)
        * scale_factor
    )
    row_ids = row_start + jnp.arange(query_rows)
    causal = jnp.arange(key_rows)[None, :] <= row_ids[:, None]
    return jnp.where(causal, raw_scores, masked_score)


def routed_slots(
    hidden_in,
    attn_gain,
    w_query,
    w_key,
    w_value,
    w_output,
    moe_gain,
    w_gate,
    w_up,
    w_down,
    gate_logits,
    routes,
    out_grad,
):
    tokens, model_width = hidden_in.shape
    experts = lax.axis_size("expert")
    tensor_ranks = lax.axis_size("tensor")
    tensor_rank = lax.axis_index("tensor")
    route_width = routes.shape[1]
    route_count = tokens * route_width
    capacity = 2 * route_count // experts
    half_slots = capacity // tensor_ranks
    heads_local = w_query.shape[1] // HD
    kv_local = w_key.shape[1] // HD
    groups = heads_local // kv_local
    scale_factor = 1.0 / math.sqrt(HD)
    block_rows = min(512, tokens)
    places = jnp.arange(tokens, dtype=jnp.int32)
    flat_routes = routes.reshape(-1)
    route_hits = (flat_routes[:, None] == jnp.arange(experts, dtype=jnp.int32)[None, :]).astype(
        jnp.int32
    )
    slot_index = jnp.sum(jnp.cumsum(route_hits, axis=0) * route_hits, axis=1) - 1
    which_route = (
        jnp.full((experts * capacity,), route_count, jnp.int32)
        .at[flat_routes * capacity + slot_index]
        .set(jnp.arange(route_count, dtype=jnp.int32))
    )
    which_token = which_route // route_width
    own_half = slot_index // half_slots == tensor_rank
    back_index = jnp.where(
        own_half, flat_routes * half_slots + slot_index % half_slots, experts * half_slots
    )
    gate_weights = jax.nn.softmax(gate_logits, axis=-1)
    full_gate, full_up, full_down = (w_gate[0], w_up[0], w_down[0])

    def deliver(buffer):
        arrived_all = lax.all_to_all(buffer, "expert", split_axis=0, concat_axis=0, tiled=True)
        return arrived_all.reshape(experts * capacity, model_width)

    def give_back(partial_value):
        summed_rows = lax.psum_scatter(
            partial_value.reshape(experts, capacity, model_width).astype(jnp.bfloat16),
            "tensor",
            scatter_dimension=1,
            tiled=True,
        )
        returned = lax.all_to_all(summed_rows, "expert", split_axis=0, concat_axis=0, tiled=True)
        return jnp.concatenate(
            [
                returned.reshape(experts * half_slots, model_width),
                jnp.zeros((1, model_width), jnp.bfloat16),
            ],
            axis=0,
        )

    def collect(returned, weights):
        picked = returned[back_index].astype(jnp.float32).reshape(tokens, route_width, model_width)
        return lax.psum(
            jnp.sum(picked * weights[:, :, None], axis=1).astype(jnp.bfloat16), "tensor"
        ).astype(jnp.float32)

    source = hidden_in.astype(jnp.float32)
    scale_one = lax.rsqrt(jnp.mean(source * source, axis=-1, keepdims=True) + epsilon)
    unit_one = source * scale_one
    normed = (unit_one * attn_gain).astype(jnp.bfloat16)
    query_pre = jnp.dot(normed, w_query, preferred_element_type=jnp.float32).reshape(
        tokens, heads_local, HD
    )
    queries = (
        rotate(query_pre, places, 1.0).astype(jnp.bfloat16).reshape(tokens, kv_local, groups, HD)
    )
    key_pre = jnp.dot(normed, w_key, preferred_element_type=jnp.float32).reshape(
        tokens, kv_local, HD
    )
    keys_used = rotate(key_pre, places, 1.0).astype(jnp.bfloat16)
    values_used = (
        jnp.dot(normed, w_value, preferred_element_type=jnp.float32)
        .astype(jnp.bfloat16)
        .reshape(tokens, kv_local, HD)
    )
    row_start = 0
    query_block = queries
    raw_scores = block_scores(query_block, keys_used, row_start, scale_factor)
    biggest = jnp.max(raw_scores, axis=-1, keepdims=True)
    exponent = jnp.exp(raw_scores - biggest)
    row_total = jnp.sum(exponent, axis=-1, keepdims=True)
    weights_low = (exponent / row_total).astype(jnp.bfloat16)
    logsums = [biggest + jnp.log(row_total)]
    attended = jnp.einsum(
        "cgqk,kcd->qcgd", weights_low, values_used, preferred_element_type=jnp.float32
    )
    mixed_blocks = attended.reshape(block_rows, heads_local * HD).astype(jnp.bfloat16)
    attn_part = jnp.dot(mixed_blocks, w_output, preferred_element_type=jnp.float32)
    middle = source + lax.psum(attn_part.astype(jnp.bfloat16), "tensor").astype(jnp.float32)
    scale_two = lax.rsqrt(jnp.mean(middle * middle, axis=-1, keepdims=True) + epsilon)
    unit_two = middle * scale_two
    rows_in = (unit_two * moe_gain).astype(jnp.bfloat16)
    padded_rows = jnp.concatenate([rows_in, jnp.zeros((1, model_width), jnp.bfloat16)], axis=0)
    arrived = deliver(padded_rows[which_token].reshape(experts, capacity, model_width))
    gate_pre = jnp.dot(arrived, full_gate, preferred_element_type=jnp.float32)
    up_pre = jnp.dot(arrived, full_up, preferred_element_type=jnp.float32)
    sigmoid = jax.nn.sigmoid(gate_pre)
    activated = gate_pre * sigmoid
    hidden_units = (activated * up_pre).astype(jnp.bfloat16)
    produced = jnp.dot(hidden_units, full_down, preferred_element_type=jnp.float32)
    moe_result = collect(give_back(produced), gate_weights)
    block_out = (middle + moe_result).astype(jnp.bfloat16)
    grad_out = out_grad.astype(jnp.float32)
    route_grads = (
        (gate_weights[:, :, None] * grad_out[:, None, :])
        .astype(jnp.bfloat16)
        .reshape(route_count, model_width)
    )
    padded_grads = jnp.concatenate([route_grads, jnp.zeros((1, model_width), jnp.bfloat16)], axis=0)
    grad_arrived = deliver(padded_grads[which_route].reshape(experts, capacity, model_width))
    grad_down = contract_rows(hidden_units, grad_arrived)
    grad_inner = contract_cols(grad_arrived, full_down)
    grad_gate_pre = (grad_inner * up_pre * sigmoid * (1.0 + gate_pre * (1.0 - sigmoid))).astype(
        jnp.bfloat16
    )
    grad_up_pre = (grad_inner * activated).astype(jnp.bfloat16)
    grad_gate = contract_rows(arrived, grad_gate_pre)
    grad_up = contract_rows(arrived, grad_up_pre)
    grad_arrived_rows = contract_cols(grad_gate_pre, full_gate) + contract_cols(
        grad_up_pre, full_up
    )
    grad_rows = collect(give_back(grad_arrived_rows), jnp.ones_like(gate_weights))
    grad_unit_two = grad_rows * moe_gain
    grad_moe_gain = jnp.sum(grad_rows * unit_two, axis=0)
    grad_middle = grad_out + scale_two * (
        grad_unit_two - unit_two * jnp.mean(grad_unit_two * unit_two, axis=-1, keepdims=True)
    )
    grad_attn = grad_middle.astype(jnp.bfloat16)
    grad_output = contract_rows(mixed_blocks, grad_attn)
    grad_mixed = (
        contract_cols(grad_attn, w_output)
        .astype(jnp.bfloat16)
        .reshape(tokens, kv_local, groups, HD)
    )
    grad_query_blocks = []
    grad_keys = jnp.zeros((tokens, kv_local, HD), jnp.float32)
    grad_values = jnp.zeros((tokens, kv_local, HD), jnp.float32)
    for block_number, row_start in enumerate(range(0, tokens, block_rows)):
        query_block = queries
        raw_scores = block_scores(query_block, keys_used, row_start, scale_factor)
        probs = jnp.exp(raw_scores - logsums[block_number])
        probs_low = probs.astype(jnp.bfloat16)
        grad_probs = jnp.einsum(
            "qcgd,kcd->cgqk", grad_mixed, values_used, preferred_element_type=jnp.float32
        )
        delta = jnp.sum(probs * grad_probs, axis=-1, keepdims=True)
        grad_scores = (probs * (grad_probs - delta)).astype(jnp.bfloat16)
        grad_query_blocks.append(
            jnp.einsum("cgqk,kcd->qcgd", grad_scores, keys_used, preferred_element_type=jnp.float32)
            * scale_factor
        )
        grad_keys = (
            jnp.einsum(
                "cgqk,qcgd->kcd", grad_scores, query_block, preferred_element_type=jnp.float32
            )
            * scale_factor
        )
        grad_values = jnp.einsum(
            "cgqk,qcgd->kcd", probs_low, grad_mixed, preferred_element_type=jnp.float32
        )
    grad_queries = grad_query_blocks[0].reshape(tokens, heads_local, HD)
    grad_query_pre = (
        rotate(grad_queries, places, -1.0).astype(jnp.bfloat16).reshape(tokens, heads_local * HD)
    )
    grad_key_pre = (
        rotate(grad_keys, places, -1.0).astype(jnp.bfloat16).reshape(tokens, kv_local * HD)
    )
    grad_value_pre = grad_values.astype(jnp.bfloat16).reshape(tokens, kv_local * HD)
    grad_query = contract_rows(normed, grad_query_pre)
    grad_key = contract_rows(normed, grad_key_pre)
    grad_value = contract_rows(normed, grad_value_pre)
    grad_normed_part = (
        contract_cols(grad_query_pre, w_query)
        + contract_cols(grad_key_pre, w_key)
        + contract_cols(grad_value_pre, w_value)
    )
    grad_normed = lax.psum(grad_normed_part.astype(jnp.bfloat16), "tensor").astype(jnp.float32)
    grad_unit_one = grad_normed * attn_gain
    grad_attn_gain = jnp.sum(grad_normed * unit_one, axis=0)
    grad_in = grad_middle + scale_one * (
        grad_unit_one - unit_one * jnp.mean(grad_unit_one * unit_one, axis=-1, keepdims=True)
    )
    summed = lax.psum(
        (grad_query, grad_key, grad_value, grad_output, grad_attn_gain, grad_moe_gain), "expert"
    )
    return (
        block_out,
        grad_in,
        summed[4],
        summed[0],
        summed[1],
        summed[2],
        summed[3],
        summed[5],
        grad_gate[None],
        grad_up[None],
        grad_down[None],
    )


VMEM_BYTES = 60 * 2**20


def small_cost(**_):
    return pl.CostEstimate(flops=1000, bytes_accessed=1000, transcendentals=0)


def dot(left, right):
    return jnp.dot(left, right, preferred_element_type=jnp.float32)


def whole(*shape):
    return pl.BlockSpec(shape, lambda *_: (0,) * len(shape), pipeline_mode=pl.Buffered(1))


def swap(value):
    return lax.ppermute(value, "tensor", [(0, 1), (1, 0)])


def flip(value, bit):
    places = lax.axis_size("expert")
    return lax.ppermute(value, "expert", [(i, i ^ bit) for i in range(places)])


def outer(value):
    return flip(value, 4)


def inner(value):
    places = lax.axis_size("expert")
    return lax.ppermute(value, "expert", [(i, i ^ 12 if i // 4 in (1, 2) else i) for i in range(places)])


def part(value, index, count):
    size = value.shape[0] // count
    return lax.dynamic_slice_in_dim(value, index * size, size, 0)


def ordered(own, other, place):
    return jnp.where(
        place == 0,
        jnp.concatenate([own, other], axis=0),
        jnp.concatenate([other, own], axis=0),
    )


def add_low(kept, arrived):
    return (kept.astype(jnp.float32) + arrived.astype(jnp.float32)).astype(jnp.bfloat16)


def plane_scatter_first(value, bit_x, bit_y):
    left, right = jnp.split(value, 2, axis=0)
    left = add_low(part(left, bit_x, 2), flip(part(left, 1 - bit_x, 2), 1))
    right = add_low(part(right, bit_y, 2), flip(part(right, 1 - bit_y, 2), 2))
    return left, right


def plane_scatter_second(halves, bit_x, bit_y):
    left, right = halves
    left = add_low(part(left, bit_y, 2), flip(part(left, 1 - bit_y, 2), 2))
    right = add_low(part(right, bit_x, 2), flip(part(right, 1 - bit_x, 2), 1))
    return left, right


def plane_gather_first(left, right, bit_x, bit_y):
    return ordered(left, flip(left, 2), bit_y), ordered(right, flip(right, 1), bit_x)


def plane_gather_second(left, right):
    return flip(left, 1), flip(right, 2)


def lay_out(bits, halves, widths, arrived, earlier=()):
    rows, columns = halves[0].shape

    def kernel(bits_ref, *refs):
        sources, refs = refs[:2], refs[2 + len(earlier) :]
        results, (wide, semaphores) = refs[: len(widths)], refs[len(widths) :]
        copies = []
        for side in range(2):
            wide[side] = sources[side][...].astype(jnp.float32)
            bit = bits_ref[side]
            place = pl.multiple_of((2 * side + (1 - bit if arrived else bit)) * rows, rows)
            start = 0
            for n, (result, size) in enumerate(zip(results, widths, strict=True)):
                copies.append(
                    pltpu.make_async_copy(
                        wide.at[side, :, pl.ds(start, size)],
                        result.at[pl.ds(place, rows), :],
                        semaphores.at[side, n],
                    )
                )
                copies[-1].start()
                start += size
        for copy in copies:
            copy.wait()

    anywhere = pl.BlockSpec(memory_space=pl.ANY)
    return pl.pallas_call(
        kernel,
        in_specs=[pl.BlockSpec(memory_space=pltpu.SMEM)]
        + [pl.BlockSpec(memory_space=pltpu.VMEM)] * 2
        + [anywhere] * len(earlier),
        out_specs=[anywhere] * len(widths),
        out_shape=[jax.ShapeDtypeStruct((4 * rows, size), jnp.float32) for size in widths],
        scratch_shapes=[
            pltpu.VMEM((2, rows, columns), jnp.float32),
            pltpu.SemaphoreType.DMA((2, len(widths))),
        ],
        input_output_aliases={3 + n: n for n in range(len(earlier))},
        compiler_params=pltpu.CompilerParams(vmem_limit_bytes=VMEM_BYTES),
        cost_estimate=small_cost(),
        name="lay_out",
    )(bits, *halves, *earlier)


def rotary_tables(tokens):
    halfway = HD // 2
    frequency = rope_base ** (-np.arange(halfway, dtype=np.float64) / halfway)
    angles = np.arange(tokens)[:, None] * frequency[None, :]
    cosine, sine = np.cos(angles), np.sin(angles)
    return (
        np.concatenate([cosine, cosine], axis=1).astype(np.float32),
        np.concatenate([-sine, sine], axis=1).astype(np.float32),
    )


def causal_scores(query_block, keys, row_start, scale_factor):
    raw = contract_cols(query_block, keys) * scale_factor
    row_ids = row_start + lax.broadcasted_iota(jnp.int32, raw.shape, 0)
    return jnp.where(lax.broadcasted_iota(jnp.int32, raw.shape, 1) <= row_ids, raw, masked_score)


def softmax_rows(raw):
    exponent = jnp.exp(raw - jnp.max(raw, axis=-1, keepdims=True))
    return exponent / jnp.sum(exponent, axis=-1, keepdims=True)


def attention_forward(core, hidden, gain, w_query, w_key, w_value, w_output, cosine, sine):
    tokens, width = hidden.shape
    half = tokens // 2
    local = w_query.shape[1]
    heads = local // HD
    scale_factor = 1.0 / math.sqrt(HD)

    def kernel(
        core_ref, hidden_ref, gain_ref, wq_ref, wk_ref, wv_ref, wo_ref, cos_ref, sin_ref,
        normed_ref, query_ref, key_ref, value_ref, mixed_ref, keep_ref, send_ref, part_ref,
    ):
        for block in range(2):
            rows = pl.ds(block * half, half)
            source = hidden_ref[rows, :].astype(jnp.float32)
            scale = lax.rsqrt(jnp.mean(source * source, axis=-1, keepdims=True) + epsilon)
            normed = (source * scale * gain_ref[...]).astype(jnp.bfloat16)
            normed_ref[rows, :] = normed
            cos, sin = cos_ref[rows, :], sin_ref[rows, :]

            def turned(value):
                return (value * cos + pltpu.roll(value, HD // 2, 1) * sin).astype(jnp.bfloat16)

            query_pre = dot(normed, wq_ref[...])
            for head in range(heads):
                lanes = slice(head * HD, (head + 1) * HD)
                query_ref[rows, lanes] = turned(query_pre[:, lanes])
            key_ref[rows, :] = turned(dot(normed, wk_ref[...]))
            value_ref[rows, :] = dot(normed, wv_ref[...]).astype(jnp.bfloat16)
        for block in range(2):
            rows = pl.ds(block * half, half)
            seen = pl.ds(0, (block + 1) * half)
            keys, values = key_ref[seen, :], value_ref[seen, :]
            for head in range(heads):
                lanes = slice(head * HD, (head + 1) * HD)
                raw = causal_scores(query_ref[rows, lanes], keys, block * half, scale_factor)
                probs_low = softmax_rows(raw).astype(jnp.bfloat16)
                mixed_ref[rows, lanes] = dot(probs_low, values).astype(jnp.bfloat16)
            part_ref[rows, :] = dot(mixed_ref[rows, :], wo_ref[...])
        own = pl.ds(pl.multiple_of(core_ref[0] * half, half), half)
        other = pl.ds(pl.multiple_of((1 - core_ref[0]) * half, half), half)
        keep_ref[...] = hidden_ref[own, :].astype(jnp.float32) + part_ref[own, :]
        send_ref[...] = part_ref[other, :].astype(jnp.bfloat16)

    def low(rows, columns):
        return jax.ShapeDtypeStruct((rows, columns), jnp.bfloat16)

    shapes = [
        low(tokens, width), low(tokens, local), low(tokens, HD), low(tokens, HD),
        low(tokens, local), jax.ShapeDtypeStruct((half, width), jnp.float32), low(half, width),
    ]
    operands = [hidden, gain, w_query, w_key, w_value, w_output, cosine, sine]
    return pl.pallas_call(
        kernel,
        out_shape=shapes,
        in_specs=[pl.BlockSpec(memory_space=pltpu.SMEM)]
        + [pl.BlockSpec(memory_space=pltpu.VMEM) for _ in operands],
        out_specs=[pl.BlockSpec(memory_space=pltpu.VMEM) for _ in shapes],
        scratch_shapes=[pltpu.VMEM((tokens, width), jnp.float32)],
        compiler_params=pltpu.CompilerParams(vmem_limit_bytes=VMEM_BYTES),
        cost_estimate=small_cost(
            flops=40 * 10**9, bytes_accessed=16 * 10**6, transcendentals=2 * 10**6
        ),
        name="attention_forward",
    )(core, *operands)


def output_gradient(places, mixed, own, other):
    half, width = own.shape
    local = mixed.shape[1]
    piece = local // 4

    def kernel(places_ref, mixed_ref, own_ref, other_ref, *refs):
        pieces, (whole_ref, result) = refs[:4], refs[4:]
        core = places_ref[0]
        whole_ref[pl.ds(pl.multiple_of(core * half, half), half), :] = own_ref[...]
        whole_ref[pl.ds(pl.multiple_of((1 - core) * half, half), half), :] = other_ref[...]
        result[...] = contract_rows(mixed_ref[...], whole_ref[...]).astype(jnp.bfloat16)
        give_pieces(places_ref, result, pieces, piece)

    low = jax.ShapeDtypeStruct((piece, width), jnp.bfloat16)
    results = pl.pallas_call(
        kernel,
        in_specs=[pl.BlockSpec(memory_space=pltpu.SMEM)]
        + [pl.BlockSpec(memory_space=pltpu.VMEM)] * 3,
        out_specs=[pl.BlockSpec(memory_space=pltpu.VMEM)] * 5,
        out_shape=[low] * 4 + [jax.ShapeDtypeStruct((2 * half, width), jnp.bfloat16)],
        scratch_shapes=[pltpu.VMEM((local, width), jnp.bfloat16)],
        compiler_params=pltpu.CompilerParams(vmem_limit_bytes=VMEM_BYTES),
        cost_estimate=small_cost(),
        name="output_gradient",
    )(places, mixed, own, other)
    return results[:4], results[4]


def give_pieces(places_ref, result, pieces, rows):
    for side in range(2):
        bit = places_ref[1 + side]
        for n, place in enumerate((bit, 1 - bit)):
            start = pl.multiple_of((2 * side + place) * rows, rows)
            pieces[2 * side + n][...] = result[pl.ds(start, rows), :]


def attention_backward(grad_attn, w_output, queries, keys, values, cosine, sine):
    tokens, local = queries.shape
    half = tokens // 2
    heads = local // HD
    scale_factor = 1.0 / math.sqrt(HD)

    def kernel(
        ga_ref, wo_ref, query_ref, key_ref, value_ref, cos_ref, sin_ref, grad_ref, gk_ref, gv_ref, gm_ref
    ):
        gm_ref[...] = contract_cols(ga_ref[...], wo_ref[...]).astype(jnp.bfloat16)
        for block in range(2):
            rows = pl.ds(block * half, half)
            seen = pl.ds(0, (block + 1) * half)
            keys, values = key_ref[seen, :], value_ref[seen, :]
            cos, sin = cos_ref[rows, :], sin_ref[rows, :]
            grad_keys = jnp.zeros(((block + 1) * half, HD), jnp.float32)
            grad_values = grad_keys
            for head in range(heads):
                lanes = slice(head * HD, (head + 1) * HD)
                query, grad = query_ref[rows, lanes], gm_ref[rows, lanes]
                probs = softmax_rows(causal_scores(query, keys, block * half, scale_factor))
                grad_probs = contract_cols(grad, values)
                delta = jnp.sum(probs * grad_probs, axis=-1, keepdims=True)
                grad_scores = (probs * (grad_probs - delta)).astype(jnp.bfloat16)
                turned = dot(grad_scores, keys) * scale_factor
                grad_ref[rows, lanes] = (
                    turned * cos - pltpu.roll(turned, HD // 2, 1) * sin
                ).astype(jnp.bfloat16)
                grad_keys = grad_keys + contract_rows(grad_scores, query)
                grad_values = grad_values + contract_rows(probs.astype(jnp.bfloat16), grad)
            if block == 0:
                gk_ref[pl.ds(0, half), :] = grad_keys
                gv_ref[pl.ds(0, half), :] = grad_values
            else:
                first = pl.ds(0, half)
                gk_ref[first, :] = gk_ref[first, :] + grad_keys[:half]
                gv_ref[first, :] = gv_ref[first, :] + grad_values[:half]
                gk_ref[rows, :] = grad_keys[half:]
                gv_ref[rows, :] = grad_values[half:]
        turned = gk_ref[...] * scale_factor
        grad_ref[:, local : local + HD] = (
            turned * cos_ref[...] - pltpu.roll(turned, HD // 2, 1) * sin_ref[...]
        ).astype(jnp.bfloat16)
        grad_ref[:, local + HD :] = gv_ref[...].astype(jnp.bfloat16)

    return pl.pallas_call(
        kernel,
        out_shape=jax.ShapeDtypeStruct((tokens, local + 2 * HD), jnp.bfloat16),
        in_specs=[pl.BlockSpec(memory_space=pltpu.VMEM)] * 7,
        out_specs=pl.BlockSpec(memory_space=pltpu.VMEM),
        scratch_shapes=[pltpu.VMEM((tokens, HD), jnp.float32)] * 2
        + [pltpu.VMEM((tokens, local), jnp.bfloat16)],
        compiler_params=pltpu.CompilerParams(vmem_limit_bytes=VMEM_BYTES),
        cost_estimate=small_cost(
            flops=10 * 10**9, bytes_accessed=4 * 10**6, transcendentals=2 * 10**6
        ),
        name="attention_backward",
    )(grad_attn, w_output, queries, keys, values, cosine, sine)


def expert_weights_of(expert_ref, packs, half):
    start = 2 * half
    count = packs[0].shape[0] - start
    row_ids = lax.broadcasted_iota(jnp.int32, (count, 128), 0)
    lane_ids = lax.broadcasted_iota(jnp.int32, (count, 128), 1)
    pick = (row_ids == (expert_ref[0] ^ lane_ids)).astype(jnp.bfloat16)
    sides = []
    for ref in packs:
        coarse, fine = ref[start:, :half], ref[start:, half : 2 * half]
        sides.append(contract_rows(coarse, pick) + contract_rows(fine, pick))
    return jnp.concatenate(sides, axis=0)


def expert_terms(expert, joins, pieces, first, keep):
    sequences = [sequence for own, _ in joins for sequence in own]
    width = sequences[0][0].shape[1]
    half = sequences[0][0].shape[0] // 2 // 128 * 128
    number = len(pieces)
    arrays = [array for own in pieces for array, _ in own]
    columns = arrays[0].shape[-1]
    hidden = columns // 3
    tokens = 2 * half
    total = len(sequences)
    flat = [array for sequence in sequences for array in sequence]

    loads = []
    n = 0
    for own in pieces:
        loads.append([])
        place = 0
        for array, index in own:
            loads[-1].append((n, index, place, array.shape[-2]))
            place += array.shape[-2]
            n += 1
    copy_count = n

    def kernel(expert_ref, *refs):
        sources, refs = refs[: len(flat)], refs[len(flat) :]
        piece_refs, refs = refs[: len(arrays)], refs[len(arrays) :]
        results, (w_ref, packs, gate_all, semaphores) = refs[:-4], refs[-4:]
        e = pl.program_id(0)

        def copies_of(one):
            for which, index, place, rows in loads[one]:
                source = piece_refs[which] if index is None else piece_refs[which].at[index]
                yield pltpu.make_async_copy(
                    source, w_ref.at[one, pl.ds(place, rows), :], semaphores.at[which]
                )

        def kept(one):
            return pltpu.make_async_copy(
                w_ref.at[one], results[-1].at[one], semaphores.at[copy_count + one]
            )

        def pack_copy(n):
            return pltpu.make_async_copy(
                sources[n], packs.at[n], semaphores.at[copy_count + number + n]
            )

        @pl.when(e == 0)
        def _():
            for copy in copies_of(0):
                copy.start()
            for n in range(2 * total):
                pack_copy(n).start()
            for one in range(1, number):
                for copy in copies_of(one):
                    copy.start()

        for one in range(number):

            @pl.when(e == one)
            def _(one=one):
                for copy in copies_of(one):
                    copy.wait()
                if keep:
                    kept(one).start()

        lanes = lax.broadcasted_iota(jnp.int32, (half, 128), 1)
        n = 0
        for join, (own, start) in enumerate(joins):
            inner_ref, grad_ref = results[2 * join : 2 * join + 2]
            for s in range(len(own)):

                @pl.when(e == 0)
                def _(n=n):
                    for side in range(2):
                        pack_copy(2 * n + side).wait()
                    gate_all[n * tokens : (n + 1) * tokens, :] = expert_weights_of(
                        expert_ref, [packs.at[2 * n], packs.at[2 * n + 1]], half
                    )

                def run(n=n, s=s, inner_ref=inner_ref, grad_ref=grad_ref):
                    for side in range(2):
                        pack = packs.at[2 * n + side]
                        here = pl.ds(s * tokens + side * half, half)
                        gate = gate_all[n * tokens + side * half : n * tokens + (side + 1) * half, :]
                        weight = jnp.sum(
                            jnp.where(lanes == e + first, gate, 0.0), axis=1, keepdims=True
                        )
                        both = dot(pack[:half, :], w_ref[e, :, : 2 * hidden])
                        grad_inner = dot(pack[half : 2 * half, :], w_ref[e, :, 2 * hidden :]) * weight
                        gate_pre, up_pre = both[:, :hidden], both[:, hidden:]
                        sigmoid = jax.nn.sigmoid(gate_pre)
                        activated = gate_pre * sigmoid
                        grad_gate = (
                            grad_inner * up_pre * sigmoid * (1.0 + gate_pre * (1.0 - sigmoid))
                        )
                        grad_ref[here, :hidden] = grad_gate.astype(jnp.bfloat16)
                        grad_ref[here, hidden:] = (grad_inner * activated).astype(jnp.bfloat16)
                        inner_ref[here, :] = (activated * up_pre * weight).astype(jnp.bfloat16)

                if start:
                    pl.when(e >= start)(run)
                else:
                    run()
                n += 1

        if keep:

            @pl.when(e == number - 1)
            def _():
                for one in range(number):
                    kept(one).wait()

    out_specs, out_shape = [], []
    for own, start in joins:
        for size in (hidden, 2 * hidden):
            out_specs.append(
                pl.BlockSpec(
                    (len(own) * tokens, size), lambda e, start=start: (0, jnp.maximum(e - start, 0))
                )
            )
            out_shape.append(
                jax.ShapeDtypeStruct((len(own) * tokens, (number - start) * size), jnp.bfloat16)
            )
    if keep:
        out_specs.append(pl.BlockSpec(memory_space=pl.ANY))
        out_shape.append(jax.ShapeDtypeStruct((number, width, columns), jnp.bfloat16))
    results = pl.pallas_call(
        kernel,
        grid=(number,),
        in_specs=[pl.BlockSpec(memory_space=pltpu.SMEM)]
        + [pl.BlockSpec(memory_space=pl.ANY)] * (len(flat) + len(arrays)),
        out_specs=out_specs,
        out_shape=out_shape,
        scratch_shapes=[
            pltpu.VMEM((number, width, columns), jnp.bfloat16),
            pltpu.VMEM((2 * total, *flat[0].shape), jnp.bfloat16),
            pltpu.VMEM((total * tokens, 128), jnp.float32),
            pltpu.SemaphoreType.DMA((copy_count + number + 2 * total,)),
        ],
        compiler_params=pltpu.CompilerParams(vmem_limit_bytes=VMEM_BYTES),
        cost_estimate=small_cost(),
        name="expert_terms",
    )(expert, *flat, *arrays)
    terms = [tuple(results[2 * n : 2 * n + 2]) for n in range(len(joins))]
    return (*terms, results[-1]) if keep else tuple(terms)


def expert_sums(groups, weights, half):
    number, width = weights.shape[:2]
    hidden = weights.shape[2] // 3
    counts = [group[0][0].shape[0] // (2 * half) for group in groups]
    total = sum(counts)
    flat = [array for group in groups for part in group for array in part[:2]]
    block = 512

    def kernel(*refs):
        terms, refs = refs[: len(flat)], refs[len(flat) :]
        w_ref, back_own, back_other, out_own, out_other = refs
        n = place = 0
        for group, count in zip(groups, counts, strict=True):
            back = out = None
            for inner, _, start in group:
                for e in range(inner.shape[1] // hidden):
                    grad = terms[n + 1][:, 2 * e * hidden : 2 * (e + 1) * hidden]
                    one = contract_cols(grad, w_ref[start + e, :, : 2 * hidden])
                    back = one if back is None else back + one
                n += 2
            n -= 2 * len(group)
            for inner, _, start in group:
                for e in range(inner.shape[1] // hidden):
                    one = contract_cols(
                        terms[n][:, e * hidden : (e + 1) * hidden], w_ref[start + e, :, 2 * hidden :]
                    )
                    out = one if out is None else out + one
                n += 2
            for s in range(count):
                start = 2 * s * half
                back_own[place + s] = back[start : start + half].astype(jnp.bfloat16)
                back_other[place + s] = back[start + half : start + 2 * half].astype(jnp.bfloat16)
                out_own[place + s] = out[start : start + half].astype(jnp.bfloat16)
                out_other[place + s] = out[start + half : start + 2 * half].astype(jnp.bfloat16)
            place += count

    low = jax.ShapeDtypeStruct((total, half, width), jnp.bfloat16)
    return pl.pallas_call(
        kernel,
        grid=(width // block,),
        in_specs=[whole(*a.shape) for a in flat]
        + [pl.BlockSpec((number, block, 3 * hidden), lambda n: (0, n, 0))],
        out_specs=[pl.BlockSpec((total, half, block), lambda n: (0, 0, n))] * 4,
        out_shape=[low] * 4,
        compiler_params=pltpu.CompilerParams(vmem_limit_bytes=VMEM_BYTES),
        cost_estimate=small_cost(),
        name="expert_sums",
    )(*flat, weights)


def load_copies(sequence, half, sources, x_all, dy_all, semaphores, which=range(4)):
    for n in which:
        target = x_all if n < 2 else dy_all
        yield pltpu.make_async_copy(
            sources[2 * sequence + n % 2].at[pl.ds((n // 2) * half, half), :],
            target.at[pl.ds((2 * sequence + n % 2) * half, half), :],
            semaphores.at[4 * sequence + n],
        )


def expert_weight_grads(sequences, terms, number, hidden):
    width = sequences[0][0].shape[1]
    half = sequences[0][0].shape[0] // 2 // 128 * 128
    tokens = 2 * half
    flat = [array for sequence in sequences for array in sequence]
    total = len(sequences)
    quarter = width // 4
    per_load = 4 * total

    def kernel(*refs):
        sources, refs = refs[: len(flat)], refs[len(flat) :]
        term_refs, refs = refs[: 2 * len(terms)], refs[2 * len(terms) :]
        result_refs, refs = refs[: 4 * number], refs[4 * number :]
        x_all, dy_all, inner_all, grad_all, result, semaphores, term_semaphores, out_semaphores = refs

        def row_copies(of_gradients):
            for s in range(total):
                yield from load_copies(
                    s, half, sources, x_all, dy_all, semaphores, (2, 3) if of_gradients else (0, 1)
                )

        def term_copies(e, of_products):
            place = 0
            for n, (inner, _, start) in enumerate(terms):
                rows = inner.shape[0]
                size = 2 * hidden if of_products else hidden
                yield pltpu.make_async_copy(
                    term_refs[2 * n + of_products].at[:, pl.ds((start + e) * size, size)],
                    (grad_all if of_products else inner_all).at[e, pl.ds(place, rows), :],
                    term_semaphores.at[2 * len(terms) * e + 2 * n + of_products],
                )
                place += rows

        def out_copies(e):
            for q in range(4):
                yield pltpu.make_async_copy(
                    result.at[e, pl.ds(q * quarter, quarter), :],
                    result_refs[4 * e + q],
                    out_semaphores.at[4 * e + q],
                )

        first = [*row_copies(True), *term_copies(0, 0)]
        second = [*row_copies(False), *term_copies(0, 1)]
        later = [[*term_copies(e, 0), *term_copies(e, 1)] for e in range(1, number)]
        for copy in [*first, *second, *(copy for one in later for copy in one)]:
            copy.start()
        for e in range(number):
            for copy in first if e == 0 else later[e - 1]:
                copy.wait()
            result[e, :, 2 * hidden :] = contract_rows(dy_all[...], inner_all[e]).astype(jnp.bfloat16)
            if e == 0:
                for copy in second:
                    copy.wait()
            result[e, :, : 2 * hidden] = contract_rows(x_all[...], grad_all[e]).astype(jnp.bfloat16)
            for copy in out_copies(e):
                copy.start()
        for e in range(number):
            for copy in out_copies(e):
                copy.wait()

    anywhere = pl.BlockSpec(memory_space=pl.ANY)
    return pl.pallas_call(
        kernel,
        in_specs=[anywhere] * (len(flat) + 2 * len(terms)),
        out_specs=[anywhere] * (4 * number),
        scratch_shapes=[pltpu.VMEM((total * tokens, width), jnp.bfloat16)] * 2
        + [
            pltpu.VMEM((number, total * tokens, hidden), jnp.bfloat16),
            pltpu.VMEM((number, total * tokens, 2 * hidden), jnp.bfloat16),
            pltpu.VMEM((number, width, 3 * hidden), jnp.bfloat16),
            pltpu.SemaphoreType.DMA((per_load,)),
            pltpu.SemaphoreType.DMA((2 * len(terms) * number,)),
            pltpu.SemaphoreType.DMA((4 * number,)),
        ],
        out_shape=[jax.ShapeDtypeStruct((quarter, 3 * hidden), jnp.bfloat16)] * (4 * number),
        compiler_params=pltpu.CompilerParams(vmem_limit_bytes=VMEM_BYTES),
        cost_estimate=small_cost(),
        name="expert_weight_grads",
    )(*flat, *(array for term in terms for array in term[:2]))


def own_weight_grads(sequences, terms, arrived, hidden):
    width = sequences[0][0].shape[1]
    half = sequences[0][0].shape[0] // 2 // 128 * 128
    tokens = 2 * half
    counts = [pair[0].shape[0] // tokens for pair in terms]
    flat = [array for sequence in sequences for array in sequence]
    total = len(sequences)
    quarter = width // 4

    def kernel(*refs):
        sources, refs = refs[: len(flat)], refs[len(flat) :]
        term_refs, refs = refs[: 2 * len(counts)], refs[2 * len(counts) :]
        arrived_refs, refs = refs[:6], refs[6:]
        gate_ref, up_ref, down_ref, x_all, dy_all, semaphores = refs
        for s in range(total):
            for copy in load_copies(s, half, sources, x_all, dy_all, semaphores):
                copy.start()
        gate_up = down = None
        first = 0
        for joined, count in enumerate(counts):
            for s in range(first, first + count):
                for copy in load_copies(s, half, sources, x_all, dy_all, semaphores):
                    copy.wait()
            span = pl.ds(first * tokens, count * tokens)
            one = contract_rows(x_all[span, :], term_refs[2 * joined + 1][...])
            two = contract_rows(term_refs[2 * joined][...], dy_all[span, :])
            gate_up = one if gate_up is None else gate_up + one
            down = two if down is None else down + two
            first += count
        for q in range(4):
            rows = slice(q * quarter, (q + 1) * quarter)
            inside = slice(q % 2 * quarter, (q % 2 + 1) * quarter)
            more = arrived_refs[q][...].astype(jnp.float32) + arrived_refs[4 + q // 2][
                inside, :
            ].astype(jnp.float32)
            both = gate_up[rows] + more[:, : 2 * hidden]
            gate_ref[0, rows, :] = both[:, :hidden]
            up_ref[0, rows, :] = both[:, hidden:]
            down_ref[0, :, rows] = down[:, rows] + more[:, 2 * hidden :].T

    def beside(count, columns):
        return pl.BlockSpec((count * tokens, columns), lambda e: (0, 0))

    tall = jax.ShapeDtypeStruct((1, width, hidden), jnp.float32)
    flat_down = jax.ShapeDtypeStruct((1, hidden, width), jnp.float32)
    return pl.pallas_call(
        kernel,
        grid=(1,),
        in_specs=[pl.BlockSpec(memory_space=pl.ANY)] * len(flat)
        + [beside(count, columns) for count in counts for columns in (hidden, 2 * hidden)]
        + [whole(quarter, 3 * hidden)] * 4
        + [whole(2 * quarter, 3 * hidden)] * 2,
        out_specs=[whole(*tall.shape), whole(*tall.shape), whole(*flat_down.shape)],
        scratch_shapes=[pltpu.VMEM((total * tokens, width), jnp.bfloat16)] * 2
        + [pltpu.SemaphoreType.DMA((4 * total,))],
        out_shape=[tall, tall, flat_down],
        compiler_params=pltpu.CompilerParams(vmem_limit_bytes=VMEM_BYTES),
        cost_estimate=small_cost(),
        name="own_weight_grads",
    )(*flat, *(array for pair in terms for array in pair), *arrived)


def planes_of_four(
    hidden_in,
    attn_gain,
    w_query,
    w_key,
    w_value,
    w_output,
    moe_gain,
    w_gate,
    w_up,
    w_down,
    gate_logits,
    routes,
    out_grad,
):
    tokens, width = hidden_in.shape
    half = tokens // 2
    experts = lax.axis_size("expert")
    columns = [[4 * z + r for z in range(4)] for r in range(4)]
    core = lax.axis_index("tensor")
    expert = lax.axis_index("expert")
    plane = expert // 4
    bit_x = expert % 2
    bit_y = (expert // 2) % 2
    hidden = w_down.shape[1]
    together = lax.optimization_barrier

    own_weights = jnp.concatenate([w_gate[0], w_up[0], w_down[0].T], axis=1)
    quarter = width // 4
    pieces = [own_weights[:quarter], own_weights[quarter : 2 * quarter], own_weights[2 * quarter :]]
    gate_weights = jax.nn.softmax(gate_logits, axis=-1)
    names = jnp.arange(experts, dtype=jnp.int32)
    dense = jnp.sum(
        jnp.where(routes.T[:, None, :] == names[None, :, None], gate_weights.T[:, None, :], 0.0),
        axis=0,
    )
    dense = lax.dynamic_slice_in_dim(dense, core * half, half, 1)
    coarse = dense.astype(jnp.bfloat16)
    fine = (dense - coarse.astype(jnp.float32)).astype(jnp.bfloat16)
    extra = jnp.pad(jnp.concatenate([coarse, fine], axis=1), ((0, 0), (0, width - 2 * half)))
    out_grad_half = part(out_grad, core, 2)
    dy_own = jnp.concatenate([out_grad_half, extra], axis=0)

    x0, y0 = flip(pieces[0], 1), flip(pieces[0], 2)
    dy_out_one, dy_in_one = outer(dy_own), inner(dy_own)
    cosine, sine = (jnp.asarray(table) for table in rotary_tables(tokens))
    normed, queries, keys, values, mixed, keep, send = attention_forward(
        core.reshape(1), hidden_in, attn_gain[None], w_query, w_key, w_value, w_output, cosine, sine
    )
    send, x0, y0, dy_out_one, dy_in_one, piece = together(
        (send, x0, y0, dy_out_one, dy_in_one, pieces[1])
    )
    x1, y1 = flip(piece, 1), flip(piece, 2)
    middle = keep + swap(send).astype(jnp.float32)
    scale_two = lax.rsqrt(jnp.mean(middle * middle, axis=-1, keepdims=True) + epsilon)
    unit_two = middle * scale_two
    rows_in = (unit_two * moe_gain).astype(jnp.bfloat16)
    out_one, in_one = outer(rows_in), inner(rows_in)
    x1, y1, out_one, in_one, dy_out_one, dy_in_one, piece = together(
        (x1, y1, out_one, in_one, dy_out_one, dy_in_one, pieces[2])
    )
    out_one = jnp.concatenate([out_one, dy_out_one], axis=0)
    in_one = jnp.concatenate([in_one, dy_in_one], axis=0)
    out_one, in_one, piece = together((out_one, in_one, piece))
    x2, y2 = flip(piece, 1), flip(piece, 2)
    out_two, in_two = outer(in_one), inner(out_one)
    own = jnp.concatenate([rows_in, dy_own], axis=0)
    own, first = (own, swap(own)), (out_one, swap(out_one))
    far_from_y = jnp.concatenate([y0, y1], axis=0)
    x2, y2, out_two, in_two, own, first, far_from_y = together(
        (x2, y2, out_two, in_two, own, first, far_from_y)
    )
    far_weights = [flip(far_from_y, 1), flip(x2, 2)]
    out_three = outer(in_two)
    at_end = (plane == 0) | (plane == 3)
    number = expert.reshape(1)
    second = jnp.where(at_end, out_two, in_one)
    second = (second, swap(second))
    near_pieces = [[own_weights], [x0, x1, x2], [y0, y1, y2]]
    near_early, near_second, near_weights = expert_terms(
        number,
        [([own, first], 0), ([second], 0)],
        [[(piece, None) for piece in one] for one in near_pieces],
        0,
        True,
    )
    far_weights, out_three, near_early, near_second, second = together(
        (far_weights, out_three, near_early, near_second, second)
    )
    third = jnp.where(at_end, out_three, in_two)
    third = (third, swap(third))
    far_pieces = [(piece, None) for piece in far_weights]
    all_third, far_second, far_early, weights = expert_terms(
        number,
        [([third], 0), ([second], 3), ([own, first], 3)],
        [[(near_weights, 0)], [(near_weights, 1)], [(near_weights, 2)], far_pieces],
        0,
        True,
    )
    to_far = expert_weight_grads(
        [third, second, own, first], [(*all_third, 3), (*far_second, 0), (*far_early, 0)], 1, hidden
    )
    over_x, over_y = [flip(to_far[0], 1)], [flip(to_far[2], 2)]
    to_far, near_second, far_second = together((to_far, near_second, far_second))
    late_sums = expert_sums(
        [[(*all_third, 0)], [(*near_second, 0), (*far_second, 3)]], weights, half
    )
    late_sums, over_x, over_y, to_far = together((late_sums, over_x, over_y, to_far))
    back_late = add_low(late_sums[0], swap(late_sums[1]))
    back_late, near_early, all_third = together((back_late, near_early, all_third))
    second_back, third_back = back_late[1], back_late[0]

    arrived_out = outer(third_back)
    over_x, over_y = over_x + [flip(to_far[1], 1)], over_y + [flip(to_far[3], 2)]
    beside = expert_weight_grads(
        [own, first, second, third],
        [(*near_early, 1), (*near_second, 1), (*all_third, 1)],
        2,
        hidden,
    )
    arrived_out, beside, over_x, over_y, far_early = together(
        (arrived_out, beside, over_x, over_y, far_early)
    )
    to_x, to_y = beside[:4], beside[4:]
    arrived_in, arrived_out = inner(add_low(third_back, arrived_out)), outer(second_back)
    from_x, from_y = [flip(to_x[0], 1)], [flip(to_y[2], 2)]
    early_sums = expert_sums([[(*near_early, 0), (*far_early, 3)]], weights, half)
    arrived_in, arrived_out, early_sums, from_x, from_y, to_x, to_y = together(
        (arrived_in, arrived_out, early_sums, from_x, from_y, to_x, to_y)
    )
    back_early = add_low(early_sums[0], swap(early_sums[1]))
    own_back, first_back = back_early[0], back_early[1]
    going_out = jnp.where(at_end, first_back, add_low(first_back, arrived_in))
    going_in = add_low(second_back, arrived_out)
    going_out, going_in, early_sums, late_sums, over_x = together(
        (going_out, going_in, early_sums, late_sums, over_x)
    )
    arrived_out, arrived_in = outer(going_out), inner(going_in)
    from_x, from_y = from_x + [flip(to_x[1], 1)], from_y + [flip(to_y[3], 2)]
    with_x = jnp.concatenate([add_low(to_y[n], over_x[n]) for n in range(2)], axis=0)
    with_y = jnp.concatenate([add_low(to_x[2 + n], over_y[n]) for n in range(2)], axis=0)
    out_late = add_low(late_sums[2], swap(late_sums[3]))
    out_early = add_low(early_sums[2], swap(early_sums[3]))
    own_out, first_out, second_out, third_out = out_early[0], out_early[1], out_late[1], out_late[0]
    by_plane = [
        jnp.where(plane == 0, own_out, jnp.where(plane == 1, first_out, third_out)),
        jnp.where(plane == 0, first_out, jnp.where(plane == 1, own_out, second_out)),
        jnp.where(plane == 3, first_out, jnp.where(plane == 2, own_out, second_out)),
        jnp.where(plane == 3, own_out, jnp.where(plane == 2, first_out, third_out)),
    ]
    results = jnp.concatenate(by_plane, axis=0)
    arrived_out, arrived_in, results, from_x, from_y, with_x, with_y = together(
        (arrived_out, arrived_in, results, from_x, from_y, with_x, with_y)
    )
    moe_result = lax.psum_scatter(
        results, "expert", axis_index_groups=columns, scatter_dimension=0, tiled=True
    )
    grad_rows = own_back.astype(jnp.float32) + arrived_out.astype(jnp.float32)
    grad_rows = jnp.where(at_end, grad_rows, grad_rows + arrived_in.astype(jnp.float32))
    grad_out = out_grad_half.astype(jnp.float32)
    grad_unit_two = grad_rows * moe_gain
    grad_moe_gain = jnp.sum(grad_rows * unit_two, axis=0)
    grad_middle = grad_out + scale_two * (
        grad_unit_two - unit_two * jnp.mean(grad_unit_two * unit_two, axis=-1, keepdims=True)
    )
    grad_attn_half = grad_middle.astype(jnp.bfloat16)
    places = jnp.stack([core, bit_x, bit_y])
    output_pieces, grad_attn = output_gradient(places, mixed, grad_attn_half, swap(grad_attn_half))
    output_pieces, grad_attn = together((output_pieces, grad_attn))
    left, to_x_side, right, to_y_side = output_pieces
    output_parts = add_low(left, flip(to_x_side, 1)), add_low(right, flip(to_y_side, 2))
    grad_all_pre = attention_backward(grad_attn, w_output, queries, keys, values, cosine, sine)
    grad_all_pre, output_parts = together((grad_all_pre, output_parts))
    grad_projections = contract_rows(normed, grad_all_pre).astype(jnp.bfloat16)
    output_parts = plane_scatter_second(output_parts, bit_x, bit_y)
    grad_projections, output_parts = together((grad_projections, output_parts))
    projection_parts = plane_scatter_first(grad_projections, bit_x, bit_y)
    w_all = jnp.concatenate([w_query, w_key, w_value], axis=1)
    grad_normed_part = contract_cols(grad_all_pre, w_all).astype(jnp.bfloat16)
    grad_normed = part(grad_normed_part, core, 2).astype(jnp.float32) + swap(
        part(grad_normed_part, 1 - core, 2)
    ).astype(jnp.float32)
    source_half = part(hidden_in, core, 2).astype(jnp.float32)
    scale_half = lax.rsqrt(jnp.mean(source_half * source_half, axis=-1, keepdims=True) + epsilon)
    unit_half = source_half * scale_half
    grad_unit_one = grad_normed * attn_gain
    grad_attn_gain = jnp.sum(grad_normed * unit_half, axis=0)
    grad_in_half = grad_middle + scale_half * (
        grad_unit_one - unit_half * jnp.mean(grad_unit_one * unit_half, axis=-1, keepdims=True)
    )
    gains = jnp.stack([grad_attn_gain, grad_moe_gain])
    projection_parts, gains, grad_in_half = together((projection_parts, gains, grad_in_half))
    projection_parts = plane_scatter_second(projection_parts, bit_x, bit_y)
    gains = (gains + swap(gains)).reshape(-1, grad_projections.shape[1])
    gain_rows = gains.shape[0]
    gains = jnp.pad(gains, ((0, 16 - gain_rows), (0, 0))).astype(jnp.bfloat16)
    grad_in_other = swap(grad_in_half)
    output_both = jnp.concatenate(output_parts, axis=0)
    projection_both = jnp.concatenate([*projection_parts, gains], axis=0)
    projection_both, output_both, moe_result, with_x, with_y = together(
        (projection_both, output_both, moe_result, with_x, with_y)
    )
    output_both, projection_both = lax.psum(
        (output_both, projection_both), "expert", axis_index_groups=columns
    )
    block_half = (middle + moe_result.astype(jnp.float32)).astype(jnp.bfloat16)
    block_out = ordered(block_half, swap(block_half), core)
    then_y, then_x = flip(with_x, 2), flip(with_y, 1)
    output_both, projection_both, block_out, then_x, then_y = together(
        (output_both, projection_both, block_out, then_x, then_y)
    )
    gains, projection_both = projection_both[-16:].astype(jnp.float32), projection_both[:-16]
    output_halves = plane_gather_first(*jnp.split(output_both, 2), bit_x, bit_y)
    projection_halves = plane_gather_first(*jnp.split(projection_both, 2), bit_x, bit_y)
    output_halves, projection_halves, gains, then_x, then_y, grad_in_half, grad_in_other = together(
        (output_halves, projection_halves, gains, then_x, then_y, grad_in_half, grad_in_other)
    )
    arrived = (*from_x, *from_y, then_y, then_x)
    expert_grads = own_weight_grads(
        [own, first, second, third], [near_early, near_second, all_third], arrived, hidden
    )
    grad_in = ordered(grad_in_half, grad_in_other, core)
    bits = jnp.stack([bit_x, bit_y])
    projection_widths = [w.shape[1] for w in (w_query, w_key, w_value)]
    output_early = lay_out(bits, output_halves, (width,), False)
    projections_early = lay_out(bits, projection_halves, projection_widths, False)
    output_pieces = plane_gather_second(*output_halves)
    projection_pieces = plane_gather_second(*projection_halves)
    early_ones = (output_early, projections_early, grad_in)
    expert_grads, output_pieces, projection_pieces, gains, early_ones = together(
        (expert_grads, output_pieces, projection_pieces, gains, early_ones)
    )
    output_early, projections_early, grad_in = early_ones
    gains = (gains + flip(gains, 1)) + (flip(gains, 2) + flip(gains, 3))
    gains_sum = gains[:gain_rows].reshape(2, width)
    grad_gate, grad_up, grad_down = expert_grads
    projections = lay_out(bits, projection_pieces, projection_widths, True, projections_early)
    (output_sum,) = lay_out(bits, output_pieces, (width,), True, output_early)
    return (
        block_out,
        grad_in,
        gains_sum[0],
        *projections,
        output_sum,
        gains_sum[1],
        grad_gate,
        grad_up,
        grad_down,
    )


def solution(mesh):
    on_device = planes_of_four if mesh.shape["expert"] == 16 else routed_slots
    return jax.shard_map(
        on_device,
        mesh=mesh,
        in_specs=(
            P("expert", None),
            P(),
            P(None, "tensor"),
            P(None, "tensor"),
            P(None, "tensor"),
            P("tensor", None),
            P(),
            P("expert", None, "tensor"),
            P("expert", None, "tensor"),
            P("expert", "tensor", None),
            P("expert", None),
            P("expert", None),
            P("expert", None),
        ),
        out_specs=(
            P("expert", None),
            P("expert", None),
            P(),
            P(None, "tensor"),
            P(None, "tensor"),
            P(None, "tensor"),
            P("tensor", None),
            P(),
            P("expert", None, "tensor"),
            P("expert", None, "tensor"),
            P("expert", "tensor", None),
        ),
        check_vma=False,
    )
```

```python
import math

import jax
import jax.numpy as jnp
import numpy as np
from jax import lax
from jax.experimental import pallas as pl
from jax.experimental.pallas import tpu as pltpu
from jax.sharding import PartitionSpec as P

HD = 128


epsilon = 1e-06
rope_base = 10000.0
masked_score = -1e30


def rotate(values, places, sign):
    halfway = values.shape[-1] // 2
    frequency = rope_base ** (-jnp.arange(halfway, dtype=jnp.float32) / halfway)
    angles = places.astype(jnp.float32)[:, None] * frequency[None, :]
    cosine = jnp.cos(angles)[:, None, :]
    sine = sign * jnp.sin(angles)[:, None, :]
    first = values[..., :halfway]
    second = values[..., halfway:]
    return jnp.concatenate(
        [first * cosine - second * sine, second * cosine + first * sine], axis=-1
    )


def contract_rows(left, right):
    return lax.dot_general(
        left, right, (((0,), (0,)), ((), ())), preferred_element_type=jnp.float32
    )


def contract_cols(left, right):
    return lax.dot_general(
        left, right, (((1,), (1,)), ((), ())), preferred_element_type=jnp.float32
    )


def block_scores(query_block, keys_used, row_start, scale_factor):
    query_rows = query_block.shape[0]
    key_rows = keys_used.shape[0]
    raw_scores = (
        jnp.einsum("qcgd,kcd->cgqk", query_block, keys_used, preferred_element_type=jnp.float32)
        * scale_factor
    )
    row_ids = row_start + jnp.arange(query_rows)
    causal = jnp.arange(key_rows)[None, :] <= row_ids[:, None]
    return jnp.where(causal, raw_scores, masked_score)


def routed_slots(
    hidden_in,
    attn_gain,
    w_query,
    w_key,
    w_value,
    w_output,
    moe_gain,
    w_gate,
    w_up,
    w_down,
    gate_logits,
    routes,
    out_grad,
):
    tokens, model_width = hidden_in.shape
    experts = lax.axis_size("expert")
    tensor_ranks = lax.axis_size("tensor")
    tensor_rank = lax.axis_index("tensor")
    route_width = routes.shape[1]
    route_count = tokens * route_width
    capacity = 2 * route_count // experts
    half_slots = capacity // tensor_ranks
    heads_local = w_query.shape[1] // HD
    kv_local = w_key.shape[1] // HD
    groups = heads_local // kv_local
    scale_factor = 1.0 / math.sqrt(HD)
    block_rows = min(512, tokens)
    places = jnp.arange(tokens, dtype=jnp.int32)
    flat_routes = routes.reshape(-1)
    route_hits = (flat_routes[:, None] == jnp.arange(experts, dtype=jnp.int32)[None, :]).astype(
        jnp.int32
    )
    slot_index = jnp.sum(jnp.cumsum(route_hits, axis=0) * route_hits, axis=1) - 1
    which_route = (
        jnp.full((experts * capacity,), route_count, jnp.int32)
        .at[flat_routes * capacity + slot_index]
        .set(jnp.arange(route_count, dtype=jnp.int32))
    )
    which_token = which_route // route_width
    own_half = slot_index // half_slots == tensor_rank
    back_index = jnp.where(
        own_half, flat_routes * half_slots + slot_index % half_slots, experts * half_slots
    )
    gate_weights = jax.nn.softmax(gate_logits, axis=-1)
    full_gate, full_up, full_down = (w_gate[0], w_up[0], w_down[0])

    def deliver(buffer):
        arrived_all = lax.all_to_all(buffer, "expert", split_axis=0, concat_axis=0, tiled=True)
        return arrived_all.reshape(experts * capacity, model_width)

    def give_back(partial_value):
        summed_rows = lax.psum_scatter(
            partial_value.reshape(experts, capacity, model_width).astype(jnp.bfloat16),
            "tensor",
            scatter_dimension=1,
            tiled=True,
        )
        returned = lax.all_to_all(summed_rows, "expert", split_axis=0, concat_axis=0, tiled=True)
        return jnp.concatenate(
            [
                returned.reshape(experts * half_slots, model_width),
                jnp.zeros((1, model_width), jnp.bfloat16),
            ],
            axis=0,
        )

    def collect(returned, weights):
        picked = returned[back_index].astype(jnp.float32).reshape(tokens, route_width, model_width)
        return lax.psum(
            jnp.sum(picked * weights[:, :, None], axis=1).astype(jnp.bfloat16), "tensor"
        ).astype(jnp.float32)

    source = hidden_in.astype(jnp.float32)
    scale_one = lax.rsqrt(jnp.mean(source * source, axis=-1, keepdims=True) + epsilon)
    unit_one = source * scale_one
    normed = (unit_one * attn_gain).astype(jnp.bfloat16)
    query_pre = jnp.dot(normed, w_query, preferred_element_type=jnp.float32).reshape(
        tokens, heads_local, HD
    )
    queries = (
        rotate(query_pre, places, 1.0).astype(jnp.bfloat16).reshape(tokens, kv_local, groups, HD)
    )
    key_pre = jnp.dot(normed, w_key, preferred_element_type=jnp.float32).reshape(
        tokens, kv_local, HD
    )
    keys_used = rotate(key_pre, places, 1.0).astype(jnp.bfloat16)
    values_used = (
        jnp.dot(normed, w_value, preferred_element_type=jnp.float32)
        .astype(jnp.bfloat16)
        .reshape(tokens, kv_local, HD)
    )
    row_start = 0
    query_block = queries
    raw_scores = block_scores(query_block, keys_used, row_start, scale_factor)
    biggest = jnp.max(raw_scores, axis=-1, keepdims=True)
    exponent = jnp.exp(raw_scores - biggest)
    row_total = jnp.sum(exponent, axis=-1, keepdims=True)
    weights_low = (exponent / row_total).astype(jnp.bfloat16)
    logsums = [biggest + jnp.log(row_total)]
    attended = jnp.einsum(
        "cgqk,kcd->qcgd", weights_low, values_used, preferred_element_type=jnp.float32
    )
    mixed_blocks = attended.reshape(block_rows, heads_local * HD).astype(jnp.bfloat16)
    attn_part = jnp.dot(mixed_blocks, w_output, preferred_element_type=jnp.float32)
    middle = source + lax.psum(attn_part.astype(jnp.bfloat16), "tensor").astype(jnp.float32)
    scale_two = lax.rsqrt(jnp.mean(middle * middle, axis=-1, keepdims=True) + epsilon)
    unit_two = middle * scale_two
    rows_in = (unit_two * moe_gain).astype(jnp.bfloat16)
    padded_rows = jnp.concatenate([rows_in, jnp.zeros((1, model_width), jnp.bfloat16)], axis=0)
    arrived = deliver(padded_rows[which_token].reshape(experts, capacity, model_width))
    gate_pre = jnp.dot(arrived, full_gate, preferred_element_type=jnp.float32)
    up_pre = jnp.dot(arrived, full_up, preferred_element_type=jnp.float32)
    sigmoid = jax.nn.sigmoid(gate_pre)
    activated = gate_pre * sigmoid
    hidden_units = (activated * up_pre).astype(jnp.bfloat16)
    produced = jnp.dot(hidden_units, full_down, preferred_element_type=jnp.float32)
    moe_result = collect(give_back(produced), gate_weights)
    block_out = (middle + moe_result).astype(jnp.bfloat16)
    grad_out = out_grad.astype(jnp.float32)
    route_grads = (
        (gate_weights[:, :, None] * grad_out[:, None, :])
        .astype(jnp.bfloat16)
        .reshape(route_count, model_width)
    )
    padded_grads = jnp.concatenate([route_grads, jnp.zeros((1, model_width), jnp.bfloat16)], axis=0)
    grad_arrived = deliver(padded_grads[which_route].reshape(experts, capacity, model_width))
    grad_down = contract_rows(hidden_units, grad_arrived)
    grad_inner = contract_cols(grad_arrived, full_down)
    grad_gate_pre = (grad_inner * up_pre * sigmoid * (1.0 + gate_pre * (1.0 - sigmoid))).astype(
        jnp.bfloat16
    )
    grad_up_pre = (grad_inner * activated).astype(jnp.bfloat16)
    grad_gate = contract_rows(arrived, grad_gate_pre)
    grad_up = contract_rows(arrived, grad_up_pre)
    grad_arrived_rows = contract_cols(grad_gate_pre, full_gate) + contract_cols(
        grad_up_pre, full_up
    )
    grad_rows = collect(give_back(grad_arrived_rows), jnp.ones_like(gate_weights))
    grad_unit_two = grad_rows * moe_gain
    grad_moe_gain = jnp.sum(grad_rows * unit_two, axis=0)
    grad_middle = grad_out + scale_two * (
        grad_unit_two - unit_two * jnp.mean(grad_unit_two * unit_two, axis=-1, keepdims=True)
    )
    grad_attn = grad_middle.astype(jnp.bfloat16)
    grad_output = contract_rows(mixed_blocks, grad_attn)
    grad_mixed = (
        contract_cols(grad_attn, w_output)
        .astype(jnp.bfloat16)
        .reshape(tokens, kv_local, groups, HD)
    )
    grad_query_blocks = []
    grad_keys = jnp.zeros((tokens, kv_local, HD), jnp.float32)
    grad_values = jnp.zeros((tokens, kv_local, HD), jnp.float32)
    for block_number, row_start in enumerate(range(0, tokens, block_rows)):
        query_block = queries
        raw_scores = block_scores(query_block, keys_used, row_start, scale_factor)
        probs = jnp.exp(raw_scores - logsums[block_number])
        probs_low = probs.astype(jnp.bfloat16)
        grad_probs = jnp.einsum(
            "qcgd,kcd->cgqk", grad_mixed, values_used, preferred_element_type=jnp.float32
        )
        delta = jnp.sum(probs * grad_probs, axis=-1, keepdims=True)
        grad_scores = (probs * (grad_probs - delta)).astype(jnp.bfloat16)
        grad_query_blocks.append(
            jnp.einsum("cgqk,kcd->qcgd", grad_scores, keys_used, preferred_element_type=jnp.float32)
            * scale_factor
        )
        grad_keys = (
            jnp.einsum(
                "cgqk,qcgd->kcd", grad_scores, query_block, preferred_element_type=jnp.float32
            )
            * scale_factor
        )
        grad_values = jnp.einsum(
            "cgqk,qcgd->kcd", probs_low, grad_mixed, preferred_element_type=jnp.float32
        )
    grad_queries = grad_query_blocks[0].reshape(tokens, heads_local, HD)
    grad_query_pre = (
        rotate(grad_queries, places, -1.0).astype(jnp.bfloat16).reshape(tokens, heads_local * HD)
    )
    grad_key_pre = (
        rotate(grad_keys, places, -1.0).astype(jnp.bfloat16).reshape(tokens, kv_local * HD)
    )
    grad_value_pre = grad_values.astype(jnp.bfloat16).reshape(tokens, kv_local * HD)
    grad_query = contract_rows(normed, grad_query_pre)
    grad_key = contract_rows(normed, grad_key_pre)
    grad_value = contract_rows(normed, grad_value_pre)
    grad_normed_part = (
        contract_cols(grad_query_pre, w_query)
        + contract_cols(grad_key_pre, w_key)
        + contract_cols(grad_value_pre, w_value)
    )
    grad_normed = lax.psum(grad_normed_part.astype(jnp.bfloat16), "tensor").astype(jnp.float32)
    grad_unit_one = grad_normed * attn_gain
    grad_attn_gain = jnp.sum(grad_normed * unit_one, axis=0)
    grad_in = grad_middle + scale_one * (
        grad_unit_one - unit_one * jnp.mean(grad_unit_one * unit_one, axis=-1, keepdims=True)
    )
    summed = lax.psum(
        (grad_query, grad_key, grad_value, grad_output, grad_attn_gain, grad_moe_gain), "expert"
    )
    return (
        block_out,
        grad_in,
        summed[4],
        summed[0],
        summed[1],
        summed[2],
        summed[3],
        summed[5],
        grad_gate[None],
        grad_up[None],
        grad_down[None],
    )


VMEM_BYTES = 60 * 2**20


def small_cost(**_):
    return pl.CostEstimate(flops=1000, bytes_accessed=1000, transcendentals=0)


def dot(left, right):
    return jnp.dot(left, right, preferred_element_type=jnp.float32)


def whole(*shape):
    return pl.BlockSpec(shape, lambda *_: (0,) * len(shape), pipeline_mode=pl.Buffered(1))


def swap(value):
    return lax.ppermute(value, "tensor", [(0, 1), (1, 0)])


def flip(value, bit):
    places = lax.axis_size("expert")
    return lax.ppermute(value, "expert", [(i, i ^ bit) for i in range(places)])


def outer(value):
    return flip(value, 4)


def inner(value):
    places = lax.axis_size("expert")
    return lax.ppermute(value, "expert", [(i, i ^ 12 if i // 4 in (1, 2) else i) for i in range(places)])


def part(value, index, count):
    size = value.shape[0] // count
    return lax.dynamic_slice_in_dim(value, index * size, size, 0)


def ordered(own, other, place):
    return jnp.where(
        place == 0,
        jnp.concatenate([own, other], axis=0),
        jnp.concatenate([other, own], axis=0),
    )


def add_low(kept, arrived):
    return (kept.astype(jnp.float32) + arrived.astype(jnp.float32)).astype(jnp.bfloat16)


def plane_scatter_first(value, bit_x, bit_y):
    left, right = jnp.split(value, 2, axis=0)
    left = add_low(part(left, bit_x, 2), flip(part(left, 1 - bit_x, 2), 1))
    right = add_low(part(right, bit_y, 2), flip(part(right, 1 - bit_y, 2), 2))
    return left, right


def plane_scatter_second(halves, bit_x, bit_y):
    left, right = halves
    left = add_low(part(left, bit_y, 2), flip(part(left, 1 - bit_y, 2), 2))
    right = add_low(part(right, bit_x, 2), flip(part(right, 1 - bit_x, 2), 1))
    return left, right


def plane_gather_first(left, right, bit_x, bit_y):
    return ordered(left, flip(left, 2), bit_y), ordered(right, flip(right, 1), bit_x)


def plane_gather_second(left, right):
    return flip(left, 1), flip(right, 2)


def lay_out(bits, halves, widths, arrived, earlier=()):
    rows, columns = halves[0].shape

    def kernel(bits_ref, *refs):
        sources, refs = refs[:2], refs[2 + len(earlier) :]
        results, (wide, semaphores) = refs[: len(widths)], refs[len(widths) :]
        copies = []
        for side in range(2):
            wide[side] = sources[side][...].astype(jnp.float32)
            bit = bits_ref[side]
            place = pl.multiple_of((2 * side + (1 - bit if arrived else bit)) * rows, rows)
            start = 0
            for n, (result, size) in enumerate(zip(results, widths, strict=True)):
                copies.append(
                    pltpu.make_async_copy(
                        wide.at[side, :, pl.ds(start, size)],
                        result.at[pl.ds(place, rows), :],
                        semaphores.at[side, n],
                    )
                )
                copies[-1].start()
                start += size
        for copy in copies:
            copy.wait()

    anywhere = pl.BlockSpec(memory_space=pl.ANY)
    return pl.pallas_call(
        kernel,
        in_specs=[pl.BlockSpec(memory_space=pltpu.SMEM)]
        + [pl.BlockSpec(memory_space=pltpu.VMEM)] * 2
        + [anywhere] * len(earlier),
        out_specs=[anywhere] * len(widths),
        out_shape=[jax.ShapeDtypeStruct((4 * rows, size), jnp.float32) for size in widths],
        scratch_shapes=[
            pltpu.VMEM((2, rows, columns), jnp.float32),
            pltpu.SemaphoreType.DMA((2, len(widths))),
        ],
        input_output_aliases={3 + n: n for n in range(len(earlier))},
        compiler_params=pltpu.CompilerParams(vmem_limit_bytes=VMEM_BYTES),
        cost_estimate=small_cost(),
        name="lay_out",
    )(bits, *halves, *earlier)


def rotary_tables(tokens):
    halfway = HD // 2
    frequency = rope_base ** (-np.arange(halfway, dtype=np.float64) / halfway)
    angles = np.arange(tokens)[:, None] * frequency[None, :]
    cosine, sine = np.cos(angles), np.sin(angles)
    return (
        np.concatenate([cosine, cosine], axis=1).astype(np.float32),
        np.concatenate([-sine, sine], axis=1).astype(np.float32),
    )


def causal_scores(query_block, keys, row_start, scale_factor):
    raw = contract_cols(query_block, keys) * scale_factor
    row_ids = row_start + lax.broadcasted_iota(jnp.int32, raw.shape, 0)
    return jnp.where(lax.broadcasted_iota(jnp.int32, raw.shape, 1) <= row_ids, raw, masked_score)


def softmax_rows(raw):
    exponent = jnp.exp(raw - jnp.max(raw, axis=-1, keepdims=True))
    return exponent / jnp.sum(exponent, axis=-1, keepdims=True)


def attention_forward(core, hidden, gain, w_query, w_key, w_value, w_output, cosine, sine):
    tokens, width = hidden.shape
    half = tokens // 2
    local = w_query.shape[1]
    heads = local // HD
    scale_factor = 1.0 / math.sqrt(HD)

    def kernel(
        core_ref, hidden_ref, gain_ref, wq_ref, wk_ref, wv_ref, wo_ref, cos_ref, sin_ref,
        normed_ref, query_ref, key_ref, value_ref, mixed_ref, keep_ref, send_ref, part_ref,
    ):
        for block in range(2):
            rows = pl.ds(block * half, half)
            source = hidden_ref[rows, :].astype(jnp.float32)
            scale = lax.rsqrt(jnp.mean(source * source, axis=-1, keepdims=True) + epsilon)
            normed = (source * scale * gain_ref[...]).astype(jnp.bfloat16)
            normed_ref[rows, :] = normed
            cos, sin = cos_ref[rows, :], sin_ref[rows, :]

            def turned(value):
                return (value * cos + pltpu.roll(value, HD // 2, 1) * sin).astype(jnp.bfloat16)

            query_pre = dot(normed, wq_ref[...])
            for head in range(heads):
                lanes = slice(head * HD, (head + 1) * HD)
                query_ref[rows, lanes] = turned(query_pre[:, lanes])
            key_ref[rows, :] = turned(dot(normed, wk_ref[...]))
            value_ref[rows, :] = dot(normed, wv_ref[...]).astype(jnp.bfloat16)
        for block in range(2):
            rows = pl.ds(block * half, half)
            seen = pl.ds(0, (block + 1) * half)
            keys, values = key_ref[seen, :], value_ref[seen, :]
            for head in range(heads):
                lanes = slice(head * HD, (head + 1) * HD)
                raw = causal_scores(query_ref[rows, lanes], keys, block * half, scale_factor)
                probs_low = softmax_rows(raw).astype(jnp.bfloat16)
                mixed_ref[rows, lanes] = dot(probs_low, values).astype(jnp.bfloat16)
            part_ref[rows, :] = dot(mixed_ref[rows, :], wo_ref[...])
        own = pl.ds(pl.multiple_of(core_ref[0] * half, half), half)
        other = pl.ds(pl.multiple_of((1 - core_ref[0]) * half, half), half)
        keep_ref[...] = hidden_ref[own, :].astype(jnp.float32) + part_ref[own, :]
        send_ref[...] = part_ref[other, :].astype(jnp.bfloat16)

    def low(rows, columns):
        return jax.ShapeDtypeStruct((rows, columns), jnp.bfloat16)

    shapes = [
        low(tokens, width), low(tokens, local), low(tokens, HD), low(tokens, HD),
        low(tokens, local), jax.ShapeDtypeStruct((half, width), jnp.float32), low(half, width),
    ]
    operands = [hidden, gain, w_query, w_key, w_value, w_output, cosine, sine]
    return pl.pallas_call(
        kernel,
        out_shape=shapes,
        in_specs=[pl.BlockSpec(memory_space=pltpu.SMEM)]
        + [pl.BlockSpec(memory_space=pltpu.VMEM) for _ in operands],
        out_specs=[pl.BlockSpec(memory_space=pltpu.VMEM) for _ in shapes],
        scratch_shapes=[pltpu.VMEM((tokens, width), jnp.float32)],
        compiler_params=pltpu.CompilerParams(vmem_limit_bytes=VMEM_BYTES),
        cost_estimate=small_cost(
            flops=40 * 10**9, bytes_accessed=16 * 10**6, transcendentals=2 * 10**6
        ),
        name="attention_forward",
    )(core, *operands)


def second_norm(keep, arrived, gain):
    def kernel(keep_ref, arrived_ref, gain_ref, middle_ref, rows_ref):
        middle = keep_ref[...] + arrived_ref[...].astype(jnp.float32)
        middle_ref[...] = middle
        scale = lax.rsqrt(jnp.mean(middle * middle, axis=-1, keepdims=True) + epsilon)
        rows_ref[...] = (middle * scale * gain_ref[...]).astype(jnp.bfloat16)

    vmem = pl.BlockSpec(memory_space=pltpu.VMEM)
    return pl.pallas_call(
        kernel,
        in_specs=[vmem] * 3,
        out_specs=[vmem] * 2,
        out_shape=[
            jax.ShapeDtypeStruct(keep.shape, jnp.float32),
            jax.ShapeDtypeStruct(keep.shape, jnp.bfloat16),
        ],
        compiler_params=pltpu.CompilerParams(vmem_limit_bytes=VMEM_BYTES),
        cost_estimate=small_cost(),
        name="second_norm",
    )(keep, arrived, gain)


def second_norm_gradient(at_end, own, arrived_out, arrived_in, middle, out_grad, gain):
    def kernel(
        at_end_ref, own_ref, out_ref, in_ref, middle_ref, dy_ref, gain_ref, grad_ref, low_ref, gain_grad_ref
    ):
        rows = own_ref[...].astype(jnp.float32) + out_ref[...].astype(jnp.float32)
        rows = jnp.where(at_end_ref[0] != 0, rows, rows + in_ref[...].astype(jnp.float32))
        middle = middle_ref[...]
        scale = lax.rsqrt(jnp.mean(middle * middle, axis=-1, keepdims=True) + epsilon)
        unit = middle * scale
        gain_grad_ref[...] = jnp.sum(rows * unit, axis=0, keepdims=True)
        scaled = rows * gain_ref[...]
        grad = dy_ref[...].astype(jnp.float32) + scale * (
            scaled - unit * jnp.mean(scaled * unit, axis=-1, keepdims=True)
        )
        grad_ref[...] = grad
        low_ref[...] = grad.astype(jnp.bfloat16)

    vmem = pl.BlockSpec(memory_space=pltpu.VMEM)
    return pl.pallas_call(
        kernel,
        in_specs=[pl.BlockSpec(memory_space=pltpu.SMEM)] + [vmem] * 6,
        out_specs=[vmem] * 3,
        out_shape=[
            jax.ShapeDtypeStruct(middle.shape, jnp.float32),
            jax.ShapeDtypeStruct(middle.shape, jnp.bfloat16),
            jax.ShapeDtypeStruct((1, middle.shape[1]), jnp.float32),
        ],
        compiler_params=pltpu.CompilerParams(vmem_limit_bytes=VMEM_BYTES),
        cost_estimate=small_cost(),
        name="second_norm_gradient",
    )(at_end, own, arrived_out, arrived_in, middle, out_grad, gain)


def output_gradient(places, mixed, own, other):
    half, width = own.shape
    local = mixed.shape[1]
    piece = local // 4

    def kernel(places_ref, mixed_ref, own_ref, other_ref, *refs):
        pieces, (whole_ref, result) = refs[:4], refs[4:]
        core = places_ref[0]
        whole_ref[pl.ds(pl.multiple_of(core * half, half), half), :] = own_ref[...]
        whole_ref[pl.ds(pl.multiple_of((1 - core) * half, half), half), :] = other_ref[...]
        result[...] = contract_rows(mixed_ref[...], whole_ref[...]).astype(jnp.bfloat16)
        give_pieces(places_ref, result, pieces, piece)

    low = jax.ShapeDtypeStruct((piece, width), jnp.bfloat16)
    results = pl.pallas_call(
        kernel,
        in_specs=[pl.BlockSpec(memory_space=pltpu.SMEM)]
        + [pl.BlockSpec(memory_space=pltpu.VMEM)] * 3,
        out_specs=[pl.BlockSpec(memory_space=pltpu.VMEM)] * 5,
        out_shape=[low] * 4 + [jax.ShapeDtypeStruct((2 * half, width), jnp.bfloat16)],
        scratch_shapes=[pltpu.VMEM((local, width), jnp.bfloat16)],
        compiler_params=pltpu.CompilerParams(vmem_limit_bytes=VMEM_BYTES),
        cost_estimate=small_cost(),
        name="output_gradient",
    )(places, mixed, own, other)
    return results[:4], results[4]


def give_pieces(places_ref, result, pieces, rows):
    for side in range(2):
        bit = places_ref[1 + side]
        for n, place in enumerate((bit, 1 - bit)):
            start = pl.multiple_of((2 * side + place) * rows, rows)
            pieces[2 * side + n][...] = result[pl.ds(start, rows), :]


def attention_backward(grad_attn, w_output, queries, keys, values, cosine, sine):
    tokens, local = queries.shape
    half = tokens // 2
    heads = local // HD
    scale_factor = 1.0 / math.sqrt(HD)

    def kernel(
        ga_ref, wo_ref, query_ref, key_ref, value_ref, cos_ref, sin_ref, grad_ref, gk_ref, gv_ref, gm_ref
    ):
        gm_ref[...] = contract_cols(ga_ref[...], wo_ref[...]).astype(jnp.bfloat16)
        for block in range(2):
            rows = pl.ds(block * half, half)
            seen = pl.ds(0, (block + 1) * half)
            keys, values = key_ref[seen, :], value_ref[seen, :]
            cos, sin = cos_ref[rows, :], sin_ref[rows, :]
            grad_keys = jnp.zeros(((block + 1) * half, HD), jnp.float32)
            grad_values = grad_keys
            for head in range(heads):
                lanes = slice(head * HD, (head + 1) * HD)
                query, grad = query_ref[rows, lanes], gm_ref[rows, lanes]
                probs = softmax_rows(causal_scores(query, keys, block * half, scale_factor))
                grad_probs = contract_cols(grad, values)
                delta = jnp.sum(probs * grad_probs, axis=-1, keepdims=True)
                grad_scores = (probs * (grad_probs - delta)).astype(jnp.bfloat16)
                turned = dot(grad_scores, keys) * scale_factor
                grad_ref[rows, lanes] = (
                    turned * cos - pltpu.roll(turned, HD // 2, 1) * sin
                ).astype(jnp.bfloat16)
                grad_keys = grad_keys + contract_rows(grad_scores, query)
                grad_values = grad_values + contract_rows(probs.astype(jnp.bfloat16), grad)
            if block == 0:
                gk_ref[pl.ds(0, half), :] = grad_keys
                gv_ref[pl.ds(0, half), :] = grad_values
            else:
                first = pl.ds(0, half)
                gk_ref[first, :] = gk_ref[first, :] + grad_keys[:half]
                gv_ref[first, :] = gv_ref[first, :] + grad_values[:half]
                gk_ref[rows, :] = grad_keys[half:]
                gv_ref[rows, :] = grad_values[half:]
        turned = gk_ref[...] * scale_factor
        grad_ref[:, local : local + HD] = (
            turned * cos_ref[...] - pltpu.roll(turned, HD // 2, 1) * sin_ref[...]
        ).astype(jnp.bfloat16)
        grad_ref[:, local + HD :] = gv_ref[...].astype(jnp.bfloat16)

    return pl.pallas_call(
        kernel,
        out_shape=jax.ShapeDtypeStruct((tokens, local + 2 * HD), jnp.bfloat16),
        in_specs=[pl.BlockSpec(memory_space=pltpu.VMEM)] * 7,
        out_specs=pl.BlockSpec(memory_space=pltpu.VMEM),
        scratch_shapes=[pltpu.VMEM((tokens, HD), jnp.float32)] * 2
        + [pltpu.VMEM((tokens, local), jnp.bfloat16)],
        compiler_params=pltpu.CompilerParams(vmem_limit_bytes=VMEM_BYTES),
        cost_estimate=small_cost(
            flops=10 * 10**9, bytes_accessed=4 * 10**6, transcendentals=2 * 10**6
        ),
        name="attention_backward",
    )(grad_attn, w_output, queries, keys, values, cosine, sine)


def expert_weights_of(expert_ref, packs, half):
    start = 2 * half
    count = packs[0].shape[0] - start
    row_ids = lax.broadcasted_iota(jnp.int32, (count, 128), 0)
    lane_ids = lax.broadcasted_iota(jnp.int32, (count, 128), 1)
    pick = (row_ids == (expert_ref[0] ^ lane_ids)).astype(jnp.bfloat16)
    sides = []
    for ref in packs:
        coarse, fine = ref[start:, :half], ref[start:, half : 2 * half]
        sides.append(contract_rows(coarse, pick) + contract_rows(fine, pick))
    return jnp.concatenate(sides, axis=0)


def expert_terms(expert, joins, pieces, first, keep):
    sequences = [sequence for own, _ in joins for sequence in own]
    width = sequences[0][0].shape[1]
    half = sequences[0][0].shape[0] // 2 // 128 * 128
    number = len(pieces)
    arrays = [array for own in pieces for array, _ in own]
    columns = arrays[0].shape[-1]
    hidden = columns // 3
    tokens = 2 * half
    total = len(sequences)
    flat = [array for sequence in sequences for array in sequence]

    loads = []
    n = 0
    for own in pieces:
        loads.append([])
        place = 0
        for array, index in own:
            loads[-1].append((n, index, place, array.shape[-2]))
            place += array.shape[-2]
            n += 1
    copy_count = n

    def kernel(expert_ref, *refs):
        sources, refs = refs[: len(flat)], refs[len(flat) :]
        piece_refs, refs = refs[: len(arrays)], refs[len(arrays) :]
        results, (w_ref, packs, gate_all, semaphores) = refs[:-4], refs[-4:]
        e = pl.program_id(0)

        def copies_of(one):
            for which, index, place, rows in loads[one]:
                source = piece_refs[which] if index is None else piece_refs[which].at[index]
                yield pltpu.make_async_copy(
                    source, w_ref.at[one, pl.ds(place, rows), :], semaphores.at[which]
                )

        def kept(one):
            return pltpu.make_async_copy(
                w_ref.at[one], results[-1].at[one], semaphores.at[copy_count + one]
            )

        def pack_copy(n):
            return pltpu.make_async_copy(
                sources[n], packs.at[n], semaphores.at[copy_count + number + n]
            )

        @pl.when(e == 0)
        def _():
            for copy in copies_of(0):
                copy.start()
            for n in range(2 * total):
                pack_copy(n).start()
            for one in range(1, number):
                for copy in copies_of(one):
                    copy.start()

        for one in range(number):

            @pl.when(e == one)
            def _(one=one):
                for copy in copies_of(one):
                    copy.wait()
                if keep:
                    kept(one).start()

        lanes = lax.broadcasted_iota(jnp.int32, (half, 128), 1)
        n = 0
        for join, (own, start) in enumerate(joins):
            inner_ref, grad_ref = results[2 * join : 2 * join + 2]
            for s in range(len(own)):

                @pl.when(e == 0)
                def _(n=n):
                    for side in range(2):
                        pack_copy(2 * n + side).wait()
                    gate_all[n * tokens : (n + 1) * tokens, :] = expert_weights_of(
                        expert_ref, [packs.at[2 * n], packs.at[2 * n + 1]], half
                    )

                def run(n=n, s=s, inner_ref=inner_ref, grad_ref=grad_ref):
                    for side in range(2):
                        pack = packs.at[2 * n + side]
                        here = pl.ds(s * tokens + side * half, half)
                        gate = gate_all[n * tokens + side * half : n * tokens + (side + 1) * half, :]
                        weight = jnp.sum(
                            jnp.where(lanes == e + first, gate, 0.0), axis=1, keepdims=True
                        )
                        both = dot(pack[:half, :], w_ref[e, :, : 2 * hidden])
                        grad_inner = dot(pack[half : 2 * half, :], w_ref[e, :, 2 * hidden :]) * weight
                        gate_pre, up_pre = both[:, :hidden], both[:, hidden:]
                        sigmoid = jax.nn.sigmoid(gate_pre)
                        activated = gate_pre * sigmoid
                        grad_gate = (
                            grad_inner * up_pre * sigmoid * (1.0 + gate_pre * (1.0 - sigmoid))
                        )
                        grad_ref[here, :hidden] = grad_gate.astype(jnp.bfloat16)
                        grad_ref[here, hidden:] = (grad_inner * activated).astype(jnp.bfloat16)
                        inner_ref[here, :] = (activated * up_pre * weight).astype(jnp.bfloat16)

                if start:
                    pl.when(e >= start)(run)
                else:
                    run()
                n += 1

        if keep:

            @pl.when(e == number - 1)
            def _():
                for one in range(number):
                    kept(one).wait()

    out_specs, out_shape = [], []
    for own, start in joins:
        for size in (hidden, 2 * hidden):
            out_specs.append(
                pl.BlockSpec(
                    (len(own) * tokens, size), lambda e, start=start: (0, jnp.maximum(e - start, 0))
                )
            )
            out_shape.append(
                jax.ShapeDtypeStruct((len(own) * tokens, (number - start) * size), jnp.bfloat16)
            )
    if keep:
        out_specs.append(pl.BlockSpec(memory_space=pl.ANY))
        out_shape.append(jax.ShapeDtypeStruct((number, width, columns), jnp.bfloat16))
    results = pl.pallas_call(
        kernel,
        grid=(number,),
        in_specs=[pl.BlockSpec(memory_space=pltpu.SMEM)]
        + [pl.BlockSpec(memory_space=pl.ANY)] * (len(flat) + len(arrays)),
        out_specs=out_specs,
        out_shape=out_shape,
        scratch_shapes=[
            pltpu.VMEM((number, width, columns), jnp.bfloat16),
            pltpu.VMEM((2 * total, *flat[0].shape), jnp.bfloat16),
            pltpu.VMEM((total * tokens, 128), jnp.float32),
            pltpu.SemaphoreType.DMA((copy_count + number + 2 * total,)),
        ],
        compiler_params=pltpu.CompilerParams(vmem_limit_bytes=VMEM_BYTES),
        cost_estimate=small_cost(),
        name="expert_terms",
    )(expert, *flat, *arrays)
    terms = [tuple(results[2 * n : 2 * n + 2]) for n in range(len(joins))]
    return (*terms, results[-1]) if keep else tuple(terms)


def expert_sums(groups, weights, half):
    number, width = weights.shape[:2]
    hidden = weights.shape[2] // 3
    counts = [group[0][0].shape[0] // (2 * half) for group in groups]
    total = sum(counts)
    flat = [array for group in groups for part in group for array in part[:2]]
    block = 512

    def kernel(*refs):
        terms, refs = refs[: len(flat)], refs[len(flat) :]
        w_ref, back_own, back_other, out_own, out_other = refs
        n = place = 0
        for group, count in zip(groups, counts, strict=True):
            back = out = None
            for inner, _, start in group:
                for e in range(inner.shape[1] // hidden):
                    grad = terms[n + 1][:, 2 * e * hidden : 2 * (e + 1) * hidden]
                    one = contract_cols(grad, w_ref[start + e, :, : 2 * hidden])
                    back = one if back is None else back + one
                n += 2
            n -= 2 * len(group)
            for inner, _, start in group:
                for e in range(inner.shape[1] // hidden):
                    one = contract_cols(
                        terms[n][:, e * hidden : (e + 1) * hidden], w_ref[start + e, :, 2 * hidden :]
                    )
                    out = one if out is None else out + one
                n += 2
            for s in range(count):
                start = 2 * s * half
                back_own[place + s] = back[start : start + half].astype(jnp.bfloat16)
                back_other[place + s] = back[start + half : start + 2 * half].astype(jnp.bfloat16)
                out_own[place + s] = out[start : start + half].astype(jnp.bfloat16)
                out_other[place + s] = out[start + half : start + 2 * half].astype(jnp.bfloat16)
            place += count

    low = jax.ShapeDtypeStruct((total, half, width), jnp.bfloat16)
    return pl.pallas_call(
        kernel,
        grid=(width // block,),
        in_specs=[whole(*a.shape) for a in flat]
        + [pl.BlockSpec((number, block, 3 * hidden), lambda n: (0, n, 0))],
        out_specs=[pl.BlockSpec((total, half, block), lambda n: (0, 0, n))] * 4,
        out_shape=[low] * 4,
        compiler_params=pltpu.CompilerParams(vmem_limit_bytes=VMEM_BYTES),
        cost_estimate=small_cost(),
        name="expert_sums",
    )(*flat, weights)


def load_copies(sequence, half, sources, x_all, dy_all, semaphores, which=range(4)):
    for n in which:
        target = x_all if n < 2 else dy_all
        yield pltpu.make_async_copy(
            sources[2 * sequence + n % 2].at[pl.ds((n // 2) * half, half), :],
            target.at[pl.ds((2 * sequence + n % 2) * half, half), :],
            semaphores.at[4 * sequence + n],
        )


def expert_weight_grads(sequences, terms, number, hidden):
    width = sequences[0][0].shape[1]
    half = sequences[0][0].shape[0] // 2 // 128 * 128
    tokens = 2 * half
    flat = [array for sequence in sequences for array in sequence]
    total = len(sequences)
    quarter = width // 4
    per_load = 4 * total

    def kernel(*refs):
        sources, refs = refs[: len(flat)], refs[len(flat) :]
        term_refs, refs = refs[: 2 * len(terms)], refs[2 * len(terms) :]
        result_refs, refs = refs[: 4 * number], refs[4 * number :]
        x_all, dy_all, inner_all, grad_all, result, semaphores, term_semaphores, out_semaphores = refs

        def row_copies(of_gradients):
            for s in range(total):
                yield from load_copies(
                    s, half, sources, x_all, dy_all, semaphores, (2, 3) if of_gradients else (0, 1)
                )

        def term_copies(e, of_products):
            place = 0
            for n, (inner, _, start) in enumerate(terms):
                rows = inner.shape[0]
                size = 2 * hidden if of_products else hidden
                yield pltpu.make_async_copy(
                    term_refs[2 * n + of_products].at[:, pl.ds((start + e) * size, size)],
                    (grad_all if of_products else inner_all).at[e, pl.ds(place, rows), :],
                    term_semaphores.at[2 * len(terms) * e + 2 * n + of_products],
                )
                place += rows

        def out_copies(e):
            for q in range(4):
                yield pltpu.make_async_copy(
                    result.at[e, pl.ds(q * quarter, quarter), :],
                    result_refs[4 * e + q],
                    out_semaphores.at[4 * e + q],
                )

        first = [*row_copies(True), *term_copies(0, 0)]
        second = [*row_copies(False), *term_copies(0, 1)]
        later = [[*term_copies(e, 0), *term_copies(e, 1)] for e in range(1, number)]
        for copy in [*first, *second, *(copy for one in later for copy in one)]:
            copy.start()
        for e in range(number):
            for copy in first if e == 0 else later[e - 1]:
                copy.wait()
            result[e, :, 2 * hidden :] = contract_rows(dy_all[...], inner_all[e]).astype(jnp.bfloat16)
            if e == 0:
                for copy in second:
                    copy.wait()
            result[e, :, : 2 * hidden] = contract_rows(x_all[...], grad_all[e]).astype(jnp.bfloat16)
            for copy in out_copies(e):
                copy.start()
        for e in range(number):
            for copy in out_copies(e):
                copy.wait()

    anywhere = pl.BlockSpec(memory_space=pl.ANY)
    return pl.pallas_call(
        kernel,
        in_specs=[anywhere] * (len(flat) + 2 * len(terms)),
        out_specs=[anywhere] * (4 * number),
        scratch_shapes=[pltpu.VMEM((total * tokens, width), jnp.bfloat16)] * 2
        + [
            pltpu.VMEM((number, total * tokens, hidden), jnp.bfloat16),
            pltpu.VMEM((number, total * tokens, 2 * hidden), jnp.bfloat16),
            pltpu.VMEM((number, width, 3 * hidden), jnp.bfloat16),
            pltpu.SemaphoreType.DMA((per_load,)),
            pltpu.SemaphoreType.DMA((2 * len(terms) * number,)),
            pltpu.SemaphoreType.DMA((4 * number,)),
        ],
        out_shape=[jax.ShapeDtypeStruct((quarter, 3 * hidden), jnp.bfloat16)] * (4 * number),
        compiler_params=pltpu.CompilerParams(vmem_limit_bytes=VMEM_BYTES),
        cost_estimate=small_cost(),
        name="expert_weight_grads",
    )(*flat, *(array for term in terms for array in term[:2]))


def own_weight_grads(sequences, terms, arrived, hidden):
    width = sequences[0][0].shape[1]
    half = sequences[0][0].shape[0] // 2 // 128 * 128
    tokens = 2 * half
    counts = [pair[0].shape[0] // tokens for pair in terms]
    flat = [array for sequence in sequences for array in sequence]
    total = len(sequences)
    quarter = width // 4

    def kernel(*refs):
        sources, refs = refs[: len(flat)], refs[len(flat) :]
        term_refs, refs = refs[: 2 * len(counts)], refs[2 * len(counts) :]
        arrived_refs, refs = refs[:6], refs[6:]
        gate_ref, up_ref, down_ref, x_all, dy_all, semaphores = refs
        for s in range(total):
            for copy in load_copies(s, half, sources, x_all, dy_all, semaphores):
                copy.start()
        gate_up = down = None
        first = 0
        for joined, count in enumerate(counts):
            for s in range(first, first + count):
                for copy in load_copies(s, half, sources, x_all, dy_all, semaphores):
                    copy.wait()
            span = pl.ds(first * tokens, count * tokens)
            one = contract_rows(x_all[span, :], term_refs[2 * joined + 1][...])
            two = contract_rows(term_refs[2 * joined][...], dy_all[span, :])
            gate_up = one if gate_up is None else gate_up + one
            down = two if down is None else down + two
            first += count
        for q in range(4):
            rows = slice(q * quarter, (q + 1) * quarter)
            inside = slice(q % 2 * quarter, (q % 2 + 1) * quarter)
            more = arrived_refs[q][...].astype(jnp.float32) + arrived_refs[4 + q // 2][
                inside, :
            ].astype(jnp.float32)
            both = gate_up[rows] + more[:, : 2 * hidden]
            gate_ref[0, rows, :] = both[:, :hidden]
            up_ref[0, rows, :] = both[:, hidden:]
            down_ref[0, :, rows] = down[:, rows] + more[:, 2 * hidden :].T

    def beside(count, columns):
        return pl.BlockSpec((count * tokens, columns), lambda e: (0, 0))

    tall = jax.ShapeDtypeStruct((1, width, hidden), jnp.float32)
    flat_down = jax.ShapeDtypeStruct((1, hidden, width), jnp.float32)
    return pl.pallas_call(
        kernel,
        grid=(1,),
        in_specs=[pl.BlockSpec(memory_space=pl.ANY)] * len(flat)
        + [beside(count, columns) for count in counts for columns in (hidden, 2 * hidden)]
        + [whole(quarter, 3 * hidden)] * 4
        + [whole(2 * quarter, 3 * hidden)] * 2,
        out_specs=[whole(*tall.shape), whole(*tall.shape), whole(*flat_down.shape)],
        scratch_shapes=[pltpu.VMEM((total * tokens, width), jnp.bfloat16)] * 2
        + [pltpu.SemaphoreType.DMA((4 * total,))],
        out_shape=[tall, tall, flat_down],
        compiler_params=pltpu.CompilerParams(vmem_limit_bytes=VMEM_BYTES),
        cost_estimate=small_cost(),
        name="own_weight_grads",
    )(*flat, *(array for pair in terms for array in pair), *arrived)


def planes_of_four(
    hidden_in,
    attn_gain,
    w_query,
    w_key,
    w_value,
    w_output,
    moe_gain,
    w_gate,
    w_up,
    w_down,
    gate_logits,
    routes,
    out_grad,
):
    tokens, width = hidden_in.shape
    half = tokens // 2
    experts = lax.axis_size("expert")
    columns = [[4 * z + r for z in range(4)] for r in range(4)]
    core = lax.axis_index("tensor")
    expert = lax.axis_index("expert")
    plane = expert // 4
    bit_x = expert % 2
    bit_y = (expert // 2) % 2
    hidden = w_down.shape[1]
    together = lax.optimization_barrier

    own_weights = jnp.concatenate([w_gate[0], w_up[0], w_down[0].T], axis=1)
    quarter = width // 4
    pieces = [own_weights[:quarter], own_weights[quarter : 2 * quarter], own_weights[2 * quarter :]]
    gate_weights = jax.nn.softmax(gate_logits, axis=-1)
    names = jnp.arange(experts, dtype=jnp.int32)
    dense = jnp.sum(
        jnp.where(routes.T[:, None, :] == names[None, :, None], gate_weights.T[:, None, :], 0.0),
        axis=0,
    )
    dense = lax.dynamic_slice_in_dim(dense, core * half, half, 1)
    coarse = dense.astype(jnp.bfloat16)
    fine = (dense - coarse.astype(jnp.float32)).astype(jnp.bfloat16)
    extra = jnp.pad(jnp.concatenate([coarse, fine], axis=1), ((0, 0), (0, width - 2 * half)))
    out_grad_half = part(out_grad, core, 2)
    dy_own = jnp.concatenate([out_grad_half, extra], axis=0)

    x0, y0 = flip(pieces[0], 1), flip(pieces[0], 2)
    dy_out_one, dy_in_one = outer(dy_own), inner(dy_own)
    cosine, sine = (jnp.asarray(table) for table in rotary_tables(tokens))
    normed, queries, keys, values, mixed, keep, send = attention_forward(
        core.reshape(1), hidden_in, attn_gain[None], w_query, w_key, w_value, w_output, cosine, sine
    )
    send, x0, y0, dy_out_one, dy_in_one, piece = together(
        (send, x0, y0, dy_out_one, dy_in_one, pieces[1])
    )
    x1, y1 = flip(piece, 1), flip(piece, 2)
    middle, rows_in = second_norm(keep, swap(send), moe_gain[None])
    out_one, in_one = outer(rows_in), inner(rows_in)
    x1, y1, out_one, in_one, dy_out_one, dy_in_one, piece = together(
        (x1, y1, out_one, in_one, dy_out_one, dy_in_one, pieces[2])
    )
    out_one = jnp.concatenate([out_one, dy_out_one], axis=0)
    in_one = jnp.concatenate([in_one, dy_in_one], axis=0)
    out_one, in_one, piece = together((out_one, in_one, piece))
    x2, y2 = flip(piece, 1), flip(piece, 2)
    out_two, in_two = outer(in_one), inner(out_one)
    own = jnp.concatenate([rows_in, dy_own], axis=0)
    own, first = (own, swap(own)), (out_one, swap(out_one))
    far_from_y = jnp.concatenate([y0, y1], axis=0)
    x2, y2, out_two, in_two, own, first, far_from_y = together(
        (x2, y2, out_two, in_two, own, first, far_from_y)
    )
    far_weights = [flip(far_from_y, 1), flip(x2, 2)]
    out_three = outer(in_two)
    at_end = (plane == 0) | (plane == 3)
    number = expert.reshape(1)
    second = jnp.where(at_end, out_two, in_one)
    second = (second, swap(second))
    near_pieces = [[own_weights], [x0, x1, x2], [y0, y1, y2]]
    near_early, near_second, near_weights = expert_terms(
        number,
        [([own, first], 0), ([second], 0)],
        [[(piece, None) for piece in one] for one in near_pieces],
        0,
        True,
    )
    far_weights, out_three, near_early, near_second, second = together(
        (far_weights, out_three, near_early, near_second, second)
    )
    third = jnp.where(at_end, out_three, in_two)
    third = (third, swap(third))
    far_pieces = [(piece, None) for piece in far_weights]
    all_third, far_second, far_early, weights = expert_terms(
        number,
        [([third], 0), ([second], 3), ([own, first], 3)],
        [[(near_weights, 0)], [(near_weights, 1)], [(near_weights, 2)], far_pieces],
        0,
        True,
    )
    to_far = expert_weight_grads(
        [third, second, own, first], [(*all_third, 3), (*far_second, 0), (*far_early, 0)], 1, hidden
    )
    over_x, over_y = [flip(to_far[0], 1)], [flip(to_far[2], 2)]
    to_far, near_second, far_second = together((to_far, near_second, far_second))
    late_sums = expert_sums(
        [[(*all_third, 0)], [(*near_second, 0), (*far_second, 3)]], weights, half
    )
    late_sums, over_x, over_y, to_far = together((late_sums, over_x, over_y, to_far))
    back_late = add_low(late_sums[0], swap(late_sums[1]))
    back_late, near_early, all_third = together((back_late, near_early, all_third))
    second_back, third_back = back_late[1], back_late[0]

    arrived_out = outer(third_back)
    over_x, over_y = over_x + [flip(to_far[1], 1)], over_y + [flip(to_far[3], 2)]
    beside = expert_weight_grads(
        [own, first, second, third],
        [(*near_early, 1), (*near_second, 1), (*all_third, 1)],
        2,
        hidden,
    )
    arrived_out, beside, over_x, over_y, far_early = together(
        (arrived_out, beside, over_x, over_y, far_early)
    )
    to_x, to_y = beside[:4], beside[4:]
    arrived_in, arrived_out = inner(add_low(third_back, arrived_out)), outer(second_back)
    from_x, from_y = [flip(to_x[0], 1)], [flip(to_y[2], 2)]
    early_sums = expert_sums([[(*near_early, 0), (*far_early, 3)]], weights, half)
    arrived_in, arrived_out, early_sums, from_x, from_y, to_x, to_y = together(
        (arrived_in, arrived_out, early_sums, from_x, from_y, to_x, to_y)
    )
    back_early = add_low(early_sums[0], swap(early_sums[1]))
    own_back, first_back = back_early[0], back_early[1]
    going_out = jnp.where(at_end, first_back, add_low(first_back, arrived_in))
    going_in = add_low(second_back, arrived_out)
    going_out, going_in, early_sums, late_sums, over_x = together(
        (going_out, going_in, early_sums, late_sums, over_x)
    )
    arrived_out, arrived_in = outer(going_out), inner(going_in)
    from_x, from_y = from_x + [flip(to_x[1], 1)], from_y + [flip(to_y[3], 2)]
    with_x = jnp.concatenate([add_low(to_y[n], over_x[n]) for n in range(2)], axis=0)
    with_y = jnp.concatenate([add_low(to_x[2 + n], over_y[n]) for n in range(2)], axis=0)
    out_late = add_low(late_sums[2], swap(late_sums[3]))
    out_early = add_low(early_sums[2], swap(early_sums[3]))
    own_out, first_out, second_out, third_out = out_early[0], out_early[1], out_late[1], out_late[0]
    by_plane = [
        jnp.where(plane == 0, own_out, jnp.where(plane == 1, first_out, third_out)),
        jnp.where(plane == 0, first_out, jnp.where(plane == 1, own_out, second_out)),
        jnp.where(plane == 3, first_out, jnp.where(plane == 2, own_out, second_out)),
        jnp.where(plane == 3, own_out, jnp.where(plane == 2, first_out, third_out)),
    ]
    results = jnp.concatenate(by_plane, axis=0)
    arrived_out, arrived_in, results, from_x, from_y, with_x, with_y = together(
        (arrived_out, arrived_in, results, from_x, from_y, with_x, with_y)
    )
    moe_result = lax.psum_scatter(
        results, "expert", axis_index_groups=columns, scatter_dimension=0, tiled=True
    )
    grad_middle, grad_attn_half, grad_moe_gain = second_norm_gradient(
        at_end.astype(jnp.int32).reshape(1),
        own_back,
        arrived_out,
        arrived_in,
        middle,
        out_grad_half,
        moe_gain[None],
    )
    places = jnp.stack([core, bit_x, bit_y])
    output_pieces, grad_attn = output_gradient(places, mixed, grad_attn_half, swap(grad_attn_half))
    output_pieces, grad_attn = together((output_pieces, grad_attn))
    left, to_x_side, right, to_y_side = output_pieces
    output_parts = add_low(left, flip(to_x_side, 1)), add_low(right, flip(to_y_side, 2))
    grad_all_pre = attention_backward(grad_attn, w_output, queries, keys, values, cosine, sine)
    grad_all_pre, output_parts = together((grad_all_pre, output_parts))
    grad_projections = contract_rows(normed, grad_all_pre).astype(jnp.bfloat16)
    output_parts = plane_scatter_second(output_parts, bit_x, bit_y)
    grad_projections, output_parts = together((grad_projections, output_parts))
    projection_parts = plane_scatter_first(grad_projections, bit_x, bit_y)
    w_all = jnp.concatenate([w_query, w_key, w_value], axis=1)
    grad_normed_part = contract_cols(grad_all_pre, w_all).astype(jnp.bfloat16)
    grad_normed = part(grad_normed_part, core, 2).astype(jnp.float32) + swap(
        part(grad_normed_part, 1 - core, 2)
    ).astype(jnp.float32)
    source_half = part(hidden_in, core, 2).astype(jnp.float32)
    scale_half = lax.rsqrt(jnp.mean(source_half * source_half, axis=-1, keepdims=True) + epsilon)
    unit_half = source_half * scale_half
    grad_unit_one = grad_normed * attn_gain
    grad_attn_gain = jnp.sum(grad_normed * unit_half, axis=0)
    grad_in_half = grad_middle + scale_half * (
        grad_unit_one - unit_half * jnp.mean(grad_unit_one * unit_half, axis=-1, keepdims=True)
    )
    gains = jnp.stack([grad_attn_gain, grad_moe_gain[0]])
    projection_parts, gains, grad_in_half = together((projection_parts, gains, grad_in_half))
    projection_parts = plane_scatter_second(projection_parts, bit_x, bit_y)
    gains = (gains + swap(gains)).reshape(-1, grad_projections.shape[1])
    gain_rows = gains.shape[0]
    gains = jnp.pad(gains, ((0, 16 - gain_rows), (0, 0))).astype(jnp.bfloat16)
    grad_in_other = swap(grad_in_half)
    output_both = jnp.concatenate(output_parts, axis=0)
    projection_both = jnp.concatenate([*projection_parts, gains], axis=0)
    projection_both, output_both, moe_result, with_x, with_y = together(
        (projection_both, output_both, moe_result, with_x, with_y)
    )
    output_both, projection_both = lax.psum(
        (output_both, projection_both), "expert", axis_index_groups=columns
    )
    block_half = (middle + moe_result.astype(jnp.float32)).astype(jnp.bfloat16)
    block_out = ordered(block_half, swap(block_half), core)
    then_y, then_x = flip(with_x, 2), flip(with_y, 1)
    output_both, projection_both, block_out, then_x, then_y = together(
        (output_both, projection_both, block_out, then_x, then_y)
    )
    gains, projection_both = projection_both[-16:].astype(jnp.float32), projection_both[:-16]
    output_halves = plane_gather_first(*jnp.split(output_both, 2), bit_x, bit_y)
    projection_halves = plane_gather_first(*jnp.split(projection_both, 2), bit_x, bit_y)
    output_halves, projection_halves, gains, then_x, then_y, grad_in_half, grad_in_other = together(
        (output_halves, projection_halves, gains, then_x, then_y, grad_in_half, grad_in_other)
    )
    arrived = (*from_x, *from_y, then_y, then_x)
    expert_grads = own_weight_grads(
        [own, first, second, third], [near_early, near_second, all_third], arrived, hidden
    )
    grad_in = ordered(grad_in_half, grad_in_other, core)
    bits = jnp.stack([bit_x, bit_y])
    projection_widths = [w.shape[1] for w in (w_query, w_key, w_value)]
    output_early = lay_out(bits, output_halves, (width,), False)
    projections_early = lay_out(bits, projection_halves, projection_widths, False)
    output_pieces = plane_gather_second(*output_halves)
    projection_pieces = plane_gather_second(*projection_halves)
    early_ones = (output_early, projections_early, grad_in)
    expert_grads, output_pieces, projection_pieces, gains, early_ones = together(
        (expert_grads, output_pieces, projection_pieces, gains, early_ones)
    )
    output_early, projections_early, grad_in = early_ones
    gains = (gains + flip(gains, 1)) + (flip(gains, 2) + flip(gains, 3))
    gains_sum = gains[:gain_rows].reshape(2, width)
    grad_gate, grad_up, grad_down = expert_grads
    projections = lay_out(bits, projection_pieces, projection_widths, True, projections_early)
    (output_sum,) = lay_out(bits, output_pieces, (width,), True, output_early)
    return (
        block_out,
        grad_in,
        gains_sum[0],
        *projections,
        output_sum,
        gains_sum[1],
        grad_gate,
        grad_up,
        grad_down,
    )


def solution(mesh):
    on_device = planes_of_four if mesh.shape["expert"] == 16 else routed_slots
    return jax.shard_map(
        on_device,
        mesh=mesh,
        in_specs=(
            P("expert", None),
            P(),
            P(None, "tensor"),
            P(None, "tensor"),
            P(None, "tensor"),
            P("tensor", None),
            P(),
            P("expert", None, "tensor"),
            P("expert", None, "tensor"),
            P("expert", "tensor", None),
            P("expert", None),
            P("expert", None),
            P("expert", None),
        ),
        out_specs=(
            P("expert", None),
            P("expert", None),
            P(),
            P(None, "tensor"),
            P(None, "tensor"),
            P(None, "tensor"),
            P("tensor", None),
            P(),
            P("expert", None, "tensor"),
            P("expert", None, "tensor"),
            P("expert", "tensor", None),
        ),
        check_vma=False,
    )
```
